128 devices in a mesh: hist: 8 (over x, z_lo), tok: 16 (over z_hi, y, core).
Axes of the slice: x: 4, y: 4, z: 4 (z_hi: 2, z_lo: 2; z = z_hi * 2 + z_lo), core: 2. Of those that a mesh axis runs over, the one named last changes fastest.
Arguments:
- history: bfloat16 [24, 16384, 2048], P('hist', 'tok'), may hold values from -6 to 6
- layer_ids: int32 [24], replicated, may hold values from 0 to 23, each once
- mix_weights: float32 [4, 24, 16384], P(None, None, 'tok'), may hold values from -1.5 to 1.5
- doc_ids: int32 [16384], P('tok'), may hold values from 0 to 63, never falling along the last dimension, each value on 1 to 512 neighbouring positions
- gains: float32 [5, 2048], replicated, may hold values from 0.5 to 1.5
- w_qkv: bfloat16 [2048, 3, 2048], P('tok', None, 'hist'), may hold values from -0.125 to 0.125
- w_out: bfloat16 [2048, 2048], P('tok', 'hist'), may hold values from -1 to 1
- w_up: bfloat16 [2048, 8192], P('tok', 'hist'), may hold values from -0.125 to 0.125
- w_down: bfloat16 [2048, 8192], P('tok', 'hist'), may hold values from -0.1875 to 0.1875
- da_in: bfloat16 [2048, 100], replicated, may hold values from -0.125 to 0.125
- da_out: bfloat16 [100, 100], replicated, may hold values from -0.625 to 0.625
- da_bias: float32 [100], replicated, may hold values from -3 to 3
- out_grad: bfloat16 [16384, 2048], P(('tok', 'hist')), may hold values from -6 to 6
- mix_grad_in: float32 [16384, 100], P(('tok', 'hist')), may hold values from -6 to 6
Outputs:
- block_out: bfloat16 [16384, 2048], P(('tok', 'hist'))
- mix_next: float32 [16384, 100], P(('tok', 'hist'))
- history_grad: bfloat16 [24, 16384, 2048], P('hist', 'tok')
- mix_grad: float32 [4, 24, 16384], P(None, 'hist', 'tok')
- gains_grad: float32 [5, 2048], replicated
- w_qkv_grad: float32 [2048, 3, 2048], P('tok', None, 'hist')
- w_out_grad: float32 [2048, 2048], P('tok', 'hist')
- w_up_grad: float32 [2048, 8192], P('tok', 'hist')
- w_down_grad: float32 [2048, 8192], P('tok', 'hist')
- da_in_grad: float32 [2048, 100], replicated
- da_out_grad: float32 [100, 100], replicated
- da_bias_grad: float32 [100], replicated
The draws below stay inside these ranges and needn't reach their ends.
Inputs may be any that keep to these rules, and one draw needn't show every extreme that they name: A permutation: slot j of history holds history entry layer_ids[j]. `doc_ids`: never decrease along the tokens; no document has more than 512 tokens; a sequence may begin or end inside a document.
All inputs are finite; a program needn't handle non-finite values.
Results may differ from the reference program's by a relative error of at most 0.04.
Values may be sent and summed in bfloat16 or wider, within the bound.
A program may use at most 192 MiB of HBM per device.

```python
import math
import jax
import jax.numpy as jnp
import numpy as np
from jax import lax

D = 2048
HEADS = 16
HD = 128
ROT = 32
FF = 8192
HIST = 24
STREAMS = 4
MIXO = 100
SEQ = 1024
TOKENS = 16384
N_HIST = 8
N_TOK = 16


def block_levels(stream_key, shape, cuts, least, largest):
    level = 1.0
    for position, blocks in cuts:
        heights = jax.random.uniform(jax.random.fold_in(jax.random.fold_in(stream_key, 6), position), (blocks,), jnp.float32, least / len(cuts), largest / len(cuts))
        level = level * jnp.repeat(jnp.exp(heights), shape[position] // blocks).reshape((-1,) + (1,) * (len(shape) - 1 - position))
    return level


def profile(amount, total, bound, lean):
    weights = [(1 << 20) // math.isqrt(grade ** lean) + 1 for grade in range(2, amount + 1)]
    surplus, counts = total - bound - (amount - 1), [1] * (amount - 1)
    while surplus > 0:
        free = [i for i in range(amount - 1) if counts[i] < bound]
        whole, budget = sum([weights[i] for i in free]), surplus
        for i in free:
            more = min(bound - counts[i], max(1, budget * weights[i] // whole), surplus)
            counts[i] = counts[i] + more
            surplus = surplus - more
    return np.array([bound] + counts)


def ragged(key, amount, total, reach, skew):
    if amount == 2:
        one = jax.random.randint(key, (), max(1, total - reach), min(reach, total - 1) + 1)
        return jnp.stack([one, total - one])
    tallies = jnp.asarray(profile(amount, total, reach, skew), jnp.int32)
    twos = (amount - 1) // 2
    source_of, sink = tallies[1:1 + 2 * twos:2], tallies[2:2 + 2 * twos:2]
    slack = jnp.minimum(source_of - 1, reach - sink)
    passed = jax.random.randint(jax.random.fold_in(key, 1), (twos,), 0, 1 << 20) % (slack + 1)
    tallies = tallies.at[1:1 + 2 * twos:2].set(source_of - passed).at[2:2 + 2 * twos:2].set(sink + passed)
    return tallies[jax.random.permutation(jax.random.fold_in(key, 2), amount)]


def gaussian(rng, dims, deviation, most, split=(), kind=jnp.bfloat16):
    level = block_levels(rng, dims, split, -0.22, 0.18) if split else 1.0
    result = jax.random.normal(rng, dims, jnp.float32) * deviation * level
    return jnp.minimum(jnp.maximum(result, -most), most).astype(kind)


def setup_inputs(seed: int = 0) -> dict:
    splits = jax.random.split(jax.random.key(seed), 15)
    return {
        "history": gaussian(splits[0], (HIST, TOKENS, D), 1.0, 6.0, ((0, 8), (1, 16))),
        "layer_ids": jax.random.permutation(splits[1], HIST).astype(jnp.int32),
        "mix_weights": gaussian(splits[2], (STREAMS, HIST, TOKENS), 0.25, 1.5, ((2, 16),), jnp.float32),
        "doc_ids": jnp.searchsorted(jnp.cumsum(ragged(splits[3], 4 * N_TOK, TOKENS, SEQ // 2, 1)), jnp.arange(TOKENS), side="right").astype(jnp.int32),
        "gains": jnp.clip(1.0 + 0.1 * jax.random.normal(splits[4], (5, D), jnp.float32), 0.5, 1.5),
        "w_qkv": gaussian(splits[5], (D, 3, D), D ** -0.5, 0.125, ((0, 16), (2, 8))),
        "w_out": gaussian(splits[6], (D, D), (D // 64) ** -0.5, 1.0, ((0, 16), (1, 8))),
        "w_up": gaussian(splits[7], (D, FF), D ** -0.5, 0.125, ((0, 16), (1, 8))),
        "w_down": gaussian(splits[8], (D, FF), (FF // 8) ** -0.5, 0.1875, ((0, 16), (1, 8))),
        "da_in": gaussian(splits[9], (D, MIXO), D ** -0.5, 0.125),
        "da_out": gaussian(splits[10], (MIXO, MIXO), MIXO ** -0.5, 0.625),
        "da_bias": gaussian(splits[11], (MIXO,), 0.5, 3.0, (), jnp.float32),
        "out_grad": gaussian(splits[12], (TOKENS, D), 1.0, 6.0, ((0, 128),)),
        "mix_grad_in": gaussian(splits[13], (TOKENS, MIXO), 1.0, 6.0, ((0, 128),), jnp.float32),
    }


HIGHEST = lax.Precision.HIGHEST
EPSILON = 1e-05
NEGATIVE = -1e+30

@jax.custom_vjp
def low(v):
    return lax.optimization_barrier(v.astype(jnp.bfloat16)).astype(jnp.float32)

@jax.custom_vjp
def low_back(v):
    return v

def low_keep(v):
    return (low(v), None)

def low_pass(kept, grad):
    return (grad,)

def back_keep(v):
    return (v, None)

def back_low(kept, grad):
    return (low(grad),)
low.defvjp(low_keep, low_pass)
low_back.defvjp(back_keep, back_low)

def exact_dot(left_side, right_side):
    return jnp.dot(left_side, right_side, precision=HIGHEST)

def layer_norm(values, gain):
    row_mean = lax.optimization_barrier(jnp.mean(values, axis=-1, keepdims=True))
    centered = values - row_mean
    return centered * lax.rsqrt(lax.optimization_barrier(jnp.mean(centered * centered, axis=-1, keepdims=True)) + EPSILON) * gain

def rotary_tables(length, rotated):
    half_rot = rotated // 2
    frequency = 10000.0 ** (-2.0 * jnp.arange(half_rot, dtype=jnp.float32) / rotated)
    angles = jnp.arange(length, dtype=jnp.float32)[:, None] * frequency[None, :]
    return (jnp.cos(angles), jnp.sin(angles))

def rotate(values, cosine, sine_table, direction):
    half_rot = cosine.shape[1]
    first_half = values[..., :half_rot]
    second_half = values[..., half_rot:2 * half_rot]
    cos_part = cosine[:, None, :]
    sin_part = direction * sine_table[:, None, :]
    return jnp.concatenate([first_half * cos_part - second_half * sin_part, second_half * cos_part + first_half * sin_part, values[..., 2 * half_rot:]], axis=-1)

def gelu_exact(values):
    return jax.nn.gelu(values, approximate=False)

def forward(history, mix_weights, gains, w_qkv, w_out, w_up, w_down, da_in, da_out, da_bias, layer_ids, doc_ids):
    per_group = HIST // N_HIST
    slot_weights = mix_weights[:, layer_ids, :]
    streams = jnp.zeros((STREAMS, SEQ, D), jnp.float32)
    for group_idx in range(N_HIST):
        partial_sum = jnp.zeros((STREAMS, SEQ, D), jnp.float32)
        for inner_idx in range(per_group):
            slot_idx = group_idx * per_group + inner_idx
            partial_sum = partial_sum + slot_weights[:, slot_idx, :, None] * history[slot_idx][None]
        streams = streams + low(partial_sum)
    streams = low_back(streams)
    cosine, sine_table = rotary_tables(SEQ, ROT)
    normed = [low(layer_norm(streams[which], gains[which])) for which in range(3)]
    queries = low_back(exact_dot(normed[0], w_qkv[:, 0, :])).reshape(SEQ, HEADS, HD)
    queries = low(rotate(queries, cosine, sine_table, 1.0))
    keys = low_back(exact_dot(normed[1], w_qkv[:, 1, :])).reshape(SEQ, HEADS, HD)
    keys = low(rotate(keys, cosine, sine_table, 1.0))
    values = low(low_back(exact_dot(normed[2], w_qkv[:, 2, :]))).reshape(SEQ, HEADS, HD)
    positions = jnp.arange(SEQ, dtype=jnp.int32)
    allowed = (positions[None, :] <= positions[:, None]) & (doc_ids[None, :] == doc_ids[:, None])
    scores = low_back(jnp.einsum('qhd,khd->hqk', queries, keys, precision=HIGHEST) * HD ** (-0.5))
    scores = jnp.where(allowed[None], scores, NEGATIVE)
    probs = jax.nn.softmax(scores, axis=-1)
    heads_out = jnp.einsum('hqk,khd->qhd', low(probs), values, precision=HIGHEST).reshape(SEQ, D)
    heads_out = low(low_back(heads_out))
    head_cols = D // N_HIST
    attn = jnp.zeros((SEQ, D), jnp.float32)
    for group_idx in range(N_HIST):
        cols = slice(group_idx * head_cols, (group_idx + 1) * head_cols)
        attn = attn + low(exact_dot(heads_out[:, cols], w_out[:, cols].T))
    attn = low_back(attn)
    residual = streams[3] + attn
    mid_norm = low(layer_norm(residual, gains[3]))
    up_proj = low_back(exact_dot(mid_norm, w_up))
    activated = low(gelu_exact(up_proj))
    hidden_cols = FF // N_HIST
    mlp = jnp.zeros((SEQ, D), jnp.float32)
    for group_idx in range(N_HIST):
        cols = slice(group_idx * hidden_cols, (group_idx + 1) * hidden_cols)
        mlp = mlp + low(exact_dot(activated[:, cols], w_down[:, cols].T))
    mlp = low_back(mlp)
    layer_out = residual + mlp
    rms_unit = layer_out * lax.rsqrt(lax.optimization_barrier(jnp.mean(layer_out * layer_out, axis=-1, keepdims=True)) + EPSILON)
    da_norm = low(rms_unit * gains[4])
    inner_pre = low_back(exact_dot(da_norm, da_in))
    mix_next = low_back(exact_dot(low(gelu_exact(inner_pre)), da_out)) + da_bias
    return (layer_out, mix_next)

def reference(history, layer_ids, mix_weights, doc_ids, gains, w_qkv, w_out, w_up, w_down, da_in, da_out, da_bias, out_grad, mix_grad_in):
    weights = (gains, w_qkv.astype(jnp.float32), w_out.astype(jnp.float32), w_up.astype(jnp.float32), w_down.astype(jnp.float32), da_in.astype(jnp.float32), da_out.astype(jnp.float32), da_bias)
    n_seqs = history.shape[1] // SEQ

    def one_seq(totals, seq_idx):
        begin_row = (seq_idx * SEQ).astype(jnp.int32)
        seq_hist = lax.dynamic_slice_in_dim(history, begin_row, SEQ, 1).astype(jnp.float32)
        seq_mix = lax.dynamic_slice_in_dim(mix_weights, begin_row, SEQ, 2)
        seq_docs = lax.dynamic_slice_in_dim(doc_ids, begin_row, SEQ, 0)
        cot_block = lax.dynamic_slice_in_dim(out_grad, begin_row, SEQ, 0).astype(jnp.float32)
        cot_mix = lax.dynamic_slice_in_dim(mix_grad_in, begin_row, SEQ, 0)

        def apply_layer(hist_in, mix_in, *params):
            return forward(hist_in, mix_in, *params, layer_ids, seq_docs)
        (layer_out, mix_next), pullback = jax.vjp(apply_layer, seq_hist, seq_mix, *weights)
        grads = pullback((cot_block, cot_mix))
        totals = tuple((acc + extra for acc, extra in zip(totals, grads[2:])))
        return (totals, (layer_out.astype(jnp.bfloat16), mix_next, grads[0].astype(jnp.bfloat16), grads[1][:, layer_ids, :]))
    zero_totals = tuple((jnp.zeros_like(param) for param in weights))
    totals, (blocks, mixes, hist_grads, mix_grads) = lax.scan(one_seq, zero_totals, jnp.arange(n_seqs, dtype=jnp.int32))
    block_out = blocks.reshape(n_seqs * SEQ, D)
    mix_next = mixes.reshape(n_seqs * SEQ, MIXO)
    history_grad = jnp.transpose(hist_grads, (1, 0, 2, 3)).reshape(HIST, n_seqs * SEQ, D)
    mix_grad = jnp.transpose(mix_grads, (1, 2, 0, 3)).reshape(STREAMS, HIST, n_seqs * SEQ)
    return (block_out, mix_next, history_grad, mix_grad, totals[0], totals[1], totals[2], totals[3], totals[4], totals[5], totals[6], totals[7])
```

```python
import jax
import jax.numpy as jnp
from jax import lax
from jax.experimental import pallas as pl
from jax.experimental.pallas import tpu as pltpu
from jax.sharding import PartitionSpec as P

HD = 128
ROT = 32


EPSILON = 1e-05
NEGATIVE = -1e30
HIGHEST = lax.Precision.HIGHEST


def norm_rows(values):
    row_mean = jnp.mean(values, axis=-1, keepdims=True)
    centered = values - row_mean
    inv_std = lax.rsqrt(jnp.mean(centered * centered, axis=-1, keepdims=True) + EPSILON)
    return (centered * inv_std, inv_std)


def norm_back(grad_unit, norm_unit, inv_std):
    return inv_std * (
        grad_unit
        - jnp.mean(grad_unit, axis=-1, keepdims=True)
        - norm_unit * jnp.mean(grad_unit * norm_unit, axis=-1, keepdims=True)
    )


def gelu_slope(values):
    return (
        0.5 * (1.0 + lax.erf(values * 0.7071067811865476))
        + values * jnp.exp(-0.5 * values * values) * 0.3989422804014327
    )


def rotary_tables(length, rotated):
    half_rot = rotated // 2
    frequency = 10000.0 ** (-2.0 * jnp.arange(half_rot, dtype=jnp.float32) / rotated)
    angles = jnp.arange(length, dtype=jnp.float32)[:, None] * frequency[None, :]
    return (jnp.cos(angles), jnp.sin(angles))


def rotate(values, cosine, sine_table, direction):
    half_rot = cosine.shape[1]
    first_half = values[..., :half_rot]
    second_half = values[..., half_rot : 2 * half_rot]
    cos_part = cosine[:, None, :]
    sin_part = direction * sine_table[:, None, :]
    return jnp.concatenate(
        [
            first_half * cos_part - second_half * sin_part,
            second_half * cos_part + first_half * sin_part,
            values[..., 2 * half_rot :],
        ],
        axis=-1,
    )


def contract(left_side, right_side, left_dim, right_dim):
    return lax.dot_general(
        left_side,
        right_side,
        (((left_dim,), (right_dim,)), ((), ())),
        preferred_element_type=jnp.float32,
    )


MESH = pl.DeviceIdType.MESH
ANY = pl.BlockSpec(memory_space=pl.ANY)
BF16 = jnp.bfloat16
BLOCK = 128


def coords():
    hist = lax.axis_index("hist")
    tok = lax.axis_index("tok")
    return hist // 2, hist % 2, tok // 8, (tok // 2) % 4, tok % 2


def device(x, zl, zh, y, c):
    return (x * 2 + zl, zh * 8 + y * 2 + c)


def greet(peers):
    barrier = pltpu.get_barrier_semaphore()
    for peer in peers:
        pl.semaphore_signal(barrier, inc=1, device_id=peer, device_id_type=MESH)
    pl.semaphore_wait(barrier, len(peers))


def remote(src, dst, send_sem, recv_sem, peer):
    return pltpu.make_async_remote_copy(
        src_ref=src,
        dst_ref=dst,
        send_sem=send_sem,
        recv_sem=recv_sem,
        device_id=peer,
        device_id_type=MESH,
    )


def comm_call(kernel, out_shapes, sems, collective_id, name, *args):
    return pl.pallas_call(
        kernel,
        out_shape=out_shapes,
        in_specs=[ANY] * len(args),
        out_specs=[ANY] * len(out_shapes),
        scratch_shapes=[
            pltpu.SemaphoreType.DMA((sems,)),
            pltpu.SemaphoreType.DMA((sems,)),
            pltpu.SemaphoreType.DMA((4,)),
        ],
        compiler_params=pltpu.CompilerParams(collective_id=collective_id, has_side_effects=True),
        name=name,
    )(*args)


def shape(dims, dtype=BF16):
    return jax.ShapeDtypeStruct(dims, dtype)


def x_peers(x, zl, zh, y, c):
    return [((x + k) % 4, device((x + k) % 4, zl, zh, y, c)) for k in (1, 3, 2)]


def gather_x(shard, collective_id, name):
    n, rows, width = shard.shape

    def kernel(src, dst, send, recv, local):
        x, zl, zh, y, c = coords()
        peers = x_peers(x, zl, zh, y, c)
        greet([peer for _, peer in peers])
        copies = []
        for j in range(n):
            for k, (_, peer) in enumerate(peers):
                i = j * 3 + k
                copies.append(remote(src.at[j], dst.at[j, x], send.at[i], recv.at[i], peer))
                copies[-1].start()
        own = pltpu.make_async_copy(src, dst.at[:, x], local.at[0])
        own.start()
        own.wait()
        for copy in copies:
            copy.wait()

    return comm_call(kernel, [shape((n, 4, rows, width))], 3 * n, collective_id, name, shard)[0]


def scatter_x(parts, collective_id, name):
    n, _, rows, width = parts.shape

    def kernel(src, dst, send, recv, local):
        x, zl, zh, y, c = coords()
        peers = x_peers(x, zl, zh, y, c)
        greet([peer for _, peer in peers])
        copies = []
        for j in range(n):
            for k, (px, peer) in enumerate(peers):
                i = j * 3 + k
                copies.append(remote(src.at[j, px], dst.at[j, x], send.at[i], recv.at[i], peer))
                copies[-1].start()
        own = pltpu.make_async_copy(src.at[:, x], dst.at[:, x], local.at[0])
        own.start()
        own.wait()
        for copy in copies:
            copy.wait()

    return comm_call(kernel, [shape(parts.shape)], 3 * n, collective_id, name, parts)[0]


def swap_z(mine, collective_id, name):
    def kernel(src, dst, send, recv, local):
        x, zl, zh, y, c = coords()
        peer = device(x, 1 - zl, zh, y, c)
        greet([peer])
        copy = remote(src, dst, send.at[0], recv.at[0], peer)
        copy.start()
        copy.wait()

    return comm_call(kernel, [shape(mine.shape)], 1, collective_id, name, mine)[0]


def hist_peers(x, zl):
    steps = ((0, 1), (1, 0), (3, 0), (1, 1), (3, 1), (2, 0), (2, 1))
    return [((x + dx) % 4, (zl + dz) % 2) for dx, dz in steps]


def collect(history, small, large):
    slots, _, width = history.shape

    def kernel(hist, wa, wb, own_hist, full_a, full_b, send, recv, local):
        x, zl, zh, y, c = coords()
        place = x * 2 + zl
        partner = device(x, 1 - zl, zh, y, c)
        across = device(x, 1 - zl, 1 - zh, y, c)
        sibling = device(x, zl, zh, y, 1 - c)
        rows_of = [device(x, zl, zh, (y + k) % 4, c) for k in (1, 3, 2)]
        others = hist_peers(x, zl)
        hist_devices = [device(px, pz, zh, y, c) for px, pz in others]
        greet(hist_devices + [across, sibling] + rows_of)

        def view(ref, b_zl, b_zh, b_y, b_c):
            wide = ref.shape[2] // 2
            row = (b_zh * 8 + b_y * 2 + b_c) * BLOCK
            return ref.at[
                :, pl.ds(pl.multiple_of(row, BLOCK), BLOCK), pl.ds(pl.multiple_of(b_zl * wide, wide), wide)
            ]

        fulls = (full_a, full_b)
        z_of = [(zl, zh), (1 - zl, zh), (1 - zl, 1 - zh), (zl, 1 - zh)]
        base = 7 * slots

        def arrived(zi, k, sib=0):
            steps = (0, 1, 3, 2)
            by = (y + 4 - steps[k]) % 4
            bc = 1 - c if sib else c
            out = []
            for a, full in enumerate(fulls):
                ref = view(full, *z_of[zi], by, bc)
                out.append((ref, base + ((zi * 4 + k) * 2 + sib) * 2 + a))
            return out

        def wait_block(zi, k, sib=0):
            for ref, i in arrived(zi, k, sib):
                remote(ref, ref, send.at[i], recv.at[i], sibling).wait_recv()

        started = []

        def push(src, dst, i, peer):
            copy = remote(src, dst, send.at[i], recv.at[i], peer)
            copy.start()
            started.append(copy)

        own_blocks = [view(full, zl, zh, y, c) for full in fulls]
        for a, src in enumerate((wa, wb)):
            push(src, own_blocks[a], base + (1 * 4 * 2) * 2 + a, partner)
        for a, src in enumerate((wa, wb)):
            push(src, own_blocks[a], base + (2 * 4 * 2) * 2 + a, across)
        for j in range(slots):
            for k, (px, pz) in enumerate(others):
                rows = pl.ds(pl.multiple_of((px * 2 + pz) * BLOCK, BLOCK), BLOCK)
                push(hist.at[j, rows], own_hist.at[place, j], k * slots + j, hist_devices[k])
        locals_ = [
            pltpu.make_async_copy(
                hist.at[:, pl.ds(pl.multiple_of(place * BLOCK, BLOCK), BLOCK)], own_hist.at[place], local.at[0]
            ),
            pltpu.make_async_copy(wa, own_blocks[0], local.at[1]),
            pltpu.make_async_copy(wb, own_blocks[1], local.at[2]),
        ]
        for copy in locals_:
            copy.start()

        def spread(zi, sources):
            for a, src in enumerate(sources):
                dst = view(fulls[a], *z_of[zi], y, c)
                for k, peer in enumerate(rows_of):
                    push(src, dst, base + ((zi * 4 + k + 1) * 2) * 2 + a, peer)
                push(src, dst, base + ((zi * 4) * 2 + 1) * 2 + a, sibling)

        spread(0, (wa, wb))
        wait_block(1, 0)
        for a, (ref, _) in enumerate(arrived(1, 0)):
            push(ref, ref, base + (3 * 4 * 2) * 2 + a, across)
        spread(1, [ref for ref, _ in arrived(1, 0)])
        wait_block(2, 0)
        spread(2, [ref for ref, _ in arrived(2, 0)])
        wait_block(3, 0)
        spread(3, [ref for ref, _ in arrived(3, 0)])
        for zi in range(4):
            for k in range(1, 4):
                wait_block(zi, k)
                for a, (ref, _) in enumerate(arrived(zi, k)):
                    push(ref, ref, base + ((zi * 4 + k) * 2 + 1) * 2 + a, sibling)
        for zi in range(4):
            for k in range(4):
                wait_block(zi, k, 1)
        for k, (px, pz) in enumerate(others):
            for j in range(slots):
                i = k * slots + j
                ref = own_hist.at[px * 2 + pz, j]
                remote(ref, ref, send.at[i], recv.at[i], sibling).wait_recv()
        for copy in started:
            copy.wait_send()
        for copy in locals_:
            copy.wait()

    n_a, rows_a, cols_a = small.shape
    n_b, rows_b, cols_b = large.shape
    return comm_call(
        kernel,
        [
            shape((8, slots, BLOCK, width)),
            shape((n_a, rows_a * 16, cols_a * 2)),
            shape((n_b, rows_b * 16, cols_b * 2)),
        ],
        7 * slots + 64,
        1,
        "collect",
        history,
        small,
        large,
    )


def swap_core(small, large, collective_id):
    def kernel(ga, gb, oa, ob, send, recv, local):
        x, zl, zh, y, c = coords()
        peer = device(x, zl, zh, y, 1 - c)
        greet([peer])
        copies = [
            remote(src.at[:, :, 1 - c], dst, send.at[i], recv.at[i], peer)
            for i, (src, dst) in enumerate(((ga, oa), (gb, ob)))
        ]
        for copy in copies:
            copy.start()
        for copy in copies:
            copy.wait()

    outs = [shape(g.shape[:2] + g.shape[3:]) for g in (small, large)]
    return comm_call(kernel, outs, 2, collective_id, "swap_core", small, large)


def hand_out(hist_grad, mix_grad, small, large, collective_id):
    groups, slots, rows, width = hist_grad.shape

    def kernel(hg, mg, ga, gb, ohg, omg, oa, ob, send, recv, local):
        x, zl, zh, y, c = coords()
        place = x * 2 + zl
        others = hist_peers(x, zl)
        hist_devices = [device(px, pz, zh, y, c) for px, pz in others]
        ys = [(y + k) % 4 for k in (1, 3, 2)]
        y_devices = [device(x, zl, zh, py, c) for py in ys]
        greet(hist_devices + y_devices)
        copies = []

        def push(src, dst, peer):
            i = len(copies)
            copies.append(remote(src, dst, send.at[i], recv.at[i], peer))
            copies[-1].start()

        own_rows = pl.ds(pl.multiple_of(place * BLOCK, BLOCK), BLOCK)
        for (px, pz), peer in zip(others, hist_devices):
            push(mg.at[px * 2 + pz], omg.at[place], peer)
        for py, peer in zip(ys, y_devices):
            push(gb.at[:, :, py], ob.at[y], peer)
            push(ga.at[:, :, py], oa.at[y], peer)
        for j in range(slots):
            for (px, pz), peer in zip(others, hist_devices):
                push(hg.at[px * 2 + pz, j], ohg.at[j, own_rows], peer)
        locals_ = [
            pltpu.make_async_copy(hg.at[place], ohg.at[:, own_rows], local.at[0]),
            pltpu.make_async_copy(mg.at[place], omg.at[place], local.at[1]),
            pltpu.make_async_copy(ga.at[:, :, y], oa.at[y], local.at[2]),
            pltpu.make_async_copy(gb.at[:, :, y], ob.at[y], local.at[3]),
        ]
        for copy in locals_:
            copy.start()
        for copy in copies + locals_:
            copy.wait()

    outs = [
        shape((slots, groups * rows, width)),
        shape(mix_grad.shape, jnp.float32),
    ] + [shape((4,) + g.shape[:2] + g.shape[3:]) for g in (small, large)]
    return comm_call(
        kernel, outs, 7 * (slots + 1) + 6, collective_id, "hand_out", hist_grad, mix_grad, small, large
    )


def scatter_z(small, large, collective_id):
    def kernel(ga, gb, oa, ob, send, recv, local):
        x, zl, zh, y, c = coords()
        places = [(1 - zl, zh), (1 - zl, 1 - zh), (zl, 1 - zh)]
        peers = [device(x, pl_, ph, y, c) for pl_, ph in places]
        greet(peers)
        mine = zh * 2 + zl

        def part(ref, p_zl, p_zh):
            wide = ref.shape[3] // 2
            return ref.at[:, p_zh, :, pl.ds(pl.multiple_of(p_zl * wide, wide), wide)]

        copies = []
        for place, peer in zip(places, peers):
            for src, dst in ((ga, oa), (gb, ob)):
                i = len(copies)
                copies.append(remote(part(src, *place), dst.at[mine], send.at[i], recv.at[i], peer))
                copies[-1].start()
        locals_ = [
            pltpu.make_async_copy(part(src, zl, zh), dst.at[mine], local.at[i])
            for i, (src, dst) in enumerate(((ga, oa), (gb, ob)))
        ]
        for copy in locals_:
            copy.start()
        for copy in copies + locals_:
            copy.wait()

    outs = [shape((4, g.shape[0], g.shape[2], g.shape[3] // 2)) for g in (small, large)]
    return comm_call(kernel, outs, 6, collective_id, "scatter_z", small, large)


def body(
    history,
    layer_ids,
    mix_weights,
    doc_ids,
    gains,
    w_qkv,
    w_out,
    w_up,
    w_down,
    da_in,
    da_out,
    da_bias,
    out_grad,
    mix_grad_in,
):
    place = lax.axis_index("hist")
    low_z = place % 2
    core = lax.axis_index("tok") % 2
    slots, seq_len, width = history.shape
    small = jnp.concatenate([jnp.transpose(w_qkv, (1, 0, 2)), w_out[None]], axis=0)
    large = jnp.stack([w_up, w_down], axis=0)
    own_hist, full_small, full_large = collect(history, small, large)
    w_q, w_k, w_v, full_out = (full_small[i] for i in range(4))
    full_up, full_down = full_large[0], full_large[1]
    own_hist = own_hist.reshape(8 * slots, BLOCK, width)

    own_mix = lax.dynamic_slice_in_dim(mix_weights, place * BLOCK, BLOCK, 2)
    pick = (layer_ids[:, None] == jnp.arange(own_mix.shape[1], dtype=jnp.int32)[None, :]).astype(jnp.float32)
    slot_weights = jnp.einsum("jl,slt->sjt", pick, own_mix, precision=HIGHEST)
    owned = jnp.zeros((4, BLOCK, width), jnp.float32)
    for j in range(8 * slots):
        owned = owned + slot_weights[:, j, :, None] * own_hist[j][None].astype(jnp.float32)

    norm_unit, inv_std = norm_rows(owned[:3])
    normed = (norm_unit * gains[:3, None, :]).astype(BF16)
    gathered = gather_x(normed, 2, "gather_normed").reshape(3, 4 * BLOCK, width)
    rows_here = 4 * BLOCK
    heads_here = full_out.shape[1] // HD
    cosine, sine_table = rotary_tables(seq_len, ROT)

    def here(table):
        return lax.dynamic_index_in_dim(table.reshape(4, 2, BLOCK, -1), low_z, 1, False).reshape(rows_here, -1)

    cos_here, sin_here = here(cosine), here(sine_table)

    def project(which, weight):
        return jnp.dot(gathered[which], weight, preferred_element_type=jnp.float32).reshape(
            rows_here, heads_here, HD
        )

    queries = rotate(project(0, w_q), cos_here, sin_here, 1.0).astype(BF16)
    keys_here = rotate(project(1, w_k), cos_here, sin_here, 1.0).astype(BF16)
    values_here = project(2, w_v).astype(BF16)
    mine = jnp.stack([keys_here, values_here]).reshape(2, 4, BLOCK, heads_here * HD)
    theirs = swap_z(mine, 3, "swap_keys")

    def interleave(own, other):
        first = jnp.where(low_z == 0, own, other)
        second = jnp.where(low_z == 0, other, own)
        return jnp.stack([first, second], axis=1)

    keys = interleave(mine[0], theirs[0]).reshape(seq_len, heads_here, HD)
    values = interleave(mine[1], theirs[1]).reshape(seq_len, heads_here, HD)
    key_pos = jnp.arange(seq_len, dtype=jnp.int32)
    query_pos = here(key_pos[:, None])[:, 0]
    query_docs = here(doc_ids[:, None])[:, 0]
    allowed = (key_pos[None, :] <= query_pos[:, None]) & (doc_ids[None, :] == query_docs[:, None])
    scale = HD ** (-0.5)
    scores = jnp.einsum("qhd,khd->hqk", queries, keys, preferred_element_type=jnp.float32) * scale
    scores = jnp.where(allowed[None], scores, NEGATIVE)
    row_max = jnp.max(scores, axis=-1, keepdims=True)
    shifted = jnp.exp(scores - row_max)
    row_total = jnp.sum(shifted, axis=-1, keepdims=True)
    probs = shifted / row_total
    attended = jnp.einsum("hqk,khd->qhd", probs.astype(BF16), values, preferred_element_type=jnp.float32)
    heads_flat = attended.reshape(rows_here, -1).astype(BF16)

    def reduce_rows(partial, collective_id, name):
        parts = scatter_x(partial.astype(BF16).reshape(-1, 4, BLOCK, width), collective_id, name)
        return jnp.sum(parts.astype(jnp.float32), axis=1)

    def all_rows(rows, collective_id, name):
        return gather_x(rows.astype(BF16)[None], collective_id, name).reshape(rows_here, width)

    attn_owned = reduce_rows(contract(heads_flat, full_out, 1, 1), 4, "scatter_attn")[0]
    residual = owned[3] + attn_owned
    mid_unit, mid_std = norm_rows(residual)
    mid_all = all_rows(mid_unit * gains[3], 5, "gather_mid")
    up_proj = jnp.dot(mid_all, full_up, preferred_element_type=jnp.float32)
    activated = jax.nn.gelu(up_proj, approximate=False).astype(BF16)
    mlp_owned = reduce_rows(contract(activated, full_down, 1, 1), 6, "scatter_mlp")[0]
    layer_out = residual + mlp_owned
    rms_inv = lax.rsqrt(jnp.mean(layer_out * layer_out, axis=-1, keepdims=True) + EPSILON)
    rms_unit = layer_out * rms_inv
    da_norm = (rms_unit * gains[4]).astype(BF16)
    inner_pre = jnp.dot(da_norm, da_in, preferred_element_type=jnp.float32)
    inner_act = jax.nn.gelu(inner_pre, approximate=False).astype(BF16)
    mix_next = jnp.dot(inner_act, da_out, preferred_element_type=jnp.float32) + da_bias
    bias_grad = jnp.sum(mix_grad_in, axis=0)
    mix_cot = mix_grad_in.astype(BF16)
    da_out_grad = contract(inner_act, mix_cot, 0, 0)
    inner_cot = (contract(mix_cot, da_out, 1, 1) * gelu_slope(inner_pre)).astype(BF16)
    da_in_grad = contract(da_norm, inner_cot, 0, 0)
    da_in_sum, da_out_sum, bias_sum = lax.psum((da_in_grad, da_out_grad, bias_grad), ("hist", "tok"))
    rms_grad = contract(inner_cot, da_in, 1, 1)
    rms_gain_grad = jnp.sum(rms_grad * rms_unit, axis=0)
    rms_scaled = rms_grad * gains[4]
    out_total = out_grad.astype(jnp.float32) + rms_inv * (
        rms_scaled - rms_unit * jnp.mean(rms_scaled * rms_unit, axis=-1, keepdims=True)
    )
    mlp_cot = all_rows(out_total, 7, "gather_mlp_cot")
    down_grad = contract(mlp_cot, activated, 0, 0)
    up_cot = (
        jnp.dot(mlp_cot, full_down, preferred_element_type=jnp.float32) * gelu_slope(up_proj)
    ).astype(BF16)
    up_grad = contract(mid_all, up_cot, 0, 0)
    mid_back = reduce_rows(contract(up_cot, full_up, 1, 1), 8, "scatter_mid")[0]
    mid_gain_grad = jnp.sum(mid_back * mid_unit, axis=0)
    residual_grad = out_total + norm_back(mid_back * gains[3], mid_unit, mid_std)
    attn_cot = all_rows(residual_grad, 9, "gather_attn_cot")
    out_proj_grad = contract(attn_cot, heads_flat, 0, 0)
    heads_cot = (
        jnp.dot(attn_cot, full_out, preferred_element_type=jnp.float32)
        .astype(BF16)
        .reshape(rows_here, heads_here, HD)
    )
    prob_grad = jnp.einsum("qhd,khd->hqk", heads_cot, values, preferred_element_type=jnp.float32)
    row_dot = jnp.sum(probs * prob_grad, axis=-1, keepdims=True)
    score_cot = (probs * (prob_grad - row_dot)).astype(BF16)
    query_grad = jnp.einsum("hqk,khd->qhd", score_cot, keys, preferred_element_type=jnp.float32) * scale
    key_grad = jnp.einsum("hqk,qhd->khd", score_cot, queries, preferred_element_type=jnp.float32) * scale
    value_grad = jnp.einsum("hqk,qhd->khd", probs.astype(BF16), heads_cot, preferred_element_type=jnp.float32)
    both = jnp.stack([key_grad, value_grad]).reshape(2, 4, 2, BLOCK, heads_here * HD)
    keep = lax.dynamic_index_in_dim(both, low_z, 2, False)
    give = lax.dynamic_index_in_dim(both, 1 - low_z, 2, False).astype(BF16)
    both = keep + swap_z(give, 10, "swap_key_grads").astype(jnp.float32)
    both = both.reshape(2, rows_here, heads_here, HD)
    proj_cots = (
        rotate(query_grad, cos_here, sin_here, -1.0).reshape(rows_here, -1).astype(BF16),
        rotate(both[0], cos_here, sin_here, -1.0).reshape(rows_here, -1).astype(BF16),
        both[1].reshape(rows_here, -1).astype(BF16),
    )
    small_grad = jnp.stack(
        [contract(gathered[which], proj_cots[which], 0, 0).astype(BF16) for which in range(3)]
        + [out_proj_grad.astype(BF16)]
    )
    large_grad = jnp.stack([up_grad.astype(BF16), down_grad.astype(BF16)])
    back_parts = jnp.stack(
        [contract(cot, weight, 1, 1).astype(BF16) for cot, weight in zip(proj_cots, (w_q, w_k, w_v))]
    )
    in_back = reduce_rows(back_parts, 11, "scatter_in")
    in_gain_grad = jnp.sum(in_back * norm_unit, axis=1)
    stream_part = norm_back(in_back * gains[:3, None, :], norm_unit, inv_std)
    stream_cot = jnp.concatenate([stream_part, residual_grad[None]], axis=0).astype(BF16)
    stream_wide = stream_cot.astype(jnp.float32)
    gains_local = jnp.concatenate([in_gain_grad, mid_gain_grad[None], rms_gain_grad[None]], axis=0)
    gains_sum = lax.psum(gains_local, ("hist", "tok"))

    hist_grads, mix_grads = [], []
    for j in range(8 * slots):
        hist_grads.append(jnp.sum(slot_weights[:, j, :, None] * stream_wide, axis=0).astype(BF16))
        mix_grads.append(jnp.sum(own_hist[j].astype(jnp.float32)[None] * stream_wide, axis=-1))
    hist_grads = jnp.stack(hist_grads).reshape(8, slots, BLOCK, width)
    mix_grads = jnp.stack(mix_grads).reshape(8, slots * 4, BLOCK)

    def by_core(grad):
        return grad.reshape(grad.shape[0], 8, 2, BLOCK, grad.shape[2])

    small_grad, large_grad = by_core(small_grad), by_core(large_grad)
    other_small, other_large = swap_core(small_grad, large_grad, 12)

    def add_core(grad, other):
        kept = lax.dynamic_index_in_dim(grad, core, 2, False)
        total = (kept.astype(jnp.float32) + other.astype(jnp.float32)).astype(BF16)
        return total.reshape(total.shape[0], 2, 4, BLOCK, total.shape[3])

    history_grad, mix_out, y_small, y_large = hand_out(
        hist_grads, mix_grads, add_core(small_grad, other_small), add_core(large_grad, other_large), 13
    )
    mix_grad = jnp.transpose(mix_out.reshape(8, slots, 4, BLOCK), (2, 1, 0, 3)).reshape(4, slots, seq_len)

    def add_four(parts):
        return jnp.sum(parts.astype(jnp.float32), axis=0)

    z_small, z_large = scatter_z(add_four(y_small).astype(BF16), add_four(y_large).astype(BF16), 14)
    small_sum, large_sum = add_four(z_small), add_four(z_large)
    return (
        layer_out.astype(BF16),
        mix_next,
        history_grad,
        mix_grad,
        gains_sum,
        jnp.transpose(small_sum[:3], (1, 0, 2)),
        small_sum[3],
        large_sum[0],
        large_sum[1],
        da_in_sum,
        da_out_sum,
        bias_sum,
    )


def solution(mesh):
    return jax.shard_map(
        body,
        mesh=mesh,
        in_specs=(
            P("hist", "tok", None),
            P(),
            P(None, None, "tok"),
            P("tok"),
            P(),
            P("tok", None, "hist"),
            P("tok", "hist"),
            P("tok", "hist"),
            P("tok", "hist"),
            P(),
            P(),
            P(),
            P(("tok", "hist"), None),
            P(("tok", "hist"), None),
        ),
        out_specs=(
            P(("tok", "hist"), None),
            P(("tok", "hist"), None),
            P("hist", "tok", None),
            P(None, "hist", "tok"),
            P(),
            P("tok", None, "hist"),
            P("tok", "hist"),
            P("tok", "hist"),
            P("tok", "hist"),
            P(),
            P(),
            P(),
        ),
        check_vma=False,
    )
```

```python
import jax
import jax.numpy as jnp
from jax import lax
from jax.experimental import pallas as pl
from jax.experimental.pallas import tpu as pltpu
from jax.sharding import PartitionSpec as P

HD = 128
ROT = 32


EPSILON = 1e-05
NEGATIVE = -1e30
HIGHEST = lax.Precision.HIGHEST


def norm_rows(values):
    row_mean = jnp.mean(values, axis=-1, keepdims=True)
    centered = values - row_mean
    inv_std = lax.rsqrt(jnp.mean(centered * centered, axis=-1, keepdims=True) + EPSILON)
    return (centered * inv_std, inv_std)


def norm_back(grad_unit, norm_unit, inv_std):
    return inv_std * (
        grad_unit
        - jnp.mean(grad_unit, axis=-1, keepdims=True)
        - norm_unit * jnp.mean(grad_unit * norm_unit, axis=-1, keepdims=True)
    )


def gelu_slope(values):
    return (
        0.5 * (1.0 + lax.erf(values * 0.7071067811865476))
        + values * jnp.exp(-0.5 * values * values) * 0.3989422804014327
    )


def rotary_tables(length, rotated):
    half_rot = rotated // 2
    frequency = 10000.0 ** (-2.0 * jnp.arange(half_rot, dtype=jnp.float32) / rotated)
    angles = jnp.arange(length, dtype=jnp.float32)[:, None] * frequency[None, :]
    return (jnp.cos(angles), jnp.sin(angles))


def rotate(values, cosine, sine_table, direction):
    half_rot = cosine.shape[1]
    first_half = values[..., :half_rot]
    second_half = values[..., half_rot : 2 * half_rot]
    cos_part = cosine[:, None, :]
    sin_part = direction * sine_table[:, None, :]
    return jnp.concatenate(
        [
            first_half * cos_part - second_half * sin_part,
            second_half * cos_part + first_half * sin_part,
            values[..., 2 * half_rot :],
        ],
        axis=-1,
    )


def contract(left_side, right_side, left_dim, right_dim):
    return lax.dot_general(
        left_side,
        right_side,
        (((left_dim,), (right_dim,)), ((), ())),
        preferred_element_type=jnp.float32,
    )


MESH = pl.DeviceIdType.MESH
ANY = pl.BlockSpec(memory_space=pl.ANY)
BF16 = jnp.bfloat16
BLOCK = 128


def coords():
    hist = lax.axis_index("hist")
    tok = lax.axis_index("tok")
    return hist // 2, hist % 2, tok // 8, (tok // 2) % 4, tok % 2


def device(x, zl, zh, y, c):
    return (x * 2 + zl, zh * 8 + y * 2 + c)


def greet(peers):
    barrier = pltpu.get_barrier_semaphore()
    for peer in peers:
        pl.semaphore_signal(barrier, inc=1, device_id=peer, device_id_type=MESH)
    pl.semaphore_wait(barrier, len(peers))


def remote(src, dst, send_sem, recv_sem, peer):
    return pltpu.make_async_remote_copy(
        src_ref=src,
        dst_ref=dst,
        send_sem=send_sem,
        recv_sem=recv_sem,
        device_id=peer,
        device_id_type=MESH,
    )


def comm_call(kernel, out_shapes, sems, collective_id, name, *args):
    return pl.pallas_call(
        kernel,
        out_shape=out_shapes,
        in_specs=[ANY] * len(args),
        out_specs=[ANY] * len(out_shapes),
        scratch_shapes=[
            pltpu.SemaphoreType.DMA((sems,)),
            pltpu.SemaphoreType.DMA((sems,)),
            pltpu.SemaphoreType.DMA((4,)),
        ],
        compiler_params=pltpu.CompilerParams(collective_id=collective_id, has_side_effects=True),
        name=name,
    )(*args)


def shape(dims, dtype=BF16):
    return jax.ShapeDtypeStruct(dims, dtype)


def x_peers(x, zl, zh, y, c):
    return [((x + k) % 4, device((x + k) % 4, zl, zh, y, c)) for k in (1, 3, 2)]


def z_peers(x, zl, zh, y, c):
    places = [(zh * 2 + zl + k) % 4 for k in (1, 3, 2)]
    return [(place, device(x, place % 2, place // 2, y, c)) for place in places]


def y_peers(x, zl, zh, y, c):
    return [((y + k) % 4, device(x, zl, zh, (y + k) % 4, c)) for k in (1, 3, 2)]


VMEM = pl.BlockSpec(memory_space=pltpu.VMEM)
SIDE_ROWS = 136


def exchange(src, slots, mine, peers, send, recv, first):
    copies = []
    for k, (place, peer) in enumerate(peers):
        part = src(place) if callable(src) else src
        copies.append(remote(part, slots.at[mine], send.at[first + k], recv.at[first + k], peer))
        copies[-1].start()
    return copies


def gather_x(shard, collective_id, name, down=None, up=None):
    n, rows, width = shard.shape
    side = 0 if down is None and up is None else 1

    def kernel(*refs):
        src, dst = refs[0], refs[1 + side]
        send, recv, local, sends, recvs = refs[2 + 2 * side : 7 + 2 * side]
        x, zl, zh, y, c = coords()
        z = zh * 2 + zl
        peers = x_peers(x, zl, zh, y, c)
        along_z = z_peers(x, zl, zh, y, c)
        along_y = y_peers(x, zl, zh, y, c)
        sibling = device(x, zl, zh, y, 1 - c)
        greeted = [peer for _, peer in peers]
        if side:
            greeted = greeted + [peer for _, peer in along_z + along_y]
        if down is not None:
            greeted = greeted + [sibling]
        greet(greeted)
        copies = []
        if down is not None:
            given, result = refs[1], refs[3]
            y_slots, z_part, z_slots, c_part, c_slot = refs[9:]
            first = exchange(lambda py: given.at[py], y_slots, y, along_y, sends, recvs, 0)
        if up is not None:
            given, result = refs[1], refs[3]
            x_slots, total = refs[9:]
            first = exchange(given, x_slots, x, peers, sends, recvs, 0)
        for j in range(n):
            for k, (_, peer) in enumerate(peers):
                i = j * 3 + k
                copies.append(remote(src.at[j], dst.at[j, x], send.at[i], recv.at[i], peer))
                copies[-1].start()
        own = pltpu.make_async_copy(src, dst.at[:, x], local.at[0])
        own.start()
        if down is not None:
            y_slots[y] = given[y]
            for copy in first:
                copy.wait()
            z_part[...] = y_slots[0] + y_slots[1] + y_slots[2] + y_slots[3]
            second = exchange(lambda pz: z_part.at[pz], z_slots, z, along_z, sends, recvs, 3)
            z_slots[z] = z_part[z]
            for copy in second:
                copy.wait()
            c_part[...] = z_slots[0] + z_slots[1] + z_slots[2] + z_slots[3]
            third = remote(c_part, c_slot, sends.at[6], recvs.at[6], sibling)
            third.start()
            third.wait()
            result[...] = c_part[...] + c_slot[...]
        if up is not None:
            x_slots[x] = given[...]
            for copy in first:
                copy.wait()
            total[y, z] = x_slots[0] + x_slots[1] + x_slots[2] + x_slots[3]
            second = exchange(total.at[y, z], total.at[y], z, along_z, sends, recvs, 3)
            for copy in second:
                copy.wait()
            third = exchange(total.at[y], total, y, along_y, sends, recvs, 6)
            for copy in third:
                copy.wait()
            result[...] = total[...]
        own.wait()
        for copy in copies:
            copy.wait()

    in_specs, args = [ANY], [shard]
    out_specs, outs = [ANY], [shape((n, 4, rows, width))]
    scratch = [
        pltpu.SemaphoreType.DMA((3 * n,)),
        pltpu.SemaphoreType.DMA((3 * n,)),
        pltpu.SemaphoreType.DMA((4,)),
        pltpu.SemaphoreType.DMA((9,)),
        pltpu.SemaphoreType.DMA((9,)),
    ]
    if side:
        in_specs, out_specs = [ANY, VMEM], [ANY, VMEM]
        args = [shard, down if up is None else up]
        piece = (SIDE_ROWS, 128)
        whole = (4, 4) + piece
        outs = outs + [shape(piece if up is None else whole, jnp.float32)]
        dims = (whole, (4,) + piece, (4,) + piece, piece, piece) if up is None else ((4,) + piece, whole)
        scratch = scratch + [pltpu.VMEM(d, jnp.float32) for d in dims]
    result = pl.pallas_call(
        kernel,
        out_shape=outs,
        in_specs=in_specs,
        out_specs=out_specs,
        scratch_shapes=scratch,
        compiler_params=pltpu.CompilerParams(
            collective_id=collective_id, has_side_effects=True, vmem_limit_bytes=24 * 2**20
        ),
        name=name,
    )(*args)
    return result if side else result[0]


def scatter_x(parts, collective_id, name):
    n, _, rows, width = parts.shape

    def kernel(src, dst, send, recv, local):
        x, zl, zh, y, c = coords()
        peers = x_peers(x, zl, zh, y, c)
        greet([peer for _, peer in peers])
        copies = []
        for j in range(n):
            for k, (px, peer) in enumerate(peers):
                i = j * 3 + k
                copies.append(remote(src.at[j, px], dst.at[j, x], send.at[i], recv.at[i], peer))
                copies[-1].start()
        own = pltpu.make_async_copy(src.at[:, x], dst.at[:, x], local.at[0])
        own.start()
        own.wait()
        for copy in copies:
            copy.wait()

    return comm_call(kernel, [shape(parts.shape)], 3 * n, collective_id, name, parts)[0]


def swap_z(mine, collective_id, name):
    def kernel(src, dst, send, recv, local):
        x, zl, zh, y, c = coords()
        peer = device(x, 1 - zl, zh, y, c)
        greet([peer])
        copy = remote(src, dst, send.at[0], recv.at[0], peer)
        copy.start()
        copy.wait()

    return comm_call(kernel, [shape(mine.shape)], 1, collective_id, name, mine)[0]


def hist_peers(x, zl):
    steps = ((0, 1), (1, 0), (3, 0), (1, 1), (3, 1), (2, 0), (2, 1))
    return [((x + dx) % 4, (zl + dz) % 2) for dx, dz in steps]


def collect(history, small, large):
    slots, _, width = history.shape

    def kernel(hist, wa, wb, own_hist, full_a, full_b, send, recv, local):
        x, zl, zh, y, c = coords()
        place = x * 2 + zl
        partner = device(x, 1 - zl, zh, y, c)
        across = device(x, 1 - zl, 1 - zh, y, c)
        sibling = device(x, zl, zh, y, 1 - c)
        rows_of = [device(x, zl, zh, (y + k) % 4, c) for k in (1, 3, 2)]
        others = hist_peers(x, zl)
        hist_devices = [device(px, pz, zh, y, c) for px, pz in others]
        greet(hist_devices + [across, sibling] + rows_of)

        def view(ref, b_zl, b_zh, b_y, b_c):
            wide = ref.shape[2] // 2
            row = (b_zh * 8 + b_y * 2 + b_c) * BLOCK
            return ref.at[
                :, pl.ds(pl.multiple_of(row, BLOCK), BLOCK), pl.ds(pl.multiple_of(b_zl * wide, wide), wide)
            ]

        fulls = (full_a, full_b)
        z_of = [(zl, zh), (1 - zl, zh), (1 - zl, 1 - zh), (zl, 1 - zh)]
        base = 7 * slots

        def arrived(zi, k, sib=0):
            steps = (0, 1, 3, 2)
            by = (y + 4 - steps[k]) % 4
            bc = 1 - c if sib else c
            out = []
            for a, full in enumerate(fulls):
                ref = view(full, *z_of[zi], by, bc)
                out.append((ref, base + ((zi * 4 + k) * 2 + sib) * 2 + a))
            return out

        def wait_block(zi, k, sib=0):
            for ref, i in arrived(zi, k, sib):
                remote(ref, ref, send.at[i], recv.at[i], sibling).wait_recv()

        started = []

        def push(src, dst, i, peer):
            copy = remote(src, dst, send.at[i], recv.at[i], peer)
            copy.start()
            started.append(copy)

        own_blocks = [view(full, zl, zh, y, c) for full in fulls]
        for a, src in enumerate((wa, wb)):
            push(src, own_blocks[a], base + (1 * 4 * 2) * 2 + a, partner)
        for a, src in enumerate((wa, wb)):
            push(src, own_blocks[a], base + (2 * 4 * 2) * 2 + a, across)
        for j in range(slots):
            for k, (px, pz) in enumerate(others):
                rows = pl.ds(pl.multiple_of((px * 2 + pz) * BLOCK, BLOCK), BLOCK)
                push(hist.at[j, rows], own_hist.at[place, j], k * slots + j, hist_devices[k])
        locals_ = [
            pltpu.make_async_copy(
                hist.at[:, pl.ds(pl.multiple_of(place * BLOCK, BLOCK), BLOCK)], own_hist.at[place], local.at[0]
            ),
            pltpu.make_async_copy(wa, own_blocks[0], local.at[1]),
            pltpu.make_async_copy(wb, own_blocks[1], local.at[2]),
        ]
        for copy in locals_:
            copy.start()

        def spread(zi, sources):
            for a, src in enumerate(sources):
                dst = view(fulls[a], *z_of[zi], y, c)
                for k, peer in enumerate(rows_of):
                    push(src, dst, base + ((zi * 4 + k + 1) * 2) * 2 + a, peer)
                push(src, dst, base + ((zi * 4) * 2 + 1) * 2 + a, sibling)

        spread(0, (wa, wb))
        wait_block(1, 0)
        for a, (ref, _) in enumerate(arrived(1, 0)):
            push(ref, ref, base + (3 * 4 * 2) * 2 + a, across)
        spread(1, [ref for ref, _ in arrived(1, 0)])
        wait_block(2, 0)
        spread(2, [ref for ref, _ in arrived(2, 0)])
        wait_block(3, 0)
        spread(3, [ref for ref, _ in arrived(3, 0)])
        for zi in range(4):
            for k in range(1, 4):
                wait_block(zi, k)
                for a, (ref, _) in enumerate(arrived(zi, k)):
                    push(ref, ref, base + ((zi * 4 + k) * 2 + 1) * 2 + a, sibling)
        for zi in range(4):
            for k in range(4):
                wait_block(zi, k, 1)
        for k, (px, pz) in enumerate(others):
            for j in range(slots):
                i = k * slots + j
                ref = own_hist.at[px * 2 + pz, j]
                remote(ref, ref, send.at[i], recv.at[i], sibling).wait_recv()
        for copy in started:
            copy.wait_send()
        for copy in locals_:
            copy.wait()

    n_a, rows_a, cols_a = small.shape
    n_b, rows_b, cols_b = large.shape
    return comm_call(
        kernel,
        [
            shape((8, slots, BLOCK, width)),
            shape((n_a, rows_a * 16, cols_a * 2)),
            shape((n_b, rows_b * 16, cols_b * 2)),
        ],
        7 * slots + 64,
        1,
        "collect",
        history,
        small,
        large,
    )


def send_hist(array, dx, dz=0):
    pairs = [(h, (h // 2 + dx) % 4 * 2 + (h % 2 + dz) % 2) for h in range(8)]
    return lax.ppermute(array, "hist", pairs)


def send_tok(array, dzh=0, dy=0, dc=0):
    pairs = [
        (t, (t // 8 + dzh) % 2 * 8 + (t // 2 % 4 + dy) % 4 * 2 + (t % 2 + dc) % 2) for t in range(16)
    ]
    return lax.ppermute(array, "tok", pairs)


def dot_nt(left, right):
    return lax.dot_general(left, right, (((1,), (1,)), ((), ())), preferred_element_type=jnp.float32)


def dot_nn(left, right):
    return lax.dot_general(left, right, (((1,), (0,)), ((), ())), preferred_element_type=jnp.float32)


def dot_tn(left, right):
    return lax.dot_general(left, right, (((0,), (0,)), ((), ())), preferred_element_type=jnp.float32)


def attend(queries, keys, values, other_keys, other_values, query_at, key_at):
    rows, cols = queries.shape
    heads = cols // HD
    scale = HD ** (-0.5)
    tall = 256

    def kernel(q, k, v, ok, ov, qa, ka, out, lse):
        for r in range(rows // tall):
            at = pl.ds(r * tall, tall)
            query_pos, query_doc = qa[at, 0:1], qa[at, 1:2]
            scores = []
            for half, key in enumerate((k, ok)):
                allowed = (ka[2 * half : 2 * half + 1, :] <= query_pos) & (
                    ka[2 * half + 1 : 2 * half + 2, :] == query_doc
                )
                scores.append(jnp.where(allowed, dot_nt(q[at, :], key[...]) * scale, NEGATIVE))
            top = jnp.maximum(
                jnp.max(scores[0], axis=1, keepdims=True), jnp.max(scores[1], axis=1, keepdims=True)
            )
            shifted = [jnp.exp(part - top) for part in scores]
            total = jnp.sum(shifted[0], axis=1, keepdims=True) + jnp.sum(shifted[1], axis=1, keepdims=True)
            share = 1.0 / total
            result = dot_nn((shifted[0] * share).astype(BF16), v[...])
            result = result + dot_nn((shifted[1] * share).astype(BF16), ov[...])
            out[at, :] = result.astype(BF16)
            lse[0, at, :] = top + jnp.log(total)

    head = pl.BlockSpec((rows, HD), lambda h: (0, h))
    return pl.pallas_call(
        kernel,
        grid=(heads,),
        out_shape=[shape((rows, cols)), shape((heads, rows, 1), jnp.float32)],
        in_specs=[head] * 5
        + [pl.BlockSpec(query_at.shape, lambda h: (0, 0)), pl.BlockSpec(key_at.shape, lambda h: (0, 0))],
        out_specs=[head, pl.BlockSpec((1, rows, 1), lambda h: (h, 0, 0))],
        compiler_params=pltpu.CompilerParams(vmem_limit_bytes=40 * 2**20),
        name="attend",
    )(queries, keys, values, other_keys, other_values, query_at, key_at)


def attend_back(queries, keys, values, other_keys, other_values, query_at, key_at, log_totals, out_cot):
    rows, cols = queries.shape
    heads = cols // HD
    scale = HD ** (-0.5)
    tall = 256

    def kernel(q, k, v, ok, ov, qa, ka, lse, cot, dq, dk, dv, dok, dov, key_sum, value_sum):
        for r in range(rows // tall):
            at = pl.ds(r * tall, tall)
            query_pos, query_doc = qa[at, 0:1], qa[at, 1:2]
            probs, prob_grads = [], []
            for half, (key, value) in enumerate(((k, v), (ok, ov))):
                allowed = (ka[2 * half : 2 * half + 1, :] <= query_pos) & (
                    ka[2 * half + 1 : 2 * half + 2, :] == query_doc
                )
                scores = jnp.where(allowed, dot_nt(q[at, :], key[...]) * scale, NEGATIVE)
                probs.append(jnp.exp(scores - lse[0, at, :]))
                prob_grads.append(dot_nt(cot[at, :], value[...]))
            row_dot = sum(jnp.sum(p * g, axis=1, keepdims=True) for p, g in zip(probs, prob_grads))
            query_grad = jnp.zeros((tall, HD), jnp.float32)
            for half, (p, g) in enumerate(zip(probs, prob_grads)):
                score_cot = (p * (g - row_dot)).astype(BF16)
                key = (k, ok)[half]
                query_grad = query_grad + dot_nn(score_cot, key[...])
                key_part = dot_tn(score_cot, q[at, :])
                value_part = dot_tn(p.astype(BF16), cot[at, :])
                if r == 0:
                    key_sum[half] = key_part
                    value_sum[half] = value_part
                else:
                    key_sum[half] += key_part
                    value_sum[half] += value_part
            dq[at, :] = query_grad * scale
        dk[...] = key_sum[0] * scale
        dv[...] = value_sum[0]
        dok[...] = (key_sum[1] * scale).astype(BF16)
        dov[...] = value_sum[1].astype(BF16)

    head = pl.BlockSpec((rows, HD), lambda h: (0, h))
    return pl.pallas_call(
        kernel,
        grid=(heads,),
        out_shape=[shape((rows, cols), jnp.float32)] * 3 + [shape((rows, cols))] * 2,
        in_specs=[head] * 5
        + [pl.BlockSpec(query_at.shape, lambda h: (0, 0)), pl.BlockSpec(key_at.shape, lambda h: (0, 0))]
        + [pl.BlockSpec((1, rows, 1), lambda h: (h, 0, 0)), head],
        out_specs=[head] * 5,
        scratch_shapes=[pltpu.VMEM((2, rows, HD), jnp.float32)] * 2,
        compiler_params=pltpu.CompilerParams(vmem_limit_bytes=40 * 2**20),
        name="attend_back",
    )(queries, keys, values, other_keys, other_values, query_at, key_at, log_totals, out_cot)


def erf(value):
    value = jnp.clip(value, -4.0, 4.0)
    square = value * value
    top = jnp.full_like(value, -2.72614225801306e-10)
    for factor in (
        2.77068142495902e-08,
        -2.10102402082508e-06,
        -5.69250639462346e-05,
        -7.34990630326855e-04,
        -2.95459980854025e-03,
        -1.60960333262415e-02,
    ):
        top = top * square + factor
    bottom = jnp.full_like(value, -1.45660718464996e-05)
    for factor in (-2.13374055278905e-04, -1.68282697438203e-03, -7.37332916720468e-03, -1.42647390514189e-02):
        bottom = bottom * square + factor
    return value * top / bottom


def gelu_both(value):
    share = 0.5 * (1.0 + erf(value * 0.7071067811865476))
    bell = jnp.exp(-0.5 * value * value) * 0.3989422804014327
    return value * share, share + value * bell


def row_mean(value):
    return jnp.mean(value, axis=1, keepdims=True)


def middle(heads, small, large, stream, gains, da_in, da_out, da_bias, out_grad, mix_cot_in):
    rows_all, head_cols = heads.shape
    width, hidden = large.shape[1:]
    step = 16
    half = BLOCK // 2
    tile = 2 * BLOCK
    tiles = width // tile

    def kernel(
        heads, small, large, stream, gains, da_in, da_out, da_bias, out_grad, mix_cot_in,
        block_out, mix_next, residual_grad, heads_cot, gain_grads, side_sum, other, out_proj_grad, up_sum, down_sum,
        w_out, w_up, w_down, mid_all, active, slope, cot_all, up_cot, attn_cot,
        part, got1, got3, own, residual, unit, total, flat, aux, inv, grad_stage, sums,
        y_slots, z_part, z_slots, c_part, c_slot, x_slots, result,
        load, send, recv, gsend, grecv, gkeep, sends, recvs, dload,
    ):
        x, zl, zh, y, c = coords()
        z = zh * 2 + zl
        along_z, along_y = z_peers(x, zl, zh, y, c), y_peers(x, zl, zh, y, c)
        sibling = device(x, zl, zh, y, 1 - c)
        steps = (1, 3, 2)
        places = {k: (x + k) % 4 for k in steps}
        peers = {k: device(places[k], zl, zh, y, c) for k in steps}
        right, left, far = places[1], places[3], places[2]
        loads = [
            pltpu.make_async_copy(small.at[3], w_out, load.at[0]),
            pltpu.make_async_copy(large.at[0], w_up, load.at[1]),
            pltpu.make_async_copy(large.at[1], w_down, load.at[2]),
        ]
        for copy in loads:
            copy.start()
        greet([peers[k] for k in steps] + [peer for _, peer in along_z + along_y] + [sibling])

        def block(place):
            return pl.ds(pl.multiple_of(place * BLOCK, BLOCK), BLOCK)

        def chunks(work, place=0):
            def one(r, carry):
                begin = r * step
                work(
                    pl.ds(pl.multiple_of(begin, step), step),
                    pl.ds(pl.multiple_of(place * BLOCK + begin, step), step),
                )
                return carry

            lax.fori_loop(0, BLOCK // step, one, 0)

        sent = []
        given = ({}, {}, {})

        def arrived(stage, got):
            for k in steps:
                i = stage * 3 + k - 1
                remote(got.at[k - 1], got.at[k - 1], send.at[i], recv.at[i], sibling).wait_recv()

        def push(src, dst, i, peer):
            copy = remote(src, dst, send.at[i], recv.at[i], peer)
            copy.start()
            sent.append(copy)
            return copy

        def give_part(stage, k, got, product):
            if k == 0:
                own[...] = product
                return
            slot = stage % 2
            if stage == 2:
                given[0][k].wait_send()
            part[slot, k - 1] = product.astype(BF16)
            given[stage][k] = push(part.at[slot, k - 1], got.at[k - 1], stage * 3 + k - 1, peers[k])

        def spread(buf, base):
            def piece(place, top):
                begin = pl.multiple_of(place * BLOCK + (0 if top else half), half)
                return buf.at[pl.ds(begin, half)]

            first = [
                push(piece(x, True), piece(x, True), base, peers[1]),
                push(piece(x, False), piece(x, False), base + 2, peers[3]),
                push(piece(x, False), piece(x, False), base + 1, peers[1]),
                push(piece(x, True), piece(x, True), base + 3, peers[3]),
            ]

            def forward():
                first[0].wait_recv()
                one = push(piece(left, True), piece(left, True), base + 4, peers[1])
                first[1].wait_recv()
                two = push(piece(right, False), piece(right, False), base + 5, peers[3])
                return one, two

            return first, forward

        def gathered(buf, base, work):
            first, forward = spread(buf, base)
            work(0, x)
            one, two = forward()
            first[2].wait_recv()
            work(3, left)
            first[3].wait_recv()
            work(1, right)
            one.wait_recv()
            two.wait_recv()
            work(2, far)

        loads[0].wait()
        for k in (2, 1, 3, 0):
            place = x if k == 0 else places[k]
            give_part(0, k, got1, dot_nt(heads[block(place), :], w_out[...]))
        arrived(0, got1)

        def to_mid(at, there):
            value = stream[3, at, :] + own[at, :]
            for k in range(3):
                value = value + got1[k, at, :].astype(jnp.float32)
            residual[at, :] = value
            centered = value - row_mean(value)
            scale = lax.rsqrt(row_mean(centered * centered) + EPSILON)
            inv[at, :BLOCK] = jnp.broadcast_to(scale, (step, BLOCK))
            normed = centered * scale
            unit[at, :] = normed
            mid_all[there, :] = (normed * gains[3:4, :]).astype(BF16)

        chunks(to_mid, x)

        waited = []

        def feed(k, place):
            if not waited:
                loads[1].wait()
            total[...] = dot_nn(mid_all[block(place), :], w_up[...])

            def bend(at, there):
                value, change = gelu_both(total[at, :])
                active[there, :] = value.astype(BF16)
                slope[there, :] = change.astype(slope.dtype)

            chunks(bend, place)
            if not waited:
                loads[2].wait()
                waited.append(True)
            give_part(1, k, got3, dot_nt(active[block(place), :], w_down[...]))

        gathered(mid_all, 9, feed)
        arrived(1, got3)

        def to_out(at, _):
            value = residual[at, :] + own[at, :]
            for k in range(3):
                value = value + got3[k, at, :].astype(jnp.float32)
            block_out[at, :] = value.astype(BF16)
            scale = lax.rsqrt(row_mean(value * value) + EPSILON)
            inv[at, BLOCK:] = jnp.broadcast_to(scale, (step, BLOCK))
            residual[at, :] = value * scale
            flat[at, :] = (value * scale * gains[4:5, :]).astype(BF16)

        chunks(to_out)
        inner_act, inner_slope = gelu_both(dot_nn(flat[...], da_in[...]))
        inner_act = inner_act.astype(BF16)
        mix_next[...] = dot_nn(inner_act, da_out[...]) + da_bias[...]
        mix_cot = mix_cot_in[...].astype(BF16)
        inner_cot = (dot_nt(mix_cot, da_out[...]) * inner_slope).astype(BF16)
        aux[...] = dot_nt(inner_cot, da_in[...])
        sums[...] = jnp.zeros_like(sums)

        def to_cot(at, there):
            rms_unit = residual[at, :]
            grad = aux[at, :]
            product = grad * rms_unit
            sums[0] += product[:8] + product[8:]
            scaled = grad * gains[4:5, :]
            scale = inv[at, BLOCK : BLOCK + 1]
            value = out_grad[at, :].astype(jnp.float32) + scale * (
                scaled - rms_unit * row_mean(scaled * rms_unit)
            )
            residual[at, :] = value
            cot_all[there, :] = value.astype(BF16)

        chunks(to_cot, x)

        def small_grads():
            grad = dot_tn(flat[...], inner_cot)
            c_rows = SIDE_ROWS
            bias = jnp.sum(mix_cot_in[...], axis=0, keepdims=True)
            tail = jnp.concatenate(
                [
                    dot_tn(inner_act, mix_cot)[:104],
                    jnp.where(lax.broadcasted_iota(jnp.int32, (24, BLOCK), 0) == 0, bias, 0.0),
                ],
                axis=0,
            )
            whole = jnp.concatenate([grad, tail], axis=0)
            for py in range(4):
                for pz in range(4):
                    begin = (py * 4 + pz) * c_rows
                    result[py, pz] = whole[begin : begin + c_rows]

        side = {}

        def side_start():
            small_grads()
            side[0] = exchange(lambda py: result.at[py], y_slots, y, along_y, sends, recvs, 0)
            y_slots[y] = result[y]

        def side_z():
            for copy in side[0]:
                copy.wait()
            z_part[...] = y_slots[0] + y_slots[1] + y_slots[2] + y_slots[3]
            side[1] = exchange(lambda pz: z_part.at[pz], z_slots, z, along_z, sends, recvs, 3)
            z_slots[z] = z_part[z]

        def side_core():
            for copy in side[1]:
                copy.wait()
            c_part[...] = z_slots[0] + z_slots[1] + z_slots[2] + z_slots[3]
            side[2] = remote(c_part, c_slot, sends.at[6], recvs.at[6], sibling)
            side[2].start()

        def side_x():
            side[2].wait()
            x_slots[x] = c_part[...] + c_slot[...]
            along_x = [(places[k], peers[k]) for k in steps]
            side[3] = exchange(x_slots.at[x], x_slots, x, along_x, sends, recvs, 7)

        def side_up_z():
            for copy in side[3]:
                copy.wait()
            side_sum[y, z] = x_slots[0] + x_slots[1] + x_slots[2] + x_slots[3]
            side[4] = exchange(side_sum.at[y, z], side_sum.at[y], z, along_z, sends, recvs, 10)

        def side_up_y():
            for copy in side[4]:
                copy.wait()
            side[5] = exchange(side_sum.at[y], side_sum, y, along_y, sends, recvs, 13)

        def feed_back(k, place):
            total[...] = dot_nn(cot_all[block(place), :], w_down[...])

            def bend(at, there):
                up_cot[there, :] = (total[at, :] * slope[there, :].astype(jnp.float32)).astype(BF16)

            chunks(bend, place)
            give_part(2, k, got1, dot_nt(up_cot[block(place), :], w_up[...]))

        first, forward = spread(cot_all, 15)
        side_start()
        feed_back(0, x)
        one, two = forward()
        first[2].wait_recv()
        feed_back(3, left)
        first[3].wait_recv()
        feed_back(1, right)
        side_z()
        one.wait_recv()
        two.wait_recv()
        feed_back(2, far)
        side_core()

        def weight_grad(which, left_side, right_side):
            def copies(m):
                slot = lax.rem(m, 2)
                mine = grad_stage.at[slot, pl.ds(pl.multiple_of(c * BLOCK, BLOCK), BLOCK)]
                theirs = grad_stage.at[slot, pl.ds(pl.multiple_of((1 - c) * BLOCK, BLOCK), BLOCK)]
                i = which * tiles + m
                stays = (w_up, w_down)[which].at[pl.ds(pl.multiple_of(m * BLOCK, BLOCK), BLOCK)]
                return (
                    pltpu.make_async_copy(mine, stays, gkeep.at[slot]),
                    remote(theirs, other.at[which, m], gsend.at[i], grecv.at[i], sibling),
                )

            def finish(m):
                stay, go = copies(m)
                stay.wait()
                go.wait_send()

            def one(m, carry):
                @pl.when(m >= 2)
                def _():
                    finish(m - 2)

                cols = pl.ds(pl.multiple_of(m * tile, tile), tile)
                grad_stage[lax.rem(m, 2)] = dot_tn(left_side[:, cols], right_side[...]).astype(BF16)
                for copy in copies(m):
                    copy.start()
                return carry

            lax.fori_loop(0, tiles, one, 0)
            finish(tiles - 2)
            finish(tiles - 1)

        def other_came(which):
            def one(m, carry):
                i = which * tiles + m
                remote(other.at[which, m], other.at[which, m], gsend.at[i], grecv.at[i], sibling).wait_recv()
                return carry

            return one

        def fetch_other(which):
            lax.fori_loop(0, tiles, other_came(which), 0)
            for m in range(tiles):
                fetch(which, m).start()

        def fetch(which, m):
            there = (w_up, w_down)[which].at[pl.ds((tiles + m) * BLOCK, BLOCK)]
            return pltpu.make_async_copy(other.at[which, m], there, dload.at[which * tiles + m])

        def add_cores(which):
            whole = (w_up, w_down)[which]
            for m in range(tiles):
                fetch(which, m).wait()

            def one(r, carry):
                at = pl.ds(pl.multiple_of(r * step, step), step)
                there = pl.ds(pl.multiple_of(tiles * BLOCK + r * step, step), step)
                whole[at, :] = (whole[at, :].astype(jnp.float32) + whole[there, :].astype(jnp.float32)).astype(BF16)
                return carry

            lax.fori_loop(0, tiles * BLOCK // step, one, 0)
            done = pltpu.make_async_copy(
                whole.at[pl.ds(0, tiles * BLOCK)], (up_sum, down_sum)[which], gkeep.at[2 + which]
            )
            done.start()
            return done

        weight_grad(1, cot_all, active)
        side_x()
        arrived(2, got1)

        def to_residual(at, there):
            grad = own[at, :]
            for k in range(3):
                grad = grad + got1[k, at, :].astype(jnp.float32)
            mid_unit = unit[at, :]
            product = grad * mid_unit
            sums[1] += product[:8] + product[8:]
            scaled = grad * gains[3:4, :]
            scale = inv[at, 0:1]
            value = residual[at, :] + scale * (
                scaled - row_mean(scaled) - mid_unit * row_mean(scaled * mid_unit)
            )
            residual_grad[at, :] = value
            attn_cot[there, :] = value.astype(BF16)

        chunks(to_residual, x)
        first, forward = spread(attn_cot, 21)

        def head_back(place):
            heads_cot[block(place), :] = dot_nn(attn_cot[block(place), :], w_out[...]).astype(BF16)

        side_up_z()
        head_back(x)
        one, two = forward()
        fetch_other(1)
        weight_grad(0, mid_all, up_cot)
        side_up_y()
        down_done = add_cores(1)
        fetch_other(0)
        gain_grads[...] = jnp.sum(sums[...], axis=1)
        first[2].wait_recv()
        head_back(left)
        first[3].wait_recv()
        head_back(right)
        one.wait_recv()
        two.wait_recv()
        head_back(far)

        def out_grad_copy(m):
            rows = pl.ds(pl.multiple_of(m * tile, tile), tile)
            slot = lax.rem(m, 2)
            return pltpu.make_async_copy(
                grad_stage.at[slot, :, pl.ds(0, head_cols)], out_proj_grad.at[rows], gkeep.at[slot]
            )

        def out_grad_tile(m, carry):
            @pl.when(m >= 2)
            def _():
                out_grad_copy(m - 2).wait()

            cols = pl.ds(pl.multiple_of(m * tile, tile), tile)
            grad_stage[lax.rem(m, 2), :, :head_cols] = dot_tn(attn_cot[:, cols], heads[...]).astype(BF16)
            out_grad_copy(m).start()
            return carry

        lax.fori_loop(0, tiles, out_grad_tile, 0)
        out_grad_copy(tiles - 2).wait()
        out_grad_copy(tiles - 1).wait()
        for copy in side[5]:
            copy.wait()
        up_done = add_cores(0)
        down_done.wait()
        up_done.wait()
        for i, copy in enumerate(sent):
            if all(copy is not first for first in given[0].values()):
                copy.wait_send()

    f32 = jnp.float32
    vmem = pltpu.VMEM
    piece = (SIDE_ROWS, 128)
    return pl.pallas_call(
        kernel,
        out_shape=[
            shape((BLOCK, width)),
            shape((BLOCK, BLOCK), f32),
            shape((BLOCK, width), f32),
            shape(heads.shape),
            shape((2, width), f32),
            shape((4, 4) + piece, f32),
            shape((2, tiles, BLOCK, hidden)),
            shape((width, head_cols)),
            shape((tiles * BLOCK, hidden)),
            shape((tiles * BLOCK, hidden)),
        ],
        in_specs=[VMEM, ANY, ANY] + [VMEM] * 7,
        out_specs=[VMEM] * 6 + [ANY] * 4,
        scratch_shapes=[
            vmem((width, head_cols), BF16),
            vmem((width, hidden), BF16),
            vmem((width, hidden), BF16),
            vmem((rows_all, width), BF16),
            vmem((rows_all, hidden), BF16),
            vmem((rows_all, hidden), f32),
            vmem((rows_all, width), BF16),
            vmem((rows_all, hidden), BF16),
            vmem((rows_all, width), BF16),
            vmem((2, 3, BLOCK, width), BF16),
            vmem((3, BLOCK, width), BF16),
            vmem((3, BLOCK, width), BF16),
            vmem((BLOCK, width), f32),
            vmem((BLOCK, width), f32),
            vmem((BLOCK, width), f32),
            vmem((BLOCK, width), f32),
            vmem((BLOCK, width), BF16),
            vmem((BLOCK, width), f32),
            vmem((BLOCK, 2 * BLOCK), f32),
            vmem((2, tile, hidden), BF16),
            vmem((2, 8, width), f32),
            vmem((4, 4) + piece, f32),
            vmem((4,) + piece, f32),
            vmem((4,) + piece, f32),
            vmem(piece, f32),
            vmem(piece, f32),
            vmem((4,) + piece, f32),
            vmem((4, 4) + piece, f32),
            pltpu.SemaphoreType.DMA((3,)),
            pltpu.SemaphoreType.DMA((27,)),
            pltpu.SemaphoreType.DMA((27,)),
            pltpu.SemaphoreType.DMA((2 * tiles,)),
            pltpu.SemaphoreType.DMA((2 * tiles,)),
            pltpu.SemaphoreType.DMA((4,)),
            pltpu.SemaphoreType.DMA((16,)),
            pltpu.SemaphoreType.DMA((16,)),
            pltpu.SemaphoreType.DMA((2 * tiles,)),
        ],
        compiler_params=pltpu.CompilerParams(
            collective_id=4, has_side_effects=True, vmem_limit_bytes=62 * 2**20
        ),
        name="middle",
    )(heads, small, large, stream, gains, da_in, da_out, da_bias, out_grad, mix_cot_in)


def inward(grads, gives, small, normed, out_proj_grad, streams, residual_grad, gains, late_gains, tables, down):
    rows_all, cols = grads[0].shape
    width = streams.shape[2]
    step = 16
    half = BLOCK // 2
    tile = 2 * BLOCK
    tiles = width // tile
    hidden = down.shape[3]

    def kernel(
        dq, dk, dv, give_k, give_v, small, normed, out_proj_grad, streams, residual_grad, gains, late, tables,
        down,
        stream_cot, gain_grads, small_sum, down_sum,
        weights, inputs, cots, got_k, got_v, far_part, near, hop, got, own, grad, swapped, sums, down_y,
        load, send, recv, ssend, srecv, gsend, grecv, local,
    ):
        x, zl, zh, y, c = coords()
        z = zh * 2 + zl
        along_y = y_peers(x, zl, zh, y, c)
        partner = device(x, 1 - zl, zh, y, c)
        sibling = device(x, zl, zh, y, 1 - c)
        places = {k: (x + k) % 4 for k in (1, 2, 3)}
        peers = {k: device(places[k], zl, zh, y, c) for k in (1, 3)}
        loads = [pltpu.make_async_copy(small.at[i], weights.at[i], load.at[i]) for i in range(3)]
        loads += [pltpu.make_async_copy(normed.at[i], inputs.at[i], load.at[3 + i]) for i in range(3)]
        loads.append(pltpu.make_async_copy(out_proj_grad, grad.at[3], load.at[6]))
        for copy in loads:
            copy.start()
        greet([peers[1], peers[3], partner, sibling] + [peer for _, peer in along_y])
        sides = []

        def side(src, dst, peer):
            i = len(sides)
            sides.append(remote(src, dst, ssend.at[i], srecv.at[i], peer))
            sides[-1].start()

        side(give_k, got_k, partner)
        side(give_v, got_v, partner)
        for py, peer in along_y:
            side(down.at[:, py], down_y.at[y], peer)
        locals_ = [pltpu.make_async_copy(down.at[:, y], down_y.at[y], local.at[0])]
        for copy in locals_:
            copy.start()

        def block(place):
            return pl.ds(pl.multiple_of(place * BLOCK, BLOCK), BLOCK)

        def turn_back(value):
            def one(at):
                part = value(at)
                ahead, behind = pltpu.roll(part, HD - ROT // 2, 1), pltpu.roll(part, ROT // 2, 1)
                return part * tables[0, at, :] - ahead * tables[1, at, :] - behind * tables[2, at, :]

            return one

        def to_cots(i, value):
            def one(r, carry):
                at = pl.ds(pl.multiple_of(r * step, step), step)
                for h in range(cols // HD):
                    head = slice(h * HD, (h + 1) * HD)
                    cots[i, at, head] = value(at, head).astype(BF16)
                return carry

            lax.fori_loop(0, rows_all // step, one, 0)

        def turned(value):
            return lambda at, head: turn_back(lambda at: value(at, head))(at)

        started = []

        def push(src, dst, i, peer):
            started.append(remote(src, dst, send.at[i], recv.at[i], peer))
            started[-1].start()

        def far_sums(i):
            if i == 0:
                loads[0].wait()
            else:
                loads[i].wait()
            far_part[i] = dot_nt(cots[i, block(places[2]), :], weights[i]).astype(BF16)
            push(far_part.at[i, pl.ds(0, half)], hop.at[i, 0], i * 4, peers[1])
            push(far_part.at[i, pl.ds(half, half)], hop.at[i, 1], i * 4 + 1, peers[3])

        def near_sums(i):
            for k, side_of in ((1, 0), (3, 1)):
                product = dot_nt(cots[i, block(places[k]), :], weights[i])
                begin = side_of * half
                j = i * 4 + side_of
                remote(hop.at[i, side_of], hop.at[i, side_of], send.at[j], recv.at[j], sibling).wait_recv()
                near[i, side_of] = product.astype(BF16)
                merged = product[begin : begin + half] + hop[i, side_of].astype(jnp.float32)
                near[i, side_of, begin : begin + half] = merged.astype(BF16)
                push(near.at[i, side_of], got.at[i, side_of], i * 4 + 2 + side_of, peers[k])

        def own_sums(i):
            own[i] = dot_nt(cots[i, block(x), :], weights[i])

        swaps = []

        def weight_grad(i):
            if i < 3:
                loads[3 + i].wait()

                def one(m, carry):
                    at = pl.ds(pl.multiple_of(m * tile, tile), tile)
                    grad[i, at, :] = dot_tn(inputs[i, :, at], cots[i]).astype(BF16)
                    return carry

                lax.fori_loop(0, tiles, one, 0)
            else:
                loads[6].wait()
            for m in range(tiles):
                begin = pl.multiple_of(m * tile + (1 - c) * BLOCK, BLOCK)
                j = i * tiles + m
                swaps.append(
                    remote(grad.at[i, pl.ds(begin, BLOCK)], swapped.at[i, m], gsend.at[j], grecv.at[j], sibling)
                )
                swaps[-1].start()

        def add_cores(i):
            for m in range(tiles):
                swaps_of[i][m].wait()

            def one(r, carry):
                m, part = r // (BLOCK // step), lax.rem(r, BLOCK // step)
                at = pl.ds(pl.multiple_of(m * tile + c * BLOCK + part * step, step), step)
                there = pl.ds(pl.multiple_of(part * step, step), step)
                value = grad[i, at, :].astype(jnp.float32) + swapped[i, m, there, :].astype(jnp.float32)
                swapped[i, m, there, :] = value.astype(BF16)
                return carry

            lax.fori_loop(0, tiles * BLOCK // step, one, 0)
            locals_.append(pltpu.make_async_copy(swapped.at[i], small_sum.at[:, i], local.at[1 + i]))
            locals_[-1].start()

        swaps_of = {}

        def grads_of(i):
            begin = len(swaps)
            weight_grad(i)
            swaps_of[i] = swaps[begin:]

        to_cots(0, turned(lambda at, head: dq[at, head]))
        far_sums(0)
        near_sums(0)
        grads_of(3)
        grads_of(0)
        own_sums(0)
        sides[0].wait_recv()
        to_cots(1, turned(lambda at, head: dk[at, head] + got_k[at, head].astype(jnp.float32)))
        far_sums(1)
        sides[1].wait_recv()
        to_cots(2, lambda at, head: dv[at, head] + got_v[at, head].astype(jnp.float32))
        far_sums(2)
        near_sums(1)
        near_sums(2)
        grads_of(1)
        grads_of(2)
        own_sums(1)
        own_sums(2)
        for i in (3, 0, 1, 2):
            add_cores(i)
        sums[...] = jnp.zeros_like(sums)
        for i in range(3):
            for side_of in range(2):
                j = i * 4 + 2 + side_of
                remote(got.at[i, side_of], got.at[i, side_of], send.at[j], recv.at[j], sibling).wait_recv()

            def back(r, carry, i=i):
                at = pl.ds(pl.multiple_of(r * step, step), step)
                value = streams[i, at, :]
                centered = value - row_mean(value)
                scale = lax.rsqrt(row_mean(centered * centered) + EPSILON)
                unit = centered * scale
                above = own[i, at, :] + got[i, 0, at, :].astype(jnp.float32) + got[i, 1, at, :].astype(jnp.float32)
                product = above * unit
                sums[i] += product[:8] + product[8:]
                scaled = above * gains[i : i + 1, :]
                result = scale * (scaled - row_mean(scaled) - unit * row_mean(scaled * unit))
                stream_cot[i, at, :] = result.astype(BF16)
                return carry

            lax.fori_loop(0, BLOCK // step, back, 0)
        stream_cot[3] = residual_grad[...].astype(BF16)
        gain_grads[...] = jnp.zeros_like(gain_grads)
        for i in range(3):
            gain_grads[i : i + 1, :] = jnp.sum(sums[i], axis=0, keepdims=True)
        gain_grads[3:4, :] = late[1:2, :]
        gain_grads[4:5, :] = late[0:1, :]
        for copy in sides[2:] + locals_[:1]:
            copy.wait()
        for high in range(2):

            def add_y(r, carry, high=high):
                at = pl.ds(pl.multiple_of(r * step, step), step)
                value = down_y[0, high, at, :].astype(jnp.float32)
                for src in range(1, 4):
                    value = value + down_y[src, high, at, :].astype(jnp.float32)
                down_sum[high, at, :] = value.astype(BF16)
                return carry

            lax.fori_loop(0, BLOCK // step, add_y, 0)
        for copy in started + sides[:2]:
            copy.wait_send()
        for copy in locals_[1:]:
            copy.wait()

    f32 = jnp.float32
    vmem = pltpu.VMEM
    sem = pltpu.SemaphoreType.DMA
    return pl.pallas_call(
        kernel,
        out_shape=[
            shape((4, BLOCK, width)),
            shape((8, width), f32),
            shape((tiles, 4, BLOCK, cols)),
            shape((2, BLOCK, hidden)),
        ],
        in_specs=[VMEM] * 5 + [ANY] * 3 + [VMEM] * 5 + [ANY],
        out_specs=[VMEM, VMEM, ANY, VMEM],
        scratch_shapes=[
            vmem((3, width, cols), BF16),
            vmem((3, rows_all, width), BF16),
            vmem((3, rows_all, cols), BF16),
            vmem((rows_all, cols), BF16),
            vmem((rows_all, cols), BF16),
            vmem((3, BLOCK, width), BF16),
            vmem((3, 2, BLOCK, width), BF16),
            vmem((3, 2, half, width), BF16),
            vmem((3, 2, BLOCK, width), BF16),
            vmem((3, BLOCK, width), f32),
            vmem((4, width, cols), BF16),
            vmem((4, tiles, BLOCK, cols), BF16),
            vmem((3, 8, width), f32),
            vmem((4, 2, BLOCK, hidden), BF16),
            sem((7,)),
            sem((12,)),
            sem((12,)),
            sem((8,)),
            sem((8,)),
            sem((4 * tiles,)),
            sem((4 * tiles,)),
            sem((5,)),
        ],
        compiler_params=pltpu.CompilerParams(
            collective_id=5, has_side_effects=True, vmem_limit_bytes=60 * 2**20
        ),
        name="inward",
    )(
        *grads, *gives, small, normed, out_proj_grad, streams, residual_grad, gains, late_gains, tables, down
    )


def hand_out(own_hist, weights, stream_cot, gains, small, up, down):
    groups, n, rows, width = own_hist.shape
    cols = small.shape[3]
    thin = cols // 2
    hidden = up.shape[2] // 2
    step = 16
    lanes = 128

    def kernel(
        hist, w, cot, gains, small, up, down,
        out, omg, gains_out, small_out, up_out, down_out,
        held, stage, mixes, turned, x_slots, z_slots, y_slots, c_part, c_slot,
        small_y, small_part, small_z, up_y, up_part, up_z, down_z,
        load, send, recv, msend, mrecv, local, sends, recvs, ssend, srecv,
    ):
        x, zl, zh, y, c = coords()
        z = zh * 2 + zl
        place = x * 2 + zl
        others = hist_peers(x, zl)
        peers = [device(px, pz, zh, y, c) for px, pz in others]
        holders = [px * 2 + pz for px, pz in others] + [place]
        loads = []
        for k, holder in enumerate(holders):
            for j in range(n):
                i = k * n + j
                loads.append(pltpu.make_async_copy(hist.at[holder, j], held.at[k, j], load.at[i]))
        for j in range(n):
            for copy in loads[j::n]:
                copy.start()
        along_x, along_z = x_peers(x, zl, zh, y, c), z_peers(x, zl, zh, y, c)
        along_y = y_peers(x, zl, zh, y, c)
        sibling = device(x, zl, zh, y, 1 - c)
        others_z = [device(x, 1 - zl, 1 - zh, y, c), device(x, zl, 1 - zh, y, c)]
        greet(peers + others_z + [peer for _, peer in along_y] + [sibling])
        sides = []

        def side(src, dst, peer):
            i = len(sides)
            sides.append(remote(src, dst, ssend.at[i], srecv.at[i], peer))
            sides[-1].start()

        first = exchange(gains, x_slots, x, along_x, sends, recvs, 0)
        x_slots[x] = gains[...]
        for py, peer in along_y:
            for high in range(2):
                side(small.at[high * 4 + py], small_y.at[y, high], peer)
        for py, peer in along_y:
            for high in range(2):
                side(up.at[high * 4 + py], up_y.at[y, high], peer)
        for pz, peer in along_z:
            high, low = pz // 2, pz % 2
            side(down.at[high, :, pl.ds(pl.multiple_of(low * hidden, hidden), hidden)], down_z.at[z], peer)
        own_rows = pl.ds(pl.multiple_of(place * rows, rows), rows)
        locals_ = [
            pltpu.make_async_copy(small.at[y], small_y.at[y, 0], local.at[0]),
            pltpu.make_async_copy(small.at[4 + y], small_y.at[y, 1], local.at[1]),
            pltpu.make_async_copy(
                down.at[zh, :, pl.ds(pl.multiple_of(zl * hidden, hidden), hidden)], down_z.at[z], local.at[2]
            ),
            pltpu.make_async_copy(up.at[y], up_y.at[y, 0], local.at[3]),
            pltpu.make_async_copy(up.at[4 + y], up_y.at[y, 1], local.at[4]),
        ]
        for copy in locals_:
            copy.start()
        copies = []
        lane = lax.broadcasted_iota(jnp.int32, (step, lanes), 1)

        def entry_grads(k, j):
            holder = holders[k]
            loads[k * n + j].wait()

            def some_rows(r, carry):
                at = pl.ds(pl.multiple_of(r * step, step), step)
                factors = w[holder, j, at, :]
                factors = [jnp.broadcast_to(factors[:, s : s + 1], (step, lanes)) for s in range(4)]
                totals = [jnp.zeros((step, lanes), jnp.float32) for _ in range(4)]
                for block in range(width // lanes):
                    part = pl.ds(block * lanes, lanes)
                    entry = held[k, j, at, part].astype(jnp.float32)
                    mixed = jnp.zeros((step, lanes), jnp.float32)
                    for s in range(4):
                        piece = cot[s, at, part].astype(jnp.float32)
                        mixed = mixed + factors[s] * piece
                        totals[s] = totals[s] + entry * piece
                    stage[k, j, at, part] = mixed.astype(BF16)
                packed = jnp.zeros((step, lanes), jnp.float32)
                for s in range(4):
                    packed = jnp.where(lane == s, jnp.sum(totals[s], axis=1, keepdims=True), packed)
                mixes[at, :] = packed
                return carry

            lax.fori_loop(0, rows // step, some_rows, 0)
            turned[k, j] = jnp.transpose(mixes[...])[:8]
            if k < 7:
                i = k * n + j
                copies.append(remote(stage.at[k, j], out.at[j, own_rows], send.at[i], recv.at[i], peers[k]))
                copies[-1].start()
                if j == n - 1:
                    copies.append(remote(turned.at[k], omg.at[place], msend.at[k], mrecv.at[k], peers[k]))
                    copies[-1].start()

        for k in range(7):
            entry_grads(k, 0)
        for copy in first:
            copy.wait()
        z_slots[z] = x_slots[0] + x_slots[1] + x_slots[2] + x_slots[3]
        second = exchange(z_slots.at[z], z_slots, z, along_z, sends, recvs, 3)
        for j in range(1, n):
            for k in range(7):
                entry_grads(k, j)
        for j in range(n):
            entry_grads(7, j)
            locals_.append(pltpu.make_async_copy(stage.at[7, j], out.at[j, own_rows], local.at[5 + j]))
            locals_[-1].start()
        locals_.append(pltpu.make_async_copy(turned.at[7], omg.at[place], local.at[5 + n]))
        locals_[-1].start()
        for copy in second:
            copy.wait()
        y_slots[y] = z_slots[0] + z_slots[1] + z_slots[2] + z_slots[3]
        third = exchange(y_slots.at[y], y_slots, y, along_y, sends, recvs, 6)
        for copy in third:
            copy.wait()
        c_part[...] = y_slots[0] + y_slots[1] + y_slots[2] + y_slots[3]
        fourth = remote(c_part, c_slot, sends.at[9], recvs.at[9], sibling)
        fourth.start()
        fourth.wait()
        gains_out[...] = c_part[...] + c_slot[...]

        def add_four(parts, places, dst):
            def one(r, carry):
                at = pl.ds(pl.multiple_of(r * step, step), step)
                value = parts[(0,) + places + (at,)].astype(jnp.float32)
                for src in range(1, 4):
                    value = value + parts[(src,) + places + (at,)].astype(jnp.float32)
                dst[places + (at,)] = value.astype(dst.dtype)
                return carry

            lax.fori_loop(0, rows // step, one, 0)

        def to_z(parts, slots, wide, first_sem):
            cut = [slice(None)] * (len(parts.shape) - 2)

            def piece(high, low):
                return parts.at[tuple([high] + cut + [pl.ds(pl.multiple_of(low * wide, wide), wide)])]

            out_copies = []
            for k, (pz, peer) in enumerate(along_z):
                i = first_sem + k
                out_copies.append(remote(piece(pz // 2, pz % 2), slots.at[z], ssend.at[i], srecv.at[i], peer))
            out_copies.append(pltpu.make_async_copy(piece(zh, zl), slots.at[z], local.at[6 + n + first_sem // 18]))
            for copy in out_copies:
                copy.start()
            return out_copies

        for copy in sides[:6] + locals_[:2]:
            copy.wait()
        for high in range(2):
            for i in range(4):
                add_four(small_y, (high, i), small_part)
        small_last = to_z(small_part, small_z, thin, 15)
        for copy in sides[6:12] + locals_[3:5]:
            copy.wait()
        for high in range(2):
            add_four(up_y, (high,), up_part)
        up_last = to_z(up_part, up_z, hidden, 18)
        for copy in sides[12:] + locals_[2:3]:
            copy.wait()
        add_four(down_z, (), down_out)
        for copy in small_last:
            copy.wait()
        for i in range(4):
            add_four(small_z, (i,), small_out)
        for copy in up_last:
            copy.wait()
        add_four(up_z, (), up_out)
        for copy in copies + locals_[5:]:
            copy.wait()

    f32 = jnp.float32
    vmem = pltpu.VMEM
    sem = pltpu.SemaphoreType.DMA
    return pl.pallas_call(
        kernel,
        out_shape=[
            shape((n, groups * rows, width)),
            shape((groups, n, 8, lanes), f32),
            shape(gains.shape, f32),
            shape((4, BLOCK, thin), f32),
            shape((BLOCK, hidden), f32),
            shape((BLOCK, hidden), f32),
        ],
        in_specs=[ANY, VMEM, VMEM, VMEM, ANY, ANY, ANY],
        out_specs=[ANY, ANY, VMEM, VMEM, VMEM, VMEM],
        scratch_shapes=[
            vmem((groups, n, rows, width), BF16),
            vmem((groups, n, rows, width), BF16),
            vmem((rows, lanes), f32),
            vmem((groups, n, 8, lanes), f32),
            vmem((4,) + gains.shape, f32),
            vmem((4,) + gains.shape, f32),
            vmem((4,) + gains.shape, f32),
            vmem(gains.shape, f32),
            vmem(gains.shape, f32),
            vmem((4, 2, 4, BLOCK, cols), BF16),
            vmem((2, 4, BLOCK, cols), BF16),
            vmem((4, 4, BLOCK, thin), BF16),
            vmem((4, 2, BLOCK, 2 * hidden), BF16),
            vmem((2, BLOCK, 2 * hidden), BF16),
            vmem((4, BLOCK, hidden), BF16),
            vmem((4, BLOCK, hidden), BF16),
            sem((groups * n,)),
            sem((7 * n,)),
            sem((7 * n,)),
            sem((7,)),
            sem((7,)),
            sem((n + 8,)),
            sem((10,)),
            sem((10,)),
            sem((21,)),
            sem((21,)),
        ],
        compiler_params=pltpu.CompilerParams(
            collective_id=6, has_side_effects=True, vmem_limit_bytes=56 * 2**20
        ),
        name="hand_out",
    )(own_hist, weights, stream_cot, gains, small, up, down)


def body(
    history,
    layer_ids,
    mix_weights,
    doc_ids,
    gains,
    w_qkv,
    w_out,
    w_up,
    w_down,
    da_in,
    da_out,
    da_bias,
    out_grad,
    mix_grad_in,
):
    place = lax.axis_index("hist")
    low_z = place % 2
    slots, seq_len, width = history.shape
    small = jnp.concatenate([jnp.transpose(w_qkv, (1, 0, 2)), w_out[None]], axis=0)
    large = jnp.stack([w_up, w_down], axis=0)
    own_hist, full_small, full_large = collect(history, small, large)
    w_q, w_k, w_v, full_out = (full_small[i] for i in range(4))
    full_up, full_down = full_large[0], full_large[1]
    flat_hist = own_hist.reshape(8 * slots, BLOCK, width)

    own_mix = lax.dynamic_slice_in_dim(mix_weights, place * BLOCK, BLOCK, 2)
    pick = (layer_ids[:, None] == jnp.arange(own_mix.shape[1], dtype=jnp.int32)[None, :]).astype(jnp.float32)
    slot_weights = jnp.einsum("jl,slt->sjt", pick, own_mix, precision=HIGHEST)
    owned = jnp.zeros((4, BLOCK, width), jnp.float32)
    for j in range(8 * slots):
        owned = owned + slot_weights[:, j, :, None] * flat_hist[j][None].astype(jnp.float32)

    norm_unit, inv_std = norm_rows(owned[:3])
    normed = (norm_unit * gains[:3, None, :]).astype(BF16)
    gathered = gather_x(normed, 2, "gather_normed").reshape(3, 4 * BLOCK, width)
    rows_here = 4 * BLOCK
    heads_cols = full_out.shape[1]
    cosine, sine_table = rotary_tables(seq_len, ROT)

    def here(table, side=low_z):
        return lax.dynamic_index_in_dim(table.reshape(4, 2, BLOCK, -1), side, 1, False).reshape(rows_here, -1)

    cos_here, sin_here = here(cosine), here(sine_table)
    nothing = jnp.zeros_like(sin_here)
    rest = jnp.zeros((rows_here, HD - ROT), jnp.float32)
    tables = [
        jnp.tile(jnp.concatenate(parts, axis=1), (1, heads_cols // HD))
        for parts in ((cos_here, cos_here, rest + 1.0), (-sin_here, nothing, rest), (nothing, sin_here, rest))
    ]

    def turn(values, direction):
        ahead, behind = jnp.roll(values, -ROT // 2, axis=1), jnp.roll(values, ROT // 2, axis=1)
        return values * tables[0] + direction * (ahead * tables[1] + behind * tables[2])

    def project(which, weight):
        return jnp.dot(gathered[which], weight, preferred_element_type=jnp.float32)

    keys = turn(project(1, w_k), 1.0).astype(BF16)
    values = project(2, w_v).astype(BF16)
    other_keys, other_values = send_hist(keys, 0, 1), send_hist(values, 0, 1)
    queries = turn(project(0, w_q), 1.0).astype(BF16)
    places = jnp.stack([jnp.arange(seq_len, dtype=jnp.int32), doc_ids], axis=1)
    query_at, other_at = here(places), here(places, 1 - low_z)
    key_at = jnp.concatenate([query_at.T, other_at.T], axis=0)
    attention = (queries, keys, values, other_keys, other_values, query_at, key_at)
    heads_flat, log_totals = attend(*attention)

    mixers = da_out.shape[0]
    spare = BLOCK - mixers
    (
        block_out,
        mix_next,
        residual_grad,
        heads_cot,
        late_gains,
        side,
        _,
        out_proj_grad,
        up_sum,
        down_sum,
    ) = middle(
        heads_flat,
        full_small,
        full_large,
        owned,
        gains,
        jnp.pad(da_in, ((0, 0), (0, spare))),
        jnp.pad(da_out, ((0, spare), (0, spare))),
        jnp.pad(da_bias, (0, spare))[None],
        out_grad,
        jnp.pad(mix_grad_in, ((0, 0), (0, spare))),
    )
    side = side.reshape(16 * SIDE_ROWS, BLOCK)[:, :mixers]
    da_in_sum, da_out_sum, bias_sum = side[:width], side[width : width + mixers], side[width + 104]

    *grads, key_give, value_give = attend_back(*attention, log_totals, heads_cot)
    stream_cot, gains_local, small_sum, down_sum = inward(
        grads,
        (key_give, value_give),
        full_small,
        gathered,
        out_proj_grad,
        owned,
        residual_grad,
        gains,
        late_gains,
        jnp.stack([table[:, :HD] for table in tables]),
        down_sum.reshape(2, 4, BLOCK, -1),
    )
    columns = jnp.transpose(slot_weights.reshape(4, 8, slots, BLOCK), (1, 2, 3, 0))
    history_grad, mix_out, gains_sum, small_sum, up_sum, down_sum = hand_out(
        own_hist, columns, stream_cot, gains_local, small_sum, up_sum.reshape(8, BLOCK, -1), down_sum
    )
    mix_grad = jnp.transpose(mix_out[:, :, :4], (2, 1, 0, 3)).reshape(4, slots, seq_len)
    return (
        block_out,
        mix_next[:, :mixers],
        history_grad,
        mix_grad,
        gains_sum[: gains.shape[0]],
        jnp.transpose(small_sum[:3], (1, 0, 2)),
        small_sum[3],
        up_sum,
        down_sum,
        da_in_sum,
        da_out_sum,
        bias_sum,
    )


def solution(mesh):
    return jax.shard_map(
        body,
        mesh=mesh,
        in_specs=(
            P("hist", "tok", None),
            P(),
            P(None, None, "tok"),
            P("tok"),
            P(),
            P("tok", None, "hist"),
            P("tok", "hist"),
            P("tok", "hist"),
            P("tok", "hist"),
            P(),
            P(),
            P(),
            P(("tok", "hist"), None),
            P(("tok", "hist"), None),
        ),
        out_specs=(
            P(("tok", "hist"), None),
            P(("tok", "hist"), None),
            P("hist", "tok", None),
            P(None, "hist", "tok"),
            P(),
            P("tok", None, "hist"),
            P("tok", "hist"),
            P("tok", "hist"),
            P("tok", "hist"),
            P(),
            P(),
            P(),
        ),
        check_vma=False,
    )
```

```python
import jax
import jax.numpy as jnp
from jax import lax
from jax.experimental import pallas as pl
from jax.experimental.pallas import tpu as pltpu
from jax.sharding import PartitionSpec as P

HD = 128
ROT = 32


EPSILON = 1e-05
NEGATIVE = -1e30
HIGHEST = lax.Precision.HIGHEST


def norm_rows(values):
    row_mean = jnp.mean(values, axis=-1, keepdims=True)
    centered = values - row_mean
    inv_std = lax.rsqrt(jnp.mean(centered * centered, axis=-1, keepdims=True) + EPSILON)
    return (centered * inv_std, inv_std)


def norm_back(grad_unit, norm_unit, inv_std):
    return inv_std * (
        grad_unit
        - jnp.mean(grad_unit, axis=-1, keepdims=True)
        - norm_unit * jnp.mean(grad_unit * norm_unit, axis=-1, keepdims=True)
    )


def gelu_slope(values):
    return (
        0.5 * (1.0 + lax.erf(values * 0.7071067811865476))
        + values * jnp.exp(-0.5 * values * values) * 0.3989422804014327
    )


def rotary_tables(length, rotated):
    half_rot = rotated // 2
    frequency = 10000.0 ** (-2.0 * jnp.arange(half_rot, dtype=jnp.float32) / rotated)
    angles = jnp.arange(length, dtype=jnp.float32)[:, None] * frequency[None, :]
    return (jnp.cos(angles), jnp.sin(angles))


def rotate(values, cosine, sine_table, direction):
    half_rot = cosine.shape[1]
    first_half = values[..., :half_rot]
    second_half = values[..., half_rot : 2 * half_rot]
    cos_part = cosine[:, None, :]
    sin_part = direction * sine_table[:, None, :]
    return jnp.concatenate(
        [
            first_half * cos_part - second_half * sin_part,
            second_half * cos_part + first_half * sin_part,
            values[..., 2 * half_rot :],
        ],
        axis=-1,
    )


def contract(left_side, right_side, left_dim, right_dim):
    return lax.dot_general(
        left_side,
        right_side,
        (((left_dim,), (right_dim,)), ((), ())),
        preferred_element_type=jnp.float32,
    )


MESH = pl.DeviceIdType.MESH
ANY = pl.BlockSpec(memory_space=pl.ANY)
BF16 = jnp.bfloat16
BLOCK = 128


def coords():
    hist = lax.axis_index("hist")
    tok = lax.axis_index("tok")
    return hist // 2, hist % 2, tok // 8, (tok // 2) % 4, tok % 2


def device(x, zl, zh, y, c):
    return (x * 2 + zl, zh * 8 + y * 2 + c)


def greet(peers):
    barrier = pltpu.get_barrier_semaphore()
    for peer in peers:
        pl.semaphore_signal(barrier, inc=1, device_id=peer, device_id_type=MESH)
    pl.semaphore_wait(barrier, len(peers))


def remote(src, dst, send_sem, recv_sem, peer):
    return pltpu.make_async_remote_copy(
        src_ref=src,
        dst_ref=dst,
        send_sem=send_sem,
        recv_sem=recv_sem,
        device_id=peer,
        device_id_type=MESH,
    )


def comm_call(kernel, out_shapes, sems, collective_id, name, *args):
    return pl.pallas_call(
        kernel,
        out_shape=out_shapes,
        in_specs=[ANY] * len(args),
        out_specs=[ANY] * len(out_shapes),
        scratch_shapes=[
            pltpu.SemaphoreType.DMA((sems,)),
            pltpu.SemaphoreType.DMA((sems,)),
            pltpu.SemaphoreType.DMA((4,)),
        ],
        compiler_params=pltpu.CompilerParams(collective_id=collective_id, has_side_effects=True),
        name=name,
    )(*args)


def shape(dims, dtype=BF16):
    return jax.ShapeDtypeStruct(dims, dtype)


def x_peers(x, zl, zh, y, c):
    return [((x + k) % 4, device((x + k) % 4, zl, zh, y, c)) for k in (1, 3, 2)]


def z_peers(x, zl, zh, y, c):
    places = [(zh * 2 + zl + k) % 4 for k in (1, 3, 2)]
    return [(place, device(x, place % 2, place // 2, y, c)) for place in places]


def y_peers(x, zl, zh, y, c):
    return [((y + k) % 4, device(x, zl, zh, (y + k) % 4, c)) for k in (1, 3, 2)]


VMEM = pl.BlockSpec(memory_space=pltpu.VMEM)
SIDE_ROWS = 136


def exchange(src, slots, mine, peers, send, recv, first):
    copies = []
    for k, (place, peer) in enumerate(peers):
        part = src(place) if callable(src) else src
        copies.append(remote(part, slots.at[mine], send.at[first + k], recv.at[first + k], peer))
        copies[-1].start()
    return copies


def weight_gather(srcs, fulls, place, send, recv, base):
    x, zl, zh, y, c = place
    partner = device(x, 1 - zl, zh, y, c)
    across = device(x, 1 - zl, 1 - zh, y, c)
    sibling = device(x, zl, zh, y, 1 - c)
    rows_of = [device(x, zl, zh, (y + k) % 4, c) for k in (1, 3, 2)]
    z_of = [(zl, zh), (1 - zl, zh), (1 - zl, 1 - zh), (zl, 1 - zh)]
    many = len(srcs)
    started = []

    def view(ref, b_zl, b_zh, b_y, b_c):
        wide = ref.shape[2] // 2
        row = (b_zh * 8 + b_y * 2 + b_c) * BLOCK
        return ref.at[
            :, pl.ds(pl.multiple_of(row, BLOCK), BLOCK), pl.ds(pl.multiple_of(b_zl * wide, wide), wide)
        ]

    def sem(zi, k, sib, a):
        return base + ((zi * 4 + k) * 2 + sib) * many + a

    def refs(zi, k, sib=0):
        by = (y + 4 - (0, 1, 3, 2)[k]) % 4
        return [view(full, *z_of[zi], by, 1 - c if sib else c) for full in fulls]

    def push(src, dst, i, peer):
        started.append(remote(src, dst, send.at[i], recv.at[i], peer))
        started[-1].start()

    def wait_block(zi, k, sib=0):
        for a, ref in enumerate(refs(zi, k, sib)):
            i = sem(zi, k, sib, a)
            remote(ref, ref, send.at[i], recv.at[i], sibling).wait_recv()

    def spread(zi, blocks):
        for a, src in enumerate(blocks):
            dst = view(fulls[a], *z_of[zi], y, c)
            for k, peer in enumerate(rows_of):
                push(src, dst, sem(zi, k + 1, 0, a), peer)
            push(src, dst, sem(zi, 0, 1, a), sibling)

    own = [view(full, zl, zh, y, c) for full in fulls]

    def start(local, first):
        for a, src in enumerate(srcs):
            push(src, own[a], sem(1, 0, 0, a), partner)
        for a, src in enumerate(srcs):
            push(src, own[a], sem(2, 0, 0, a), across)
        kept = [pltpu.make_async_copy(src, own[a], local.at[first + a]) for a, src in enumerate(srcs)]
        for copy in kept:
            copy.start()
        spread(0, srcs)
        return kept

    def relay_z():
        wait_block(1, 0)
        for a, ref in enumerate(refs(1, 0)):
            push(ref, ref, sem(3, 0, 0, a), across)
        spread(1, refs(1, 0))
        wait_block(2, 0)
        spread(2, refs(2, 0))
        wait_block(3, 0)
        spread(3, refs(3, 0))

    def relay_y(zi):
        for k in range(1, 4):
            wait_block(zi, k)
            for a, ref in enumerate(refs(zi, k)):
                push(ref, ref, sem(zi, k, 1, a), sibling)

    def finish():
        for zi in range(4):
            for k in range(4):
                wait_block(zi, k, 1)
        for copy in started:
            copy.wait_send()

    greeted = [partner, across, sibling] + rows_of
    return greeted, start, relay_z, relay_y, finish


def collect(history, small, up, top_weights, bottom_weights):
    slots, _, width = history.shape
    half = BLOCK // 2
    step = 16
    lanes = 128

    def kernel(
        hist, wa, wb, tw, bw, streams, top_out, bottom_out, full_a, full_b,
        top, bottom, acc, part_x, got_x, part_z, got_z,
        wsend, wrecv, send, recv, local, store,
    ):
        here = coords()
        x, zl, zh, y, c = here
        partner = device(x, 1 - zl, zh, y, c)
        peers = {k: device((x + k) % 4, zl, zh, y, c) for k in (1, 2, 3)}
        greeted, start, relay_z, relay_y, finish = weight_gather((wa, wb), (full_a, full_b), here, wsend, wrecv, 0)
        greet(greeted + [peers[1], peers[2], peers[3]])

        def rows(k, other, low):
            begin = ((x + k) % 4 * 2 + (1 - zl if other else zl)) * BLOCK + low * half
            return hist.at[:, pl.ds(pl.multiple_of(begin, half), half)]

        copies = []

        def push(src, dst, i, peer):
            copies.append(remote(src, dst, send.at[i], recv.at[i], peer))
            copies[-1].start()

        def came(ref, i):
            remote(ref, ref, send.at[i], recv.at[i], partner).wait_recv()

        own = []
        for other in range(2):
            own.append(pltpu.make_async_copy(rows(0, other, 0), top.at[other, 0], local.at[other]))
        for k in range(4):
            own.append(pltpu.make_async_copy(rows(k, 0, 1), bottom.at[k, 0], local.at[2 + k]))
        for copy in own:
            copy.start()
        kept = start(local, 6)
        for k in (2, 1, 3, 0):
            push(rows(k, 1, 1), bottom.at[k, 1], k, partner)
        for other in (1, 0):
            for k in (1, 3, 2):
                push(rows(k, other, 0), top.at[other, 4 - k], 4 + 3 * other + 3 - k, peers[k])

        def mix(entries, factors_of, groups, into, offset):
            def some_rows(r, carry):
                at = pl.ds(pl.multiple_of(r * step, step), step)
                there = pl.ds(pl.multiple_of(offset + r * step, step), step)
                for g in range(groups):
                    factors = [
                        [jnp.broadcast_to(factors_of(g * 3 + e, at)[:, s : s + 1], (step, lanes)) for s in range(4)]
                        for e in range(3)
                    ]

                    def some_cols(b, inner, g=g, factors=factors):
                        cols = pl.ds(pl.multiple_of(b * lanes, lanes), lanes)
                        entry = [entries(g, e)[at, cols].astype(jnp.float32) for e in range(3)]
                        for s in range(4):
                            value = factors[0][s] * entry[0] + factors[1][s] * entry[1] + factors[2][s] * entry[2]
                            into[s, there, cols] = value if g == 0 else into[s, there, cols] + value
                        return inner

                    lax.fori_loop(0, width // lanes, some_cols, 0, unroll=4)
                return carry

            lax.fori_loop(0, half // step, some_rows, 0)

        def mix_top(other, into, offset):
            mix(lambda g, e: top.at[other, g, e], lambda i, at: tw[other, i, at, :], 4, into, offset)

        def mix_bottom(k, into, offset):
            mix(lambda g, e: bottom.at[k, g, e], lambda i, at: bw[k, i, at, :], 2, into, offset)

        stores = []

        def keep(src, dst):
            stores.append(pltpu.make_async_copy(src, dst, store.at[len(stores)]))
            stores[-1].start()

        def bottom_sums(k):
            came(bottom.at[k, 1], k)
            own[2 + k].wait()
            keep(bottom.at[k], bottom_out.at[k])
            if k == 0:
                mix_bottom(0, streams, half)
                return
            mix_bottom(k, acc, 0)
            part_x[k - 1] = acc[...].astype(BF16)
            push(part_x.at[k - 1], got_x.at[3 - k], 10 + 3 - k, peers[k])

        relay_z()
        bottom_sums(2)
        own[1].wait()
        for k in (1, 2, 3):
            came(top.at[1, k], 4 + 3 + k - 1)
        keep(top.at[1], top_out.at[1])
        mix_top(1, acc, 0)
        part_z[...] = acc[...].astype(BF16)
        push(part_z, got_z, 13, partner)
        bottom_sums(1)
        relay_y(0)
        bottom_sums(3)
        own[0].wait()
        for k in (1, 2, 3):
            came(top.at[0, k], 4 + k - 1)
        keep(top.at[0], top_out.at[0])
        mix_top(0, streams, 0)
        relay_y(1)
        bottom_sums(0)
        relay_y(2)
        relay_y(3)
        came(got_z, 13)

        def add(r, carry, offset, parts):
            at = pl.ds(pl.multiple_of(r * step, step), step)
            there = pl.ds(pl.multiple_of(offset + r * step, step), step)
            for s in range(4):
                value = streams[s, there, :]
                for part in parts:
                    value = value + part(s, at)
                streams[s, there, :] = value
            return carry

        def add_all(offset, parts):
            lax.fori_loop(0, half // step, lambda r, carry: add(r, carry, offset, parts), 0)

        add_all(0, [lambda s, at: got_z[s, at, :].astype(jnp.float32)])
        for k in (1, 2, 3):
            came(got_x.at[k - 1], 10 + k - 1)
        add_all(half, [lambda s, at, k=k: got_x[k, s, at, :].astype(jnp.float32) for k in range(3)])
        finish()
        for copy in kept + stores:
            copy.wait()
        for copy in copies:
            copy.wait_send()

    n_a, rows_a, cols_a = small.shape
    n_b, rows_b, cols_b = up.shape
    vmem = pltpu.VMEM
    sem = pltpu.SemaphoreType.DMA
    top_shape, bottom_shape = (2, 4, slots, half, width), (4, 2, slots, half, width)
    piece = (4, half, width)
    return pl.pallas_call(
        kernel,
        out_shape=[
            shape((4, BLOCK, width), jnp.float32),
            shape(top_shape),
            shape(bottom_shape),
            shape((n_a, rows_a * 16, cols_a * 2)),
            shape((n_b, rows_b * 16, cols_b * 2)),
        ],
        in_specs=[ANY, ANY, ANY, VMEM, VMEM],
        out_specs=[VMEM, ANY, ANY, ANY, ANY],
        scratch_shapes=[
            vmem(top_shape, BF16),
            vmem(bottom_shape, BF16),
            vmem(piece, jnp.float32),
            vmem((3,) + piece, BF16),
            vmem((3,) + piece, BF16),
            vmem(piece, BF16),
            vmem(piece, BF16),
            sem((64,)),
            sem((64,)),
            sem((14,)),
            sem((14,)),
            sem((8,)),
            sem((6,)),
        ],
        compiler_params=pltpu.CompilerParams(
            collective_id=1, has_side_effects=True, vmem_limit_bytes=48 * 2**20
        ),
        name="collect",
    )(history, small, up, top_weights, bottom_weights)


def dot_nt(left, right):
    return lax.dot_general(left, right, (((1,), (1,)), ((), ())), preferred_element_type=jnp.float32)


def dot_nn(left, right):
    return lax.dot_general(left, right, (((1,), (0,)), ((), ())), preferred_element_type=jnp.float32)


def dot_tn(left, right):
    return lax.dot_general(left, right, (((0,), (0,)), ((), ())), preferred_element_type=jnp.float32)


def attend(queries, keys, values, other_keys, other_values, query_at, key_at):
    rows, cols = queries.shape
    heads = cols // HD
    scale = HD ** (-0.5)
    tall = 256

    def kernel(q, k, v, ok, ov, qa, ka, out, lse):
        for r in range(rows // tall):
            at = pl.ds(r * tall, tall)
            query_pos, query_doc = qa[at, 0:1], qa[at, 1:2]
            scores = []
            for half, key in enumerate((k, ok)):
                allowed = (ka[2 * half : 2 * half + 1, :] <= query_pos) & (
                    ka[2 * half + 1 : 2 * half + 2, :] == query_doc
                )
                scores.append(jnp.where(allowed, dot_nt(q[at, :], key[...]) * scale, NEGATIVE))
            top = jnp.maximum(
                jnp.max(scores[0], axis=1, keepdims=True), jnp.max(scores[1], axis=1, keepdims=True)
            )
            shifted = [jnp.exp(part - top) for part in scores]
            total = jnp.sum(shifted[0], axis=1, keepdims=True) + jnp.sum(shifted[1], axis=1, keepdims=True)
            share = 1.0 / total
            result = dot_nn((shifted[0] * share).astype(BF16), v[...])
            result = result + dot_nn((shifted[1] * share).astype(BF16), ov[...])
            out[at, :] = result.astype(BF16)
            lse[0, at, :] = top + jnp.log(total)

    head = pl.BlockSpec((rows, HD), lambda h: (0, h))
    return pl.pallas_call(
        kernel,
        grid=(heads,),
        out_shape=[shape((rows, cols)), shape((heads, rows, 1), jnp.float32)],
        in_specs=[head] * 5
        + [pl.BlockSpec(query_at.shape, lambda h: (0, 0)), pl.BlockSpec(key_at.shape, lambda h: (0, 0))],
        out_specs=[head, pl.BlockSpec((1, rows, 1), lambda h: (h, 0, 0))],
        compiler_params=pltpu.CompilerParams(vmem_limit_bytes=40 * 2**20),
        name="attend",
    )(queries, keys, values, other_keys, other_values, query_at, key_at)


def attend_back(queries, keys, values, other_keys, other_values, query_at, key_at, log_totals, out_cot):
    rows, cols = queries.shape
    heads = cols // HD
    scale = HD ** (-0.5)
    tall = 256

    def kernel(q, k, v, ok, ov, qa, ka, lse, cot, dq, dk, dv, dok, dov, key_sum, value_sum):
        for r in range(rows // tall):
            at = pl.ds(r * tall, tall)
            query_pos, query_doc = qa[at, 0:1], qa[at, 1:2]
            probs, prob_grads = [], []
            for half, (key, value) in enumerate(((k, v), (ok, ov))):
                allowed = (ka[2 * half : 2 * half + 1, :] <= query_pos) & (
                    ka[2 * half + 1 : 2 * half + 2, :] == query_doc
                )
                scores = jnp.where(allowed, dot_nt(q[at, :], key[...]) * scale, NEGATIVE)
                probs.append(jnp.exp(scores - lse[0, at, :]))
                prob_grads.append(dot_nt(cot[at, :], value[...]))
            row_dot = sum(jnp.sum(p * g, axis=1, keepdims=True) for p, g in zip(probs, prob_grads))
            query_grad = jnp.zeros((tall, HD), jnp.float32)
            for half, (p, g) in enumerate(zip(probs, prob_grads)):
                score_cot = (p * (g - row_dot)).astype(BF16)
                key = (k, ok)[half]
                query_grad = query_grad + dot_nn(score_cot, key[...])
                key_part = dot_tn(score_cot, q[at, :])
                value_part = dot_tn(p.astype(BF16), cot[at, :])
                if r == 0:
                    key_sum[half] = key_part
                    value_sum[half] = value_part
                else:
                    key_sum[half] += key_part
                    value_sum[half] += value_part
            dq[at, :] = query_grad * scale
        dk[...] = key_sum[0] * scale
        dv[...] = value_sum[0]
        dok[...] = (key_sum[1] * scale).astype(BF16)
        dov[...] = value_sum[1].astype(BF16)

    head = pl.BlockSpec((rows, HD), lambda h: (0, h))
    return pl.pallas_call(
        kernel,
        grid=(heads,),
        out_shape=[shape((rows, cols), jnp.float32)] * 3 + [shape((rows, cols))] * 2,
        in_specs=[head] * 5
        + [pl.BlockSpec(query_at.shape, lambda h: (0, 0)), pl.BlockSpec(key_at.shape, lambda h: (0, 0))]
        + [pl.BlockSpec((1, rows, 1), lambda h: (h, 0, 0)), head],
        out_specs=[head] * 5,
        scratch_shapes=[pltpu.VMEM((2, rows, HD), jnp.float32)] * 2,
        compiler_params=pltpu.CompilerParams(vmem_limit_bytes=40 * 2**20),
        name="attend_back",
    )(queries, keys, values, other_keys, other_values, query_at, key_at, log_totals, out_cot)


def erf(value):
    value = jnp.clip(value, -4.0, 4.0)
    square = value * value
    top = jnp.full_like(value, -2.72614225801306e-10)
    for factor in (
        2.77068142495902e-08,
        -2.10102402082508e-06,
        -5.69250639462346e-05,
        -7.34990630326855e-04,
        -2.95459980854025e-03,
        -1.60960333262415e-02,
    ):
        top = top * square + factor
    bottom = jnp.full_like(value, -1.45660718464996e-05)
    for factor in (-2.13374055278905e-04, -1.68282697438203e-03, -7.37332916720468e-03, -1.42647390514189e-02):
        bottom = bottom * square + factor
    return value * top / bottom


def gelu_both(value):
    share = 0.5 * (1.0 + erf(value * 0.7071067811865476))
    bell = jnp.exp(-0.5 * value * value) * 0.3989422804014327
    return value * share, share + value * bell


def row_mean(value):
    return jnp.mean(value, axis=1, keepdims=True)


def middle(heads, small, up, down, stream, gains, da_in, da_out, da_bias, out_grad, mix_cot_in):
    rows_all, head_cols = heads.shape
    width, hidden = up.shape[1:]
    step = 16
    half = BLOCK // 2
    tile = 2 * BLOCK
    tiles = width // tile

    def kernel(
        heads, small, up, down, stream, gains, da_in, da_out, da_bias, out_grad, mix_cot_in,
        block_out, mix_next, residual_grad, heads_cot, gain_grads, side_sum, other, out_proj_grad, up_sum, down_sum,
        w_out, w_up, w_down, mid_all, active, slope, cot_all, up_cot, attn_cot,
        part, got1, got3, own, residual, unit, total, flat, aux, inv, grad_stage, sums,
        y_slots, z_part, z_slots, c_part, c_slot, x_slots, result,
        load, send, recv, gsend, grecv, gkeep, sends, recvs, dload,
    ):
        x, zl, zh, y, c = coords()
        z = zh * 2 + zl
        along_z, along_y = z_peers(x, zl, zh, y, c), y_peers(x, zl, zh, y, c)
        sibling = device(x, zl, zh, y, 1 - c)
        steps = (1, 3, 2)
        places = {k: (x + k) % 4 for k in steps}
        peers = {k: device(places[k], zl, zh, y, c) for k in steps}
        right, left, far = places[1], places[3], places[2]
        loads = [
            pltpu.make_async_copy(small.at[3], w_out, load.at[0]),
            pltpu.make_async_copy(up.at[0], w_up, load.at[1]),
            pltpu.make_async_copy(down.at[0], w_down, load.at[2]),
        ]
        for copy in loads:
            copy.start()
        greet([peers[k] for k in steps] + [peer for _, peer in along_z + along_y] + [sibling])

        def block(place):
            return pl.ds(pl.multiple_of(place * BLOCK, BLOCK), BLOCK)

        def chunks(work, place=0):
            def one(r, carry):
                begin = r * step
                work(
                    pl.ds(pl.multiple_of(begin, step), step),
                    pl.ds(pl.multiple_of(place * BLOCK + begin, step), step),
                )
                return carry

            lax.fori_loop(0, BLOCK // step, one, 0)

        sent = []
        given = ({}, {}, {})

        def arrived(stage, got):
            for k in steps:
                i = stage * 3 + k - 1
                remote(got.at[k - 1], got.at[k - 1], send.at[i], recv.at[i], sibling).wait_recv()

        def push(src, dst, i, peer):
            copy = remote(src, dst, send.at[i], recv.at[i], peer)
            copy.start()
            sent.append(copy)
            return copy

        def give_part(stage, k, got, product):
            if k == 0:
                own[...] = product
                return
            slot = stage % 2
            if stage == 2:
                given[0][k].wait_send()
            part[slot, k - 1] = product.astype(BF16)
            given[stage][k] = push(part.at[slot, k - 1], got.at[k - 1], stage * 3 + k - 1, peers[k])

        def spread(buf, base):
            def piece(place, top):
                begin = pl.multiple_of(place * BLOCK + (0 if top else half), half)
                return buf.at[pl.ds(begin, half)]

            first = [
                push(piece(x, True), piece(x, True), base, peers[1]),
                push(piece(x, False), piece(x, False), base + 2, peers[3]),
                push(piece(x, False), piece(x, False), base + 1, peers[1]),
                push(piece(x, True), piece(x, True), base + 3, peers[3]),
            ]

            def forward():
                first[0].wait_recv()
                one = push(piece(left, True), piece(left, True), base + 4, peers[1])
                first[1].wait_recv()
                two = push(piece(right, False), piece(right, False), base + 5, peers[3])
                return one, two

            return first, forward

        def gathered(buf, base, work):
            first, forward = spread(buf, base)
            work(0, x)
            one, two = forward()
            first[2].wait_recv()
            work(3, left)
            first[3].wait_recv()
            work(1, right)
            one.wait_recv()
            two.wait_recv()
            work(2, far)

        loads[0].wait()
        for k in (2, 1, 3, 0):
            place = x if k == 0 else places[k]
            give_part(0, k, got1, dot_nt(heads[block(place), :], w_out[...]))
        arrived(0, got1)

        def to_mid(at, there):
            value = stream[3, at, :] + own[at, :]
            for k in range(3):
                value = value + got1[k, at, :].astype(jnp.float32)
            residual[at, :] = value
            centered = value - row_mean(value)
            scale = lax.rsqrt(row_mean(centered * centered) + EPSILON)
            inv[at, :BLOCK] = jnp.broadcast_to(scale, (step, BLOCK))
            normed = centered * scale
            unit[at, :] = normed
            mid_all[there, :] = (normed * gains[3:4, :]).astype(BF16)

        chunks(to_mid, x)

        waited = []

        def feed(k, place):
            if not waited:
                loads[1].wait()
            total[...] = dot_nn(mid_all[block(place), :], w_up[...])

            def bend(at, there):
                value, change = gelu_both(total[at, :])
                active[there, :] = value.astype(BF16)
                slope[there, :] = change.astype(slope.dtype)

            chunks(bend, place)
            if not waited:
                loads[2].wait()
                waited.append(True)
            give_part(1, k, got3, dot_nt(active[block(place), :], w_down[...]))

        gathered(mid_all, 9, feed)
        arrived(1, got3)

        def to_out(at, _):
            value = residual[at, :] + own[at, :]
            for k in range(3):
                value = value + got3[k, at, :].astype(jnp.float32)
            block_out[at, :] = value.astype(BF16)
            scale = lax.rsqrt(row_mean(value * value) + EPSILON)
            inv[at, BLOCK:] = jnp.broadcast_to(scale, (step, BLOCK))
            residual[at, :] = value * scale
            flat[at, :] = (value * scale * gains[4:5, :]).astype(BF16)

        chunks(to_out)
        inner_act, inner_slope = gelu_both(dot_nn(flat[...], da_in[...]))
        inner_act = inner_act.astype(BF16)
        mix_next[...] = dot_nn(inner_act, da_out[...]) + da_bias[...]
        mix_cot = mix_cot_in[...].astype(BF16)
        inner_cot = (dot_nt(mix_cot, da_out[...]) * inner_slope).astype(BF16)
        aux[...] = dot_nt(inner_cot, da_in[...])
        sums[...] = jnp.zeros_like(sums)

        def to_cot(at, there):
            rms_unit = residual[at, :]
            grad = aux[at, :]
            product = grad * rms_unit
            sums[0] += product[:8] + product[8:]
            scaled = grad * gains[4:5, :]
            scale = inv[at, BLOCK : BLOCK + 1]
            value = out_grad[at, :].astype(jnp.float32) + scale * (
                scaled - rms_unit * row_mean(scaled * rms_unit)
            )
            residual[at, :] = value
            cot_all[there, :] = value.astype(BF16)

        chunks(to_cot, x)

        def small_grads():
            grad = dot_tn(flat[...], inner_cot)
            c_rows = SIDE_ROWS
            bias = jnp.sum(mix_cot_in[...], axis=0, keepdims=True)
            tail = jnp.concatenate(
                [
                    dot_tn(inner_act, mix_cot)[:104],
                    jnp.where(lax.broadcasted_iota(jnp.int32, (24, BLOCK), 0) == 0, bias, 0.0),
                ],
                axis=0,
            )
            whole = jnp.concatenate([grad, tail], axis=0)
            for py in range(4):
                for pz in range(4):
                    begin = (py * 4 + pz) * c_rows
                    result[py, pz] = whole[begin : begin + c_rows]

        side = {}

        def side_start():
            small_grads()
            side[0] = exchange(lambda py: result.at[py], y_slots, y, along_y, sends, recvs, 0)
            y_slots[y] = result[y]

        def side_z():
            for copy in side[0]:
                copy.wait()
            z_part[...] = y_slots[0] + y_slots[1] + y_slots[2] + y_slots[3]
            side[1] = exchange(lambda pz: z_part.at[pz], z_slots, z, along_z, sends, recvs, 3)
            z_slots[z] = z_part[z]

        def side_core():
            for copy in side[1]:
                copy.wait()
            c_part[...] = z_slots[0] + z_slots[1] + z_slots[2] + z_slots[3]
            side[2] = remote(c_part, c_slot, sends.at[6], recvs.at[6], sibling)
            side[2].start()

        def side_x():
            side[2].wait()
            x_slots[x] = c_part[...] + c_slot[...]
            along_x = [(places[k], peers[k]) for k in steps]
            side[3] = exchange(x_slots.at[x], x_slots, x, along_x, sends, recvs, 7)

        def side_up_z():
            for copy in side[3]:
                copy.wait()
            side_sum[y, z] = x_slots[0] + x_slots[1] + x_slots[2] + x_slots[3]
            side[4] = exchange(side_sum.at[y, z], side_sum.at[y], z, along_z, sends, recvs, 10)

        def side_up_y():
            for copy in side[4]:
                copy.wait()
            side[5] = exchange(side_sum.at[y], side_sum, y, along_y, sends, recvs, 13)

        def feed_back(k, place):
            total[...] = dot_nn(cot_all[block(place), :], w_down[...])

            def bend(at, there):
                up_cot[there, :] = (total[at, :] * slope[there, :].astype(jnp.float32)).astype(BF16)

            chunks(bend, place)
            give_part(2, k, got1, dot_nt(up_cot[block(place), :], w_up[...]))

        first, forward = spread(cot_all, 15)
        side_start()
        feed_back(0, x)
        one, two = forward()
        first[2].wait_recv()
        feed_back(3, left)
        first[3].wait_recv()
        feed_back(1, right)
        side_z()
        one.wait_recv()
        two.wait_recv()
        feed_back(2, far)
        side_core()

        def weight_grad(which, left_side, right_side):
            def copies(m):
                slot = lax.rem(m, 2)
                mine = grad_stage.at[slot, pl.ds(pl.multiple_of(c * BLOCK, BLOCK), BLOCK)]
                theirs = grad_stage.at[slot, pl.ds(pl.multiple_of((1 - c) * BLOCK, BLOCK), BLOCK)]
                i = which * tiles + m
                stays = (w_up, w_down)[which].at[pl.ds(pl.multiple_of(m * BLOCK, BLOCK), BLOCK)]
                return (
                    pltpu.make_async_copy(mine, stays, gkeep.at[slot]),
                    remote(theirs, other.at[which, m], gsend.at[i], grecv.at[i], sibling),
                )

            def finish(m):
                stay, go = copies(m)
                stay.wait()
                go.wait_send()

            def one(m, carry):
                @pl.when(m >= 2)
                def _():
                    finish(m - 2)

                cols = pl.ds(pl.multiple_of(m * tile, tile), tile)
                grad_stage[lax.rem(m, 2)] = dot_tn(left_side[:, cols], right_side[...]).astype(BF16)
                for copy in copies(m):
                    copy.start()
                return carry

            lax.fori_loop(0, tiles, one, 0)
            finish(tiles - 2)
            finish(tiles - 1)

        def other_came(which):
            def one(m, carry):
                i = which * tiles + m
                remote(other.at[which, m], other.at[which, m], gsend.at[i], grecv.at[i], sibling).wait_recv()
                return carry

            return one

        def fetch_other(which):
            lax.fori_loop(0, tiles, other_came(which), 0)
            for m in range(tiles):
                fetch(which, m).start()

        def fetch(which, m):
            there = (w_up, w_down)[which].at[pl.ds((tiles + m) * BLOCK, BLOCK)]
            return pltpu.make_async_copy(other.at[which, m], there, dload.at[which * tiles + m])

        def add_cores(which):
            whole = (w_up, w_down)[which]
            for m in range(tiles):
                fetch(which, m).wait()

            def one(r, carry):
                at = pl.ds(pl.multiple_of(r * step, step), step)
                there = pl.ds(pl.multiple_of(tiles * BLOCK + r * step, step), step)
                whole[at, :] = (whole[at, :].astype(jnp.float32) + whole[there, :].astype(jnp.float32)).astype(BF16)
                return carry

            lax.fori_loop(0, tiles * BLOCK // step, one, 0)
            done = pltpu.make_async_copy(
                whole.at[pl.ds(0, tiles * BLOCK)], (up_sum, down_sum)[which], gkeep.at[2 + which]
            )
            done.start()
            return done

        weight_grad(1, cot_all, active)
        side_x()
        arrived(2, got1)

        def to_residual(at, there):
            grad = own[at, :]
            for k in range(3):
                grad = grad + got1[k, at, :].astype(jnp.float32)
            mid_unit = unit[at, :]
            product = grad * mid_unit
            sums[1] += product[:8] + product[8:]
            scaled = grad * gains[3:4, :]
            scale = inv[at, 0:1]
            value = residual[at, :] + scale * (
                scaled - row_mean(scaled) - mid_unit * row_mean(scaled * mid_unit)
            )
            residual_grad[at, :] = value
            attn_cot[there, :] = value.astype(BF16)

        chunks(to_residual, x)
        first, forward = spread(attn_cot, 21)

        def head_back(place):
            heads_cot[block(place), :] = dot_nn(attn_cot[block(place), :], w_out[...]).astype(BF16)

        side_up_z()
        head_back(x)
        one, two = forward()
        fetch_other(1)
        weight_grad(0, mid_all, up_cot)
        side_up_y()
        down_done = add_cores(1)
        fetch_other(0)
        gain_grads[...] = jnp.sum(sums[...], axis=1)
        first[2].wait_recv()
        head_back(left)
        first[3].wait_recv()
        head_back(right)
        one.wait_recv()
        two.wait_recv()
        head_back(far)

        def out_grad_copy(m):
            rows = pl.ds(pl.multiple_of(m * tile, tile), tile)
            slot = lax.rem(m, 2)
            return pltpu.make_async_copy(
                grad_stage.at[slot, :, pl.ds(0, head_cols)], out_proj_grad.at[rows], gkeep.at[slot]
            )

        def out_grad_tile(m, carry):
            @pl.when(m >= 2)
            def _():
                out_grad_copy(m - 2).wait()

            cols = pl.ds(pl.multiple_of(m * tile, tile), tile)
            grad_stage[lax.rem(m, 2), :, :head_cols] = dot_tn(attn_cot[:, cols], heads[...]).astype(BF16)
            out_grad_copy(m).start()
            return carry

        lax.fori_loop(0, tiles, out_grad_tile, 0)
        out_grad_copy(tiles - 2).wait()
        out_grad_copy(tiles - 1).wait()
        for copy in side[5]:
            copy.wait()
        up_done = add_cores(0)
        down_done.wait()
        up_done.wait()
        for i, copy in enumerate(sent):
            if all(copy is not first for first in given[0].values()):
                copy.wait_send()

    f32 = jnp.float32
    vmem = pltpu.VMEM
    piece = (SIDE_ROWS, 128)
    return pl.pallas_call(
        kernel,
        out_shape=[
            shape((BLOCK, width)),
            shape((BLOCK, BLOCK), f32),
            shape((BLOCK, width), f32),
            shape(heads.shape),
            shape((2, width), f32),
            shape((4, 4) + piece, f32),
            shape((2, tiles, BLOCK, hidden)),
            shape((width, head_cols)),
            shape((tiles * BLOCK, hidden)),
            shape((tiles * BLOCK, hidden)),
        ],
        in_specs=[VMEM, ANY, ANY, ANY] + [VMEM] * 7,
        out_specs=[VMEM] * 6 + [ANY] * 4,
        scratch_shapes=[
            vmem((width, head_cols), BF16),
            vmem((width, hidden), BF16),
            vmem((width, hidden), BF16),
            vmem((rows_all, width), BF16),
            vmem((rows_all, hidden), BF16),
            vmem((rows_all, hidden), f32),
            vmem((rows_all, width), BF16),
            vmem((rows_all, hidden), BF16),
            vmem((rows_all, width), BF16),
            vmem((2, 3, BLOCK, width), BF16),
            vmem((3, BLOCK, width), BF16),
            vmem((3, BLOCK, width), BF16),
            vmem((BLOCK, width), f32),
            vmem((BLOCK, width), f32),
            vmem((BLOCK, width), f32),
            vmem((BLOCK, width), f32),
            vmem((BLOCK, width), BF16),
            vmem((BLOCK, width), f32),
            vmem((BLOCK, 2 * BLOCK), f32),
            vmem((2, tile, hidden), BF16),
            vmem((2, 8, width), f32),
            vmem((4, 4) + piece, f32),
            vmem((4,) + piece, f32),
            vmem((4,) + piece, f32),
            vmem(piece, f32),
            vmem(piece, f32),
            vmem((4,) + piece, f32),
            vmem((4, 4) + piece, f32),
            pltpu.SemaphoreType.DMA((3,)),
            pltpu.SemaphoreType.DMA((27,)),
            pltpu.SemaphoreType.DMA((27,)),
            pltpu.SemaphoreType.DMA((2 * tiles,)),
            pltpu.SemaphoreType.DMA((2 * tiles,)),
            pltpu.SemaphoreType.DMA((4,)),
            pltpu.SemaphoreType.DMA((16,)),
            pltpu.SemaphoreType.DMA((16,)),
            pltpu.SemaphoreType.DMA((2 * tiles,)),
        ],
        compiler_params=pltpu.CompilerParams(
            collective_id=4, has_side_effects=True, vmem_limit_bytes=62 * 2**20
        ),
        name="middle",
    )(heads, small, up, down, stream, gains, da_in, da_out, da_bias, out_grad, mix_cot_in)


def project(streams, gains, small, tables, down):
    width = streams.shape[2]
    cols = small.shape[2]
    rows_all = 4 * BLOCK
    step = 16
    half = BLOCK // 2
    order = (1, 2, 0)

    def kernel(
        streams, gains, small, tables, down,
        queries, keys, values, other_keys, other_values, normed_out, full_down,
        weights, normed, load, send, recv, zsend, zrecv, local, wsend, wrecv,
    ):
        x, zl, zh, y, c = coords()
        partner = device(x, 1 - zl, zh, y, c)
        places = {k: (x + k) % 4 for k in (1, 2, 3)}
        right, left, far = places[1], places[3], places[2]
        peers = {k: device(places[k], zl, zh, y, c) for k in (1, 3)}
        loads = [pltpu.make_async_copy(small.at[i], weights.at[i], load.at[i]) for i in range(3)]
        for i in order:
            loads[i].start()
        greeted, start, relay_z, relay_y, finish = weight_gather(
            (down,), (full_down,), (x, zl, zh, y, c), wsend, wrecv, 0
        )
        greet(greeted + [peers[1], peers[3]])
        kept = start(local, 3)

        def block(place):
            return pl.ds(pl.multiple_of(place * BLOCK, BLOCK), BLOCK)

        def piece(i, place, top):
            begin = pl.multiple_of(place * BLOCK + (0 if top else half), half)
            return normed.at[i, pl.ds(begin, half)]

        copies = {}

        def push(i, number, place, top, peer):
            part = piece(i, place, top)
            j = i * 6 + number
            copies[i, number] = remote(part, part, send.at[j], recv.at[j], peer)
            copies[i, number].start()

        for i in order:

            def norm(r, carry, i=i):
                at = pl.ds(pl.multiple_of(r * step, step), step)
                there = pl.ds(pl.multiple_of(x * BLOCK + r * step, step), step)
                value = streams[i, at, :]
                centered = value - row_mean(value)
                scale = lax.rsqrt(row_mean(centered * centered) + EPSILON)
                normed[i, there, :] = (centered * scale * gains[i : i + 1, :]).astype(BF16)
                return carry

            lax.fori_loop(0, BLOCK // step, norm, 0)
            push(i, 0, x, True, peers[1])
            push(i, 2, x, False, peers[3])
            push(i, 1, x, False, peers[1])
            push(i, 3, x, True, peers[3])

        given = []

        def work(i, place):
            result = dot_nn(normed[i, block(place), :], weights[i])
            out = (queries, keys, values)[i]
            if i == 2:
                out[block(place), :] = result.astype(BF16)
            else:
                at = block(place)
                for h in range(cols // HD):
                    part = result[:, h * HD : (h + 1) * HD]
                    ahead, behind = pltpu.roll(part, HD - ROT // 2, 1), pltpu.roll(part, ROT // 2, 1)
                    turned = part * tables[0, at, :] + ahead * tables[1, at, :] + behind * tables[2, at, :]
                    out[at, h * HD : (h + 1) * HD] = turned.astype(BF16)
            if i > 0:
                j = len(given)
                other = (None, other_keys, other_values)[i]
                given.append(remote(out.at[block(place)], other.at[block(place)], zsend.at[j], zrecv.at[j], partner))
                given[-1].start()

        for i in order:
            loads[i].wait()
            work(i, x)
        relay_z()
        for i in order:
            copies[i, 0].wait_recv()
            push(i, 4, left, True, peers[1])
            copies[i, 2].wait_recv()
            push(i, 5, right, False, peers[3])
            copies[i, 1].wait_recv()
            work(i, left)
            copies[i, 3].wait_recv()
            work(i, right)
            relay_y((1, 2, 0).index(i))
        stores = []
        for i in order:
            copies[i, 4].wait_recv()
            copies[i, 5].wait_recv()
            stores.append(pltpu.make_async_copy(normed.at[i], normed_out.at[i], local.at[i]))
            stores[-1].start()
            work(i, far)
        relay_y(3)
        finish()
        for copy in given + stores + kept:
            copy.wait()
        for copy in copies.values():
            copy.wait_send()

    vmem = pltpu.VMEM
    sem = pltpu.SemaphoreType.DMA
    return pl.pallas_call(
        kernel,
        out_shape=[shape((rows_all, cols))] * 5
        + [shape((3, rows_all, width)), shape((1, down.shape[1] * 16, down.shape[2] * 2))],
        in_specs=[VMEM, VMEM, ANY, VMEM, ANY],
        out_specs=[VMEM] * 5 + [ANY, ANY],
        scratch_shapes=[
            vmem((3, width, cols), BF16),
            vmem((3, rows_all, width), BF16),
            sem((3,)),
            sem((18,)),
            sem((18,)),
            sem((8,)),
            sem((8,)),
            sem((4,)),
            sem((32,)),
            sem((32,)),
        ],
        compiler_params=pltpu.CompilerParams(
            collective_id=2, has_side_effects=True, vmem_limit_bytes=40 * 2**20
        ),
        name="project",
    )(streams, gains, small, tables, down)


def inward(grads, gives, small, normed, out_proj_grad, streams, residual_grad, gains, late_gains, tables, down):
    rows_all, cols = grads[0].shape
    width = streams.shape[2]
    step = 16
    half = BLOCK // 2
    tile = 2 * BLOCK
    tiles = width // tile
    hidden = down.shape[3]
    thin = hidden // 2

    def kernel(
        dq, dk, dv, give_k, give_v, small, normed, out_proj_grad, streams, residual_grad, gains, late, tables,
        down,
        stream_cot, gain_grads, small_sum, down_out,
        weights, inputs, cots, got_k, got_v, far_part, near, hop, got, own, grad, swapped, sums, down_y, down_part, down_z, stream,
        load, send, recv, ssend, srecv, gsend, grecv, local,
    ):
        x, zl, zh, y, c = coords()
        z = zh * 2 + zl
        z = zh * 2 + zl
        along_z, along_y = z_peers(x, zl, zh, y, c), y_peers(x, zl, zh, y, c)
        partner = device(x, 1 - zl, zh, y, c)
        sibling = device(x, zl, zh, y, 1 - c)
        places = {k: (x + k) % 4 for k in (1, 2, 3)}
        peers = {k: device(places[k], zl, zh, y, c) for k in (1, 3)}
        loads = [pltpu.make_async_copy(small.at[i], weights.at[i], load.at[i]) for i in range(3)]
        loads += [pltpu.make_async_copy(normed.at[i], inputs.at[i], load.at[3 + i]) for i in range(3)]
        loads.append(pltpu.make_async_copy(out_proj_grad, grad.at[0], load.at[6]))
        loads.append(pltpu.make_async_copy(streams.at[pl.ds(0, 3)], stream, load.at[7]))
        for copy in loads:
            copy.start()
        greet([peers[1], peers[3], sibling] + [peer for _, peer in along_z + along_y])
        sides = []

        def side(src, dst, peer):
            i = len(sides)
            sides.append(remote(src, dst, ssend.at[i], srecv.at[i], peer))
            sides[-1].start()

        side(give_k, got_k, partner)
        side(give_v, got_v, partner)
        for py, peer in along_y:
            side(down.at[:, py], down_y.at[y], peer)
        locals_ = [pltpu.make_async_copy(down.at[:, y], down_y.at[y], local.at[0])]
        for copy in locals_:
            copy.start()

        def block(place):
            return pl.ds(pl.multiple_of(place * BLOCK, BLOCK), BLOCK)

        def turn_back(value):
            def one(at):
                part = value(at)
                ahead, behind = pltpu.roll(part, HD - ROT // 2, 1), pltpu.roll(part, ROT // 2, 1)
                return part * tables[0, at, :] - ahead * tables[1, at, :] - behind * tables[2, at, :]

            return one

        def to_cots(i, value):
            def one(r, carry):
                at = pl.ds(pl.multiple_of(r * step, step), step)
                for h in range(cols // HD):
                    head = slice(h * HD, (h + 1) * HD)
                    cots[i, at, head] = value(at, head).astype(BF16)
                return carry

            lax.fori_loop(0, rows_all // step, one, 0)

        def turned(value):
            return lambda at, head: turn_back(lambda at: value(at, head))(at)

        started = []

        def push(src, dst, i, peer):
            started.append(remote(src, dst, send.at[i], recv.at[i], peer))
            started[-1].start()

        def far_sums(i):
            if i == 0:
                loads[0].wait()
            else:
                loads[i].wait()
            far_part[i] = dot_nt(cots[i, block(places[2]), :], weights[i]).astype(BF16)
            push(far_part.at[i, pl.ds(0, half)], hop.at[i, 0], i * 4, peers[1])
            push(far_part.at[i, pl.ds(half, half)], hop.at[i, 1], i * 4 + 1, peers[3])

        def near_sums(i):
            for k, side_of in ((1, 0), (3, 1)):
                product = dot_nt(cots[i, block(places[k]), :], weights[i])
                begin = side_of * half
                j = i * 4 + side_of
                remote(hop.at[i, side_of], hop.at[i, side_of], send.at[j], recv.at[j], sibling).wait_recv()
                near[i, side_of] = product.astype(BF16)
                merged = product[begin : begin + half] + hop[i, side_of].astype(jnp.float32)
                near[i, side_of, begin : begin + half] = merged.astype(BF16)
                push(near.at[i, side_of], got.at[i, side_of], i * 4 + 2 + side_of, peers[k])

        def own_sums(i):
            own[i] = dot_nt(cots[i, block(x), :], weights[i])

        swaps = []

        def weight_grad(i):
            slot = (1, 0, 1, 0)[i]
            if i < 3:
                loads[3 + i].wait()

                def one(m, carry):
                    at = pl.ds(pl.multiple_of(m * tile, tile), tile)
                    grad[slot, at, :] = dot_tn(inputs[i, :, at], cots[i]).astype(BF16)
                    return carry

                lax.fori_loop(0, tiles, one, 0)
            else:
                loads[6].wait()
            for m in range(tiles):
                begin = pl.multiple_of(m * tile + (1 - c) * BLOCK, BLOCK)
                j = i * tiles + m
                swaps.append(
                    remote(grad.at[slot, pl.ds(begin, BLOCK)], swapped.at[i, m], gsend.at[j], grecv.at[j], sibling)
                )
                swaps[-1].start()

        def add_cores(i):
            for m in range(tiles):
                swaps_of[i][m].wait()

            def one(r, carry):
                m, part = r // (BLOCK // step), lax.rem(r, BLOCK // step)
                at = pl.ds(pl.multiple_of(m * tile + c * BLOCK + part * step, step), step)
                there = pl.ds(pl.multiple_of(part * step, step), step)
                value = grad[(1, 0, 1, 0)[i], at, :].astype(jnp.float32) + swapped[i, m, there, :].astype(jnp.float32)
                swapped[i, m, there, :] = value.astype(BF16)
                return carry

            lax.fori_loop(0, tiles * BLOCK // step, one, 0)
            locals_.append(pltpu.make_async_copy(swapped.at[i], small_sum.at[:, i], local.at[1 + i]))
            locals_[-1].start()

        swaps_of = {}

        def grads_of(i):
            begin = len(swaps)
            weight_grad(i)
            swaps_of[i] = swaps[begin:]

        to_cots(0, turned(lambda at, head: dq[at, head]))
        far_sums(0)
        near_sums(0)
        grads_of(3)
        grads_of(0)
        own_sums(0)
        sides[0].wait_recv()
        to_cots(1, turned(lambda at, head: dk[at, head] + got_k[at, head].astype(jnp.float32)))
        far_sums(1)
        sides[1].wait_recv()
        to_cots(2, lambda at, head: dv[at, head] + got_v[at, head].astype(jnp.float32))
        far_sums(2)
        near_sums(1)
        near_sums(2)
        add_cores(3)
        add_cores(0)
        grads_of(1)
        grads_of(2)
        own_sums(1)
        own_sums(2)
        for copy in sides[2:] + locals_[:1]:
            copy.wait()

        def add_four(parts, places, dst):
            def one(r, carry):
                at = pl.ds(pl.multiple_of(r * step, step), step)
                value = parts[(0,) + places + (at,)].astype(jnp.float32)
                for src in range(1, 4):
                    value = value + parts[(src,) + places + (at,)].astype(jnp.float32)
                dst[places + (at,)] = value.astype(dst.dtype)
                return carry

            lax.fori_loop(0, BLOCK // step, one, 0)

        def down_piece(high, low):
            return down_part.at[high, :, pl.ds(pl.multiple_of(low * thin, thin), thin)]

        for high in range(2):
            add_four(down_y, (high,), down_part)
        for pz, peer in along_z:
            side(down_piece(pz // 2, pz % 2), down_z.at[z], peer)
        down_z[z] = down_part[zh, :, pl.ds(pl.multiple_of(zl * thin, thin), thin)]
        add_cores(1)
        add_cores(2)
        loads[7].wait()
        sums[...] = jnp.zeros_like(sums)
        for i in range(3):
            for side_of in range(2):
                j = i * 4 + 2 + side_of
                remote(got.at[i, side_of], got.at[i, side_of], send.at[j], recv.at[j], sibling).wait_recv()

            def back(r, carry, i=i):
                at = pl.ds(pl.multiple_of(r * step, step), step)
                value = stream[i, at, :]
                centered = value - row_mean(value)
                scale = lax.rsqrt(row_mean(centered * centered) + EPSILON)
                unit = centered * scale
                above = own[i, at, :] + got[i, 0, at, :].astype(jnp.float32) + got[i, 1, at, :].astype(jnp.float32)
                product = above * unit
                sums[i] += product[:8] + product[8:]
                scaled = above * gains[i : i + 1, :]
                result = scale * (scaled - row_mean(scaled) - unit * row_mean(scaled * unit))
                stream_cot[i, at, :] = result.astype(BF16)
                return carry

            lax.fori_loop(0, BLOCK // step, back, 0)
        stream_cot[3] = residual_grad[...].astype(BF16)
        gain_grads[...] = jnp.zeros_like(gain_grads)
        for i in range(3):
            gain_grads[i : i + 1, :] = jnp.sum(sums[i], axis=0, keepdims=True)
        gain_grads[3:4, :] = late[1:2, :]
        gain_grads[4:5, :] = late[0:1, :]
        for copy in sides[5:]:
            copy.wait()
        add_four(down_z, (), down_out)
        for copy in started + sides[:2]:
            copy.wait_send()
        for copy in locals_[1:]:
            copy.wait()

    f32 = jnp.float32
    vmem = pltpu.VMEM
    sem = pltpu.SemaphoreType.DMA
    return pl.pallas_call(
        kernel,
        out_shape=[
            shape((4, BLOCK, width)),
            shape((8, width), f32),
            shape((tiles, 4, BLOCK, cols)),
            shape((BLOCK, thin), f32),
        ],
        in_specs=[VMEM] * 5 + [ANY] * 4 + [VMEM] * 4 + [ANY],
        out_specs=[VMEM, VMEM, ANY, VMEM],
        scratch_shapes=[
            vmem((3, width, cols), BF16),
            vmem((3, rows_all, width), BF16),
            vmem((3, rows_all, cols), BF16),
            vmem((rows_all, cols), BF16),
            vmem((rows_all, cols), BF16),
            vmem((3, BLOCK, width), BF16),
            vmem((3, 2, BLOCK, width), BF16),
            vmem((3, 2, half, width), BF16),
            vmem((3, 2, BLOCK, width), BF16),
            vmem((3, BLOCK, width), f32),
            vmem((2, width, cols), BF16),
            vmem((4, tiles, BLOCK, cols), BF16),
            vmem((3, 8, width), f32),
            vmem((4, 2, BLOCK, hidden), BF16),
            vmem((2, BLOCK, hidden), BF16),
            vmem((4, BLOCK, thin), BF16),
            vmem((3, BLOCK, width), f32),
            sem((8,)),
            sem((12,)),
            sem((12,)),
            sem((8,)),
            sem((8,)),
            sem((4 * tiles,)),
            sem((4 * tiles,)),
            sem((5,)),
        ],
        compiler_params=pltpu.CompilerParams(
            collective_id=5, has_side_effects=True, vmem_limit_bytes=60 * 2**20
        ),
        name="inward",
    )(
        *grads, *gives, small, normed, out_proj_grad, streams, residual_grad, gains, late_gains, tables, down
    )


def hand_out(top_hist, bottom_hist, top_weights, bottom_weights, stream_cot, gains, small, up):
    _, _, n, half, width = top_hist.shape
    cols = small.shape[3]
    thin = cols // 2
    hidden = up.shape[2] // 2
    step = 16
    lanes = 128

    def kernel(
        top_hist, bottom_hist, tw, bw, cot, gains, small, up,
        out, top_mix, bottom_mix, gains_out, small_out, up_out,
        top, bottom, top_stage, bottom_stage, cot_z, cot_x, mixes, turned,
        x_slots, z_slots, y_slots, c_part, c_slot,
        small_y, small_part, small_z, up_y, up_part, up_z,
        load, csend, crecv, send, recv, msend, mrecv, local, sends, recvs, ssend, srecv,
    ):
        x, zl, zh, y, c = coords()
        z = zh * 2 + zl
        partner = device(x, 1 - zl, zh, y, c)
        peers = {k: device((x + k) % 4, zl, zh, y, c) for k in (1, 2, 3)}
        loads = [pltpu.make_async_copy(top_hist.at[o], top.at[o], load.at[o]) for o in range(2)]
        loads += [pltpu.make_async_copy(bottom_hist.at[k], bottom.at[k], load.at[2 + k]) for k in range(4)]
        for i in (0, 2, 1, 3, 5, 4):
            loads[i].start()
        along_x, along_z = x_peers(x, zl, zh, y, c), z_peers(x, zl, zh, y, c)
        along_y = y_peers(x, zl, zh, y, c)
        sibling = device(x, zl, zh, y, 1 - c)
        greet([peer for _, peer in along_x + along_z + along_y] + [sibling])
        sides = []

        def side(src, dst, peer):
            i = len(sides)
            sides.append(remote(src, dst, ssend.at[i], srecv.at[i], peer))
            sides[-1].start()

        first = exchange(gains, x_slots, x, along_x, sends, recvs, 0)
        x_slots[x] = gains[...]
        copies = []

        def push(src, dst, send, recv, i, peer):
            copies.append(remote(src, dst, send.at[i], recv.at[i], peer))
            copies[-1].start()

        push(cot.at[:, pl.ds(0, half)], cot_z, csend, crecv, 0, partner)
        for k in (1, 3, 2):
            push(cot.at[:, pl.ds(half, half)], cot_x.at[3 - k], csend, crecv, 1 + 3 - k, peers[k])
        for py, peer in along_y:
            for high in range(2):
                side(small.at[high * 4 + py], small_y.at[y, high], peer)
        for py, peer in along_y:
            for high in range(2):
                side(up.at[high * 4 + py], up_y.at[y, high], peer)
        locals_ = [
            pltpu.make_async_copy(small.at[y], small_y.at[y, 0], local.at[0]),
            pltpu.make_async_copy(small.at[4 + y], small_y.at[y, 1], local.at[1]),
            pltpu.make_async_copy(up.at[y], up_y.at[y, 0], local.at[2]),
            pltpu.make_async_copy(up.at[4 + y], up_y.at[y, 1], local.at[3]),
        ]
        for copy in locals_:
            copy.start()

        lane = lax.broadcasted_iota(jnp.int32, (step, lanes), 1)

        def grads_of(entry_of, factors_of, cot_of, stage, slot):
            for j in range(n):

                def some_rows(r, carry, j=j):
                    at = pl.ds(pl.multiple_of(r * step, step), step)
                    factors = factors_of(j, at)
                    factors = [jnp.broadcast_to(factors[:, s : s + 1], (step, lanes)) for s in range(4)]
                    totals = [jnp.zeros((step, lanes), jnp.float32) for _ in range(4)]
                    for block in range(width // lanes):
                        part = pl.ds(block * lanes, lanes)
                        entry = entry_of(j)[at, part].astype(jnp.float32)
                        mixed = jnp.zeros((step, lanes), jnp.float32)
                        for s in range(4):
                            piece = cot_of(s)[at, part].astype(jnp.float32)
                            mixed = mixed + factors[s] * piece
                            totals[s] = totals[s] + entry * piece
                        stage[j, at, part] = mixed.astype(BF16)
                    packed = jnp.zeros((step, lanes), jnp.float32) if j == 0 else mixes[at, :]
                    for s in range(4):
                        total = jnp.sum(totals[s], axis=1, keepdims=True)
                        packed = jnp.where(lane == j * 4 + s, total, packed)
                    mixes[at, :] = packed
                    return carry

                lax.fori_loop(0, half // step, some_rows, 0)
            turned[slot] = jnp.transpose(mixes[...])[:16]

        def out_rows(k, other, low):
            begin = ((x + k) % 4 * 2 + (1 - zl if other else zl)) * BLOCK + low * half
            return out.at[:, pl.ds(pl.multiple_of(begin, half), half)]

        def owner(k, other):
            return (x + k) % 4 * 2 + (1 - zl if other else zl)

        def keep(src, dst):
            locals_.append(pltpu.make_async_copy(src, dst, local.at[len(locals_)]))
            locals_[-1].start()

        def do_top(other, k):
            slot = other * 4 + k
            source = cot_z if other else cot
            cot_of = (lambda s: source.at[s]) if other else (lambda s: source.at[s, pl.ds(0, half)])
            grads_of(
                lambda j: top.at[other, k, j],
                lambda j, at: tw[other, k * 3 + j, at, :],
                cot_of,
                top_stage.at[other, k],
                slot,
            )
            if k == 0:
                keep(top_stage.at[other, 0], out_rows(0, other, 0))
                keep(turned.at[slot], top_mix.at[owner(0, other)])
            else:
                i = other * 3 + k - 1
                push(top_stage.at[other, k], out_rows(0, other, 0), send, recv, i, peers[k])
                push(turned.at[slot], top_mix.at[owner(0, other)], msend, mrecv, i, peers[k])

        def do_bottom(k, other):
            slot = 8 + k * 2 + other
            cot_of = (lambda s: cot_x.at[k - 1, s]) if k else (lambda s: cot.at[s, pl.ds(half, half)])
            grads_of(
                lambda j: bottom.at[k, other, j],
                lambda j, at: bw[k, other * 3 + j, at, :],
                cot_of,
                bottom_stage.at[k, other],
                slot,
            )
            if other:
                push(bottom_stage.at[k, 1], out_rows(k, 0, 1), send, recv, 6 + k, partner)
                push(turned.at[slot], bottom_mix.at[owner(k, 0)], msend, mrecv, 6 + k, partner)
            else:
                keep(bottom_stage.at[k, 0], out_rows(k, 0, 1))
                keep(turned.at[slot], bottom_mix.at[owner(k, 0)])

        def cot_came(ref, i):
            remote(ref, ref, csend.at[i], crecv.at[i], partner).wait_recv()

        mixes[...] = jnp.zeros_like(mixes)
        loads[0].wait()
        do_top(0, 1)
        do_top(0, 3)
        loads[2].wait()
        do_bottom(0, 1)
        do_top(0, 2)
        for copy in first:
            copy.wait()
        z_slots[z] = x_slots[0] + x_slots[1] + x_slots[2] + x_slots[3]
        second = exchange(z_slots.at[z], z_slots, z, along_z, sends, recvs, 3)
        cot_came(cot_z, 0)
        loads[1].wait()
        for k in (1, 3, 2):
            do_top(1, k)
        for k in (1, 3, 2):
            cot_came(cot_x.at[k - 1], k)
            loads[2 + k].wait()
            do_bottom(k, 1)
        do_top(0, 0)
        do_top(1, 0)
        for k in range(4):
            do_bottom(k, 0)
        for copy in second:
            copy.wait()
        y_slots[y] = z_slots[0] + z_slots[1] + z_slots[2] + z_slots[3]
        third = exchange(y_slots.at[y], y_slots, y, along_y, sends, recvs, 6)
        for copy in third:
            copy.wait()
        c_part[...] = y_slots[0] + y_slots[1] + y_slots[2] + y_slots[3]
        fourth = remote(c_part, c_slot, sends.at[9], recvs.at[9], sibling)
        fourth.start()
        fourth.wait()
        gains_out[...] = c_part[...] + c_slot[...]

        def add_four(parts, places, dst):
            def one(r, carry):
                at = pl.ds(pl.multiple_of(r * step, step), step)
                value = parts[(0,) + places + (at,)].astype(jnp.float32)
                for src in range(1, 4):
                    value = value + parts[(src,) + places + (at,)].astype(jnp.float32)
                dst[places + (at,)] = value.astype(dst.dtype)
                return carry

            lax.fori_loop(0, BLOCK // step, one, 0)

        def small_piece(high, low):
            return small_part.at[high, :, :, pl.ds(pl.multiple_of(low * thin, thin), thin)]

        for copy in sides[:6] + locals_[:2]:
            copy.wait()
        for high in range(2):
            for i in range(4):
                add_four(small_y, (high, i), small_part)
        small_last = []
        for k, (pz, peer) in enumerate(along_z):
            small_last.append(
                remote(small_piece(pz // 2, pz % 2), small_z.at[z], ssend.at[12 + k], srecv.at[12 + k], peer)
            )
            small_last[-1].start()
        keep(small_piece(zh, zl), small_z.at[z])
        for copy in sides[6:] + locals_[2:4]:
            copy.wait()
        for high in range(2):
            add_four(up_y, (high,), up_part)

        def up_piece(high, low):
            return up_part.at[high, :, pl.ds(pl.multiple_of(low * hidden, hidden), hidden)]

        up_last = []
        for k, (pz, peer) in enumerate(along_z):
            up_last.append(
                remote(up_piece(pz // 2, pz % 2), up_z.at[z], ssend.at[15 + k], srecv.at[15 + k], peer)
            )
            up_last[-1].start()
        keep(up_piece(zh, zl), up_z.at[z])
        for copy in small_last + locals_[4:]:
            copy.wait()
        for i in range(4):
            add_four(small_z, (i,), small_out)
        for copy in up_last:
            copy.wait()
        add_four(up_z, (), up_out)
        for copy in copies[:4]:
            copy.wait_send()
        for copy in copies[4:]:
            copy.wait()

    f32 = jnp.float32
    vmem = pltpu.VMEM
    sem = pltpu.SemaphoreType.DMA
    piece = (4, half, width)
    return pl.pallas_call(
        kernel,
        out_shape=[
            shape((n, 8 * BLOCK, width)),
            shape((8, 16, lanes), f32),
            shape((8, 16, lanes), f32),
            shape(gains.shape, f32),
            shape((4, BLOCK, thin), f32),
            shape((BLOCK, hidden), f32),
        ],
        in_specs=[ANY, ANY, VMEM, VMEM, VMEM, VMEM, ANY, ANY],
        out_specs=[ANY, ANY, ANY, VMEM, VMEM, VMEM],
        scratch_shapes=[
            vmem(top_hist.shape, BF16),
            vmem(bottom_hist.shape, BF16),
            vmem(top_hist.shape, BF16),
            vmem(bottom_hist.shape, BF16),
            vmem(piece, BF16),
            vmem((3,) + piece, BF16),
            vmem((BLOCK, lanes), f32),
            vmem((16, 16, lanes), f32),
            vmem((4,) + gains.shape, f32),
            vmem((4,) + gains.shape, f32),
            vmem((4,) + gains.shape, f32),
            vmem(gains.shape, f32),
            vmem(gains.shape, f32),
            vmem((4, 2, 4, BLOCK, cols), BF16),
            vmem((2, 4, BLOCK, cols), BF16),
            vmem((4, 4, BLOCK, thin), BF16),
            vmem((4, 2, BLOCK, 2 * hidden), BF16),
            vmem((2, BLOCK, 2 * hidden), BF16),
            vmem((4, BLOCK, hidden), BF16),
            sem((6,)),
            sem((4,)),
            sem((4,)),
            sem((10,)),
            sem((10,)),
            sem((10,)),
            sem((10,)),
            sem((18,)),
            sem((10,)),
            sem((10,)),
            sem((18,)),
            sem((18,)),
        ],
        compiler_params=pltpu.CompilerParams(
            collective_id=6, has_side_effects=True, vmem_limit_bytes=56 * 2**20
        ),
        name="hand_out",
    )(top_hist, bottom_hist, top_weights, bottom_weights, stream_cot, gains, small, up)


def body(
    history,
    layer_ids,
    mix_weights,
    doc_ids,
    gains,
    w_qkv,
    w_out,
    w_up,
    w_down,
    da_in,
    da_out,
    da_bias,
    out_grad,
    mix_grad_in,
):
    place = lax.axis_index("hist")
    along_x, low_z = place // 2, place % 2
    slots, seq_len, width = history.shape
    small = jnp.concatenate([jnp.transpose(w_qkv, (1, 0, 2)), w_out[None]], axis=0)

    def ring(values, axis):
        return lax.dynamic_slice_in_dim(jnp.concatenate([values, values], axis=axis), along_x, 4, axis)

    def own_first(values, axis):
        return jnp.where(low_z == 0, values, jnp.flip(values, axis=axis))

    def picked(ids):
        return (ids.reshape(-1, 1) == jnp.arange(layers, dtype=jnp.int32)[None, :]).astype(jnp.float32)

    layers = mix_weights.shape[1]
    ids = layer_ids.reshape(4, 2, slots)
    tokens = mix_weights.reshape(4, layers, 4, 2, 2, BLOCK // 2)
    top_ids = ring(lax.dynamic_index_in_dim(ids, low_z, 1, False), 0)
    bottom_ids = own_first(lax.dynamic_index_in_dim(ids, along_x, 0, False), 0)
    top_tokens = own_first(lax.dynamic_index_in_dim(tokens[:, :, :, :, 0], along_x, 2, False), 2)
    bottom_tokens = ring(lax.dynamic_index_in_dim(tokens[:, :, :, :, 1], low_z, 3, False), 2)
    top_weights = jnp.einsum("rl,slot->orts", picked(top_ids), top_tokens, precision=HIGHEST)
    bottom_weights = jnp.einsum("rl,slkt->krts", picked(bottom_ids), bottom_tokens, precision=HIGHEST)
    owned, top_hist, bottom_hist, full_small, full_up = collect(
        history, small, w_up[None], top_weights, bottom_weights
    )
    rows_here = 4 * BLOCK
    cosine, sine_table = rotary_tables(seq_len, ROT)

    def here(table, side=low_z):
        return lax.dynamic_index_in_dim(table.reshape(4, 2, BLOCK, -1), side, 1, False).reshape(rows_here, -1)

    nothing = jnp.zeros_like(sine_table)
    rest = jnp.zeros((seq_len, HD - ROT), jnp.float32)
    tables = jnp.stack(
        [
            here(jnp.concatenate(parts, axis=1))
            for parts in (
                (cosine, cosine, rest + 1.0),
                (-sine_table, nothing, rest),
                (nothing, sine_table, rest),
            )
        ]
    )
    queries, keys, values, other_keys, other_values, gathered, full_down = project(
        owned, gains, full_small, tables, w_down[None]
    )
    places = jnp.stack([jnp.arange(seq_len, dtype=jnp.int32), doc_ids], axis=1)
    query_at, other_at = here(places), here(places, 1 - low_z)
    key_at = jnp.concatenate([query_at.T, other_at.T], axis=0)
    attention = (queries, keys, values, other_keys, other_values, query_at, key_at)
    heads_flat, log_totals = attend(*attention)

    mixers = da_out.shape[0]
    spare = BLOCK - mixers
    (
        block_out,
        mix_next,
        residual_grad,
        heads_cot,
        late_gains,
        side,
        _,
        out_proj_grad,
        up_sum,
        down_sum,
    ) = middle(
        heads_flat,
        full_small,
        full_up,
        full_down,
        owned,
        gains,
        jnp.pad(da_in, ((0, 0), (0, spare))),
        jnp.pad(da_out, ((0, spare), (0, spare))),
        jnp.pad(da_bias, (0, spare))[None],
        out_grad,
        jnp.pad(mix_grad_in, ((0, 0), (0, spare))),
    )
    side = side.reshape(16 * SIDE_ROWS, BLOCK)[:, :mixers]
    da_in_sum, da_out_sum, bias_sum = side[:width], side[width : width + mixers], side[width + 104]

    *grads, key_give, value_give = attend_back(*attention, log_totals, heads_cot)
    stream_cot, gains_local, small_sum, down_sum = inward(
        grads,
        (key_give, value_give),
        full_small,
        gathered,
        out_proj_grad,
        owned,
        residual_grad,
        gains,
        late_gains,
        tables,
        down_sum.reshape(2, 4, BLOCK, -1),
    )
    history_grad, top_mix, bottom_mix, gains_sum, small_sum, up_sum = hand_out(
        top_hist,
        bottom_hist,
        top_weights,
        bottom_weights,
        stream_cot,
        gains_local,
        small_sum,
        up_sum.reshape(8, BLOCK, -1),
    )
    half = BLOCK // 2
    mix_out = jnp.concatenate([top_mix[:, : 4 * slots, :half], bottom_mix[:, : 4 * slots, :half]], axis=2)
    mix_grad = jnp.transpose(mix_out.reshape(8, slots, 4, BLOCK), (2, 1, 0, 3)).reshape(4, slots, seq_len)
    return (
        block_out,
        mix_next[:, :mixers],
        history_grad,
        mix_grad,
        gains_sum[: gains.shape[0]],
        jnp.transpose(small_sum[:3], (1, 0, 2)),
        small_sum[3],
        up_sum,
        down_sum,
        da_in_sum,
        da_out_sum,
        bias_sum,
    )


def solution(mesh):
    return jax.shard_map(
        body,
        mesh=mesh,
        in_specs=(
            P("hist", "tok", None),
            P(),
            P(None, None, "tok"),
            P("tok"),
            P(),
            P("tok", None, "hist"),
            P("tok", "hist"),
            P("tok", "hist"),
            P("tok", "hist"),
            P(),
            P(),
            P(),
            P(("tok", "hist"), None),
            P(("tok", "hist"), None),
        ),
        out_specs=(
            P(("tok", "hist"), None),
            P(("tok", "hist"), None),
            P("hist", "tok", None),
            P(None, "hist", "tok"),
            P(),
            P("tok", None, "hist"),
            P("tok", "hist"),
            P("tok", "hist"),
            P("tok", "hist"),
            P(),
            P(),
            P(),
        ),
        check_vma=False,
    )
```

```python
import jax
import jax.numpy as jnp
import numpy as np
from jax import lax
from jax.experimental import pallas as pl
from jax.experimental.pallas import tpu as pltpu
from jax.sharding import PartitionSpec as P

HD = 128
ROT = 32


EPSILON = 1e-05
NEGATIVE = -1e30
HIGHEST = lax.Precision.HIGHEST


def norm_rows(values):
    row_mean = jnp.mean(values, axis=-1, keepdims=True)
    centered = values - row_mean
    inv_std = lax.rsqrt(jnp.mean(centered * centered, axis=-1, keepdims=True) + EPSILON)
    return (centered * inv_std, inv_std)


def norm_back(grad_unit, norm_unit, inv_std):
    return inv_std * (
        grad_unit
        - jnp.mean(grad_unit, axis=-1, keepdims=True)
        - norm_unit * jnp.mean(grad_unit * norm_unit, axis=-1, keepdims=True)
    )


def gelu_slope(values):
    return (
        0.5 * (1.0 + lax.erf(values * 0.7071067811865476))
        + values * jnp.exp(-0.5 * values * values) * 0.3989422804014327
    )


def rotary_tables(length, rotated):
    half_rot = rotated // 2
    frequency = 10000.0 ** (-2.0 * jnp.arange(half_rot, dtype=jnp.float32) / rotated)
    angles = jnp.arange(length, dtype=jnp.float32)[:, None] * frequency[None, :]
    return (jnp.cos(angles), jnp.sin(angles))


def rotate(values, cosine, sine_table, direction):
    half_rot = cosine.shape[1]
    first_half = values[..., :half_rot]
    second_half = values[..., half_rot : 2 * half_rot]
    cos_part = cosine[:, None, :]
    sin_part = direction * sine_table[:, None, :]
    return jnp.concatenate(
        [
            first_half * cos_part - second_half * sin_part,
            second_half * cos_part + first_half * sin_part,
            values[..., 2 * half_rot :],
        ],
        axis=-1,
    )


def contract(left_side, right_side, left_dim, right_dim):
    return lax.dot_general(
        left_side,
        right_side,
        (((left_dim,), (right_dim,)), ((), ())),
        preferred_element_type=jnp.float32,
    )


MESH = pl.DeviceIdType.MESH
ANY = pl.BlockSpec(memory_space=pl.ANY)
HBM = pl.BlockSpec(memory_space=pltpu.HBM)
BF16 = jnp.bfloat16
BLOCK = 128
VMEM_LIMIT = 62 * 2**20


def coords():
    hist = lax.axis_index("hist")
    tok = lax.axis_index("tok")
    return hist // 2, hist % 2, tok // 8, (tok // 2) % 4, tok % 2


def device(x, zl, zh, y, c):
    return (x * 2 + zl, zh * 8 + y * 2 + c)


def greet(peers):
    barrier = pltpu.get_barrier_semaphore()
    for peer in peers:
        pl.semaphore_signal(barrier, inc=1, device_id=peer, device_id_type=MESH)
    pl.semaphore_wait(barrier, len(peers))


def remote(src, dst, send_sem, recv_sem, peer):
    return pltpu.make_async_remote_copy(
        src_ref=src,
        dst_ref=dst,
        send_sem=send_sem,
        recv_sem=recv_sem,
        device_id=peer,
        device_id_type=MESH,
    )


def comm_call(kernel, out_shapes, sems, collective_id, name, *args):
    return pl.pallas_call(
        kernel,
        out_shape=out_shapes,
        in_specs=[ANY] * len(args),
        out_specs=[ANY] * len(out_shapes),
        scratch_shapes=[
            pltpu.SemaphoreType.DMA((sems,)),
            pltpu.SemaphoreType.DMA((sems,)),
            pltpu.SemaphoreType.DMA((4,)),
        ],
        compiler_params=pltpu.CompilerParams(collective_id=collective_id, has_side_effects=True),
        name=name,
    )(*args)


def shape(dims, dtype=BF16):
    return jax.ShapeDtypeStruct(dims, dtype)


def x_peers(x, zl, zh, y, c):
    return [((x + k) % 4, device((x + k) % 4, zl, zh, y, c)) for k in (1, 3, 2)]


def z_peers(x, zl, zh, y, c):
    places = [(zh * 2 + zl + k) % 4 for k in (1, 3, 2)]
    return [(place, device(x, place % 2, place // 2, y, c)) for place in places]


def y_peers(x, zl, zh, y, c):
    return [((y + k) % 4, device(x, zl, zh, (y + k) % 4, c)) for k in (1, 3, 2)]


VMEM = pl.BlockSpec(memory_space=pltpu.VMEM)
SIDE_ROWS = 112
MIXERS = 104


def exchange(src, slots, mine, peers, send, recv, first):
    copies = []
    for k, (place, peer) in enumerate(peers):
        part = src(place) if callable(src) else src
        copies.append(remote(part, slots.at[mine], send.at[first + k], recv.at[first + k], peer))
        copies[-1].start()
    return copies


def weight_gather(srcs, fulls, place, send, recv, base):
    x, zl, zh, y, c = place
    partner = device(x, 1 - zl, zh, y, c)
    across = device(x, 1 - zl, 1 - zh, y, c)
    sibling = device(x, zl, zh, y, 1 - c)
    rows_of = [device(x, zl, zh, (y + k) % 4, c) for k in (1, 3, 2)]
    z_of = [(zl, zh), (1 - zl, zh), (1 - zl, 1 - zh), (zl, 1 - zh)]
    many = len(srcs)
    started = []

    def view(ref, b_zl, b_zh, b_y, b_c):
        wide = ref.shape[2] // 2
        row = (b_zh * 8 + b_y * 2 + b_c) * BLOCK
        return ref.at[
            :, pl.ds(pl.multiple_of(row, BLOCK), BLOCK), pl.ds(pl.multiple_of(b_zl * wide, wide), wide)
        ]

    def sem(zi, k, sib, a):
        return base + ((zi * 4 + k) * 2 + sib) * many + a

    def refs(zi, k, sib=0):
        by = (y + 4 - (0, 1, 3, 2)[k]) % 4
        return [view(full, *z_of[zi], by, 1 - c if sib else c) for full in fulls]

    def push(src, dst, i, peer):
        started.append(remote(src, dst, send.at[i], recv.at[i], peer))
        started[-1].start()

    def wait_block(zi, k, sib=0):
        for a, ref in enumerate(refs(zi, k, sib)):
            i = sem(zi, k, sib, a)
            remote(ref, ref, send.at[i], recv.at[i], sibling).wait_recv()

    def spread(zi, blocks):
        for a, src in enumerate(blocks):
            dst = view(fulls[a], *z_of[zi], y, c)
            for k, peer in enumerate(rows_of):
                push(src, dst, sem(zi, k + 1, 0, a), peer)
            push(src, dst, sem(zi, 0, 1, a), sibling)

    own = [view(full, zl, zh, y, c) for full in fulls]

    def start(local, first):
        for a, src in enumerate(srcs):
            push(src, own[a], sem(1, 0, 0, a), partner)
        for a, src in enumerate(srcs):
            push(src, own[a], sem(2, 0, 0, a), across)
        kept = [pltpu.make_async_copy(src, own[a], local.at[first + a]) for a, src in enumerate(srcs)]
        for copy in kept:
            copy.start()
        spread(0, srcs)
        return kept

    def relay_z():
        wait_block(1, 0)
        for a, ref in enumerate(refs(1, 0)):
            push(ref, ref, sem(3, 0, 0, a), across)
        spread(1, refs(1, 0))
        wait_block(2, 0)
        spread(2, refs(2, 0))
        wait_block(3, 0)
        spread(3, refs(3, 0))

    def relay_y(zi):
        for k in range(1, 4):
            wait_block(zi, k)
            for a, ref in enumerate(refs(zi, k)):
                push(ref, ref, sem(zi, k, 1, a), sibling)

    def finish():
        for zi in range(4):
            for k in range(4):
                wait_block(zi, k, 1)
        for copy in started:
            copy.wait_send()

    greeted = [partner, across, sibling] + rows_of
    return greeted, start, relay_z, relay_y, finish


def collect(history, small, up, layer_ids, mix_weights):
    slots, _, width = history.shape
    layers = mix_weights.shape[1]
    half = BLOCK // 2
    step = 16
    lanes = 128

    def kernel(
        hist, wa, wb, ids, given, streams, top_out, bottom_out, full_a, full_b, tw, bw,
        top, bottom, acc, far_part, hop, part_x, got_x, part_z, got_z,
        wsend, wrecv, send, recv, local, store,
    ):
        here = coords()
        x, zl, zh, y, c = here
        partner = device(x, 1 - zl, zh, y, c)
        peers = {k: device((x + k) % 4, zl, zh, y, c) for k in (1, 2, 3)}
        greeted, start, relay_z, relay_y, finish = weight_gather((wa, wb), (full_a, full_b), here, wsend, wrecv, 0)
        greet(greeted + [peers[1], peers[2], peers[3]])

        def rows(k, other, low):
            begin = ((x + k) % 4 * 2 + (1 - zl if other else zl)) * BLOCK + low * half
            return hist.at[:, pl.ds(pl.multiple_of(begin, half), half)]

        copies = []

        def push(src, dst, i, peer):
            copies.append(remote(src, dst, send.at[i], recv.at[i], peer))
            copies[-1].start()

        def came(ref, i):
            remote(ref, ref, send.at[i], recv.at[i], partner).wait_recv()

        own = []
        for other in range(2):
            own.append(pltpu.make_async_copy(rows(0, other, 0), top.at[other, 0], local.at[other]))
        for k in range(4):
            own.append(pltpu.make_async_copy(rows(k, 0, 1), bottom.at[k, 0], local.at[2 + k]))
        for copy in own:
            copy.start()
        kept = start(local, 6)
        for k in (2, 1, 3, 0):
            push(rows(k, 1, 1), bottom.at[k, 1], k, partner)
        for other in (1, 0):
            for k in (1, 3, 2):
                push(rows(k, other, 0), top.at[other, 4 - k], 4 + 3 * other + 3 - k, peers[k])

        def columns_of(slots_here, owner, low, into):
            cols = pl.ds(pl.multiple_of(owner * BLOCK, BLOCK), BLOCK)
            column = lax.broadcasted_iota(jnp.int32, (lanes, layers), 0)
            layer = lax.broadcasted_iota(jnp.int32, (lanes, layers), 1)
            wanted = jnp.full((lanes, layers), -1, jnp.int32)
            for i, slot in enumerate(slots_here):
                wanted = jnp.where(column // 4 == i, ids[slot], wanted)
            total = jnp.zeros((lanes, BLOCK), jnp.float32)
            for s in range(4):
                pick = jnp.where((layer == wanted) & (column % 4 == s), 1.0, 0.0)
                total = total + lax.dot_general(
                    pick,
                    given[s, :, cols],
                    (((1,), (0,)), ((), ())),
                    precision=HIGHEST,
                    preferred_element_type=jnp.float32,
                )
            into[...] = jnp.transpose(total)[low * half : (low + 1) * half]

        for other in range(2):
            owner = x * 2 + (1 - zl if other else zl)
            columns_of([(x + k) % 4 * 6 + zl * 3 + j for k in range(4) for j in range(3)], owner, 0, tw.at[other])
        for k in range(4):
            wanted_slots = [x * 6 + (1 - zl if r else zl) * 3 + j for r in range(2) for j in range(3)]
            columns_of(wanted_slots, (x + k) % 4 * 2 + zl, 1, bw.at[k])

        def mix(entries, factors_of, groups, into, offset):
            def some_rows(r, carry):
                at = pl.ds(pl.multiple_of(r * step, step), step)
                there = pl.ds(pl.multiple_of(offset + r * step, step), step)
                for g in range(groups):
                    factors = [
                        [
                            jnp.broadcast_to(factors_of(at)[:, i * 4 + s : i * 4 + s + 1], (step, lanes))
                            for s in range(4)
                        ]
                        for i in range(g * 3, g * 3 + 3)
                    ]

                    def some_cols(b, inner, g=g, factors=factors):
                        cols = pl.ds(pl.multiple_of(b * lanes, lanes), lanes)
                        entry = [entries(g, e)[at, cols].astype(jnp.float32) for e in range(3)]
                        for s in range(4):
                            value = factors[0][s] * entry[0] + factors[1][s] * entry[1] + factors[2][s] * entry[2]
                            into[s, there, cols] = value if g == 0 else into[s, there, cols] + value
                        return inner

                    lax.fori_loop(0, width // lanes, some_cols, 0, unroll=4)
                return carry

            lax.fori_loop(0, half // step, some_rows, 0)

        def mix_top(other, into, offset):
            mix(lambda g, e: top.at[other, g, e], lambda at: tw[other, at, :], 4, into, offset)

        def mix_bottom(k, into, offset):
            mix(lambda g, e: bottom.at[k, g, e], lambda at: bw[k, at, :], 2, into, offset)

        stores = []

        def keep(src, dst):
            stores.append(pltpu.make_async_copy(src, dst, store.at[len(stores)]))
            stores[-1].start()

        def bottom_sums(k):
            came(bottom.at[k, 1], k)
            own[2 + k].wait()
            keep(bottom.at[k], bottom_out.at[k])
            if k == 0:
                mix_bottom(0, streams, half)
                return
            mix_bottom(k, acc, 0)
            if k == 2:
                far_part[...] = acc[...].astype(BF16)
                push(far_part.at[:, pl.ds(0, half // 2)], hop.at[0], 14, peers[1])
                push(far_part.at[:, pl.ds(half // 2, half // 2)], hop.at[1], 15, peers[3])
                return
            side = 0 if k == 1 else 1
            came(hop.at[side], 14 + side)
            merged = pl.ds(side * (half // 2), half // 2)
            for s in range(4):
                acc[s, merged] = acc[s, merged] + hop[side, s].astype(jnp.float32)
            part_x[side] = acc[...].astype(BF16)
            push(part_x.at[side], got_x.at[side], 10 + side, peers[k])

        relay_z()
        bottom_sums(2)
        own[1].wait()
        for k in (1, 2, 3):
            came(top.at[1, k], 4 + 3 + k - 1)
        keep(top.at[1], top_out.at[1])
        mix_top(1, acc, 0)
        part_z[...] = acc[...].astype(BF16)
        push(part_z, got_z, 13, partner)
        bottom_sums(1)
        relay_y(0)
        bottom_sums(3)
        own[0].wait()
        for k in (1, 2, 3):
            came(top.at[0, k], 4 + k - 1)
        keep(top.at[0], top_out.at[0])
        mix_top(0, streams, 0)
        relay_y(1)
        bottom_sums(0)
        relay_y(2)
        relay_y(3)
        came(got_z, 13)

        def add(r, carry, offset, parts):
            at = pl.ds(pl.multiple_of(r * step, step), step)
            there = pl.ds(pl.multiple_of(offset + r * step, step), step)
            for s in range(4):
                value = streams[s, there, :]
                for part in parts:
                    value = value + part(s, at)
                streams[s, there, :] = value
            return carry

        def add_all(offset, parts):
            lax.fori_loop(0, half // step, lambda r, carry: add(r, carry, offset, parts), 0)

        add_all(0, [lambda s, at: got_z[s, at, :].astype(jnp.float32)])
        for side in range(2):
            came(got_x.at[side], 10 + side)
        add_all(half, [lambda s, at, k=k: got_x[k, s, at, :].astype(jnp.float32) for k in range(2)])
        finish()
        for copy in kept + stores:
            copy.wait()
        for copy in copies:
            copy.wait_send()

    n_a, rows_a, cols_a = small.shape
    n_b, rows_b, cols_b = up.shape
    vmem = pltpu.VMEM
    sem = pltpu.SemaphoreType.DMA
    top_shape, bottom_shape = (2, 4, slots, half, width), (4, 2, slots, half, width)
    piece = (4, half, width)
    return pl.pallas_call(
        kernel,
        out_shape=[
            shape((4, BLOCK, width), jnp.float32),
            shape(top_shape),
            shape(bottom_shape),
            shape((n_a, rows_a * 16, cols_a * 2)),
            shape((n_b, rows_b * 16, cols_b * 2)),
            shape((2, half, lanes), jnp.float32),
            shape((4, half, lanes), jnp.float32),
        ],
        in_specs=[ANY, ANY, ANY, pl.BlockSpec(memory_space=pltpu.SMEM), VMEM],
        out_specs=[VMEM, HBM, HBM, HBM, HBM, VMEM, VMEM],
        scratch_shapes=[
            vmem(top_shape, BF16),
            vmem(bottom_shape, BF16),
            vmem(piece, jnp.float32),
            vmem(piece, BF16),
            vmem((2, 4, half // 2, width), BF16),
            vmem((2,) + piece, BF16),
            vmem((2,) + piece, BF16),
            vmem(piece, BF16),
            vmem(piece, BF16),
            sem((64,)),
            sem((64,)),
            sem((16,)),
            sem((16,)),
            sem((8,)),
            sem((6,)),
        ],
        compiler_params=pltpu.CompilerParams(
            collective_id=1, has_side_effects=True, vmem_limit_bytes=VMEM_LIMIT
        ),
        name="collect",
    )(history, small, up, layer_ids, mix_weights)


def dot_nt(left, right):
    return lax.dot_general(left, right, (((1,), (1,)), ((), ())), preferred_element_type=jnp.float32)


def dot_nn(left, right):
    return lax.dot_general(left, right, (((1,), (0,)), ((), ())), preferred_element_type=jnp.float32)


def dot_tn(left, right):
    return lax.dot_general(left, right, (((0,), (0,)), ((), ())), preferred_element_type=jnp.float32)


def token_places(docs, zl):
    rows = docs[...].astype(jnp.float32)
    cols = jnp.transpose(rows)
    first = zl == 0
    queries = [[], []]
    keys = [[], [], [], []]
    down = lax.broadcasted_iota(jnp.int32, (BLOCK, 1), 0)
    along = lax.broadcasted_iota(jnp.int32, (1, BLOCK), 1)
    for p in range(4):
        even, odd = cols[:, 2 * p : 2 * p + 1], cols[:, 2 * p + 1 : 2 * p + 2]
        queries[0].append((down + (2 * p + zl) * BLOCK).astype(jnp.float32))
        queries[1].append(jnp.where(first, even, odd))
        even, odd = rows[2 * p : 2 * p + 1], rows[2 * p + 1 : 2 * p + 2]
        for side, low in ((0, zl), (1, 1 - zl)):
            keys[2 * side].append((along + (2 * p + low) * BLOCK).astype(jnp.float32))
        keys[1].append(jnp.where(first, even, odd))
        keys[3].append(jnp.where(first, odd, even))
    return (
        [jnp.concatenate(part, axis=0) for part in queries],
        [jnp.concatenate(part, axis=1) for part in keys],
    )


def allowed_keys(query_pos, query_doc, keys, side):
    return (keys[2 * side] <= query_pos) & (keys[2 * side + 1] == query_doc)


def attend(q, k, v, ok, ov, places, keys, out, lse):
    rows, cols = q.shape
    scale = HD ** (-0.5)
    tall = 256

    def one_head(h, carry):
        head = pl.ds(pl.multiple_of(h * HD, HD), HD)
        for r in range(rows // tall):
            at = pl.ds(r * tall, tall)
            query_pos, query_doc = places[at, 0:1], places[at, 1:2]
            scores = []
            for side, key in enumerate((k, ok)):
                allowed = allowed_keys(query_pos, query_doc, keys, side)
                scores.append(jnp.where(allowed, dot_nt(q[at, head], key[:, head]) * scale, NEGATIVE))
            top = jnp.maximum(
                jnp.max(scores[0], axis=1, keepdims=True), jnp.max(scores[1], axis=1, keepdims=True)
            )
            shifted = [jnp.exp(part - top) for part in scores]
            total = jnp.sum(shifted[0], axis=1, keepdims=True) + jnp.sum(shifted[1], axis=1, keepdims=True)
            share = 1.0 / total
            result = dot_nn((shifted[0] * share).astype(BF16), v[:, head])
            result = result + dot_nn((shifted[1] * share).astype(BF16), ov[:, head])
            out[at, head] = result.astype(BF16)
            lane = lax.broadcasted_iota(jnp.int32, (tall, HD), 1)
            lse[at, :] = jnp.where(lane == h, top + jnp.log(total), lse[at, :])
        return carry

    lax.fori_loop(0, cols // HD, one_head, 0)


def attend_back(q, k, v, ok, ov, places, keys, lse, cot, dq, dk, dv, dok, dov, key_sum, value_sum, finish):
    rows, cols = q.shape
    scale = HD ** (-0.5)
    tall = 256

    def one_head(h, carry):
        head = pl.ds(pl.multiple_of(h * HD, HD), HD)
        for r in range(rows // tall):
            at = pl.ds(r * tall, tall)
            query_pos, query_doc = places[at, 0:1], places[at, 1:2]
            lane = lax.broadcasted_iota(jnp.int32, (tall, HD), 1)
            log_total = jnp.sum(jnp.where(lane == h, lse[at, :], 0.0), axis=1, keepdims=True)
            probs, prob_grads = [], []
            for side, (key, value) in enumerate(((k, v), (ok, ov))):
                allowed = allowed_keys(query_pos, query_doc, keys, side)
                scores = jnp.where(allowed, dot_nt(q[at, head], key[:, head]) * scale, NEGATIVE)
                probs.append(jnp.exp(scores - log_total))
                prob_grads.append(dot_nt(cot[at, head], value[:, head]))
            row_dot = sum(jnp.sum(p * g, axis=1, keepdims=True) for p, g in zip(probs, prob_grads))
            query_grad = jnp.zeros((tall, HD), jnp.float32)
            for side, (p, g) in enumerate(zip(probs, prob_grads)):
                score_cot = (p * (g - row_dot)).astype(BF16)
                key = (k, ok)[side]
                query_grad = query_grad + dot_nn(score_cot, key[:, head])
                key_part = dot_tn(score_cot, q[at, head])
                value_part = dot_tn(p.astype(BF16), cot[at, head])
                if r == 0:
                    key_sum[side] = key_part
                    value_sum[side] = value_part
                else:
                    key_sum[side] += key_part
                    value_sum[side] += value_part
            dq[at, head] = query_grad * scale
        dk[:, head] = key_sum[0] * scale
        dv[:, head] = value_sum[0]
        dok[:, head] = (key_sum[1] * scale).astype(BF16)
        dov[:, head] = value_sum[1].astype(BF16)
        finish(h)
        return carry

    lax.fori_loop(0, cols // HD, one_head, 0)


def set_places(docs, zl, places):
    queries, keys = token_places(docs, zl)
    lane = lax.broadcasted_iota(jnp.int32, places.shape, 1)
    places[...] = jnp.where(lane == 0, queries[0], jnp.where(lane == 1, queries[1], 0.0))
    return keys


def erf(value):
    value = jnp.clip(value, -4.0, 4.0)
    square = value * value
    top = jnp.full_like(value, -2.72614225801306e-10)
    for factor in (
        2.77068142495902e-08,
        -2.10102402082508e-06,
        -5.69250639462346e-05,
        -7.34990630326855e-04,
        -2.95459980854025e-03,
        -1.60960333262415e-02,
    ):
        top = top * square + factor
    bottom = jnp.full_like(value, -1.45660718464996e-05)
    for factor in (-2.13374055278905e-04, -1.68282697438203e-03, -7.37332916720468e-03, -1.42647390514189e-02):
        bottom = bottom * square + factor
    return value * top / bottom


def gelu_both(value):
    share = 0.5 * (1.0 + erf(value * 0.7071067811865476))
    bell = jnp.exp(-0.5 * value * value) * 0.3989422804014327
    return value * share, share + value * bell


def row_mean(value):
    return jnp.mean(value, axis=1, keepdims=True)


def middle(heads, small, up, down, stream, gains, da_in, da_out, da_bias, out_grad, mix_cot_in):
    rows_all, head_cols = heads.shape
    width, hidden = up.shape[1:]
    step = 16
    half = BLOCK // 2
    tile = 2 * BLOCK
    tiles = width // tile
    mixers = da_out.shape[0]

    def kernel(
        heads, small, up, down, stream_in, gains, in_given, net_given, bias_given, out_grad, mix_given,
        block_out, mix_next, residual_grad, heads_cot, gain_grads, other, out_proj_grad, up_sum, down_sum,
        in_grad, net_grad, bias_grad,
        w_out, w_up, w_down, mid_all, active, slope, cot_all, up_cot, attn_cot,
        part, got1, got3, own, residual, unit, total, flat, aux, inv, grad_stage, sums,
        y_slots, z_part, z_slots, c_part, c_slot, x_slots, result, side_sum,
        stream, da_in, padded, load, send, recv, gsend, grecv, gkeep, sends, recvs, dload,
    ):
        x, zl, zh, y, c = coords()
        z = zh * 2 + zl
        along_z, along_y = z_peers(x, zl, zh, y, c), y_peers(x, zl, zh, y, c)
        sibling = device(x, zl, zh, y, 1 - c)
        steps = (1, 3, 2)
        places = {k: (x + k) % 4 for k in steps}
        peers = {k: device(places[k], zl, zh, y, c) for k in steps}
        right, left, far = places[1], places[3], places[2]
        loads = [
            pltpu.make_async_copy(small.at[3], w_out, load.at[0]),
            pltpu.make_async_copy(up.at[0], w_up, load.at[1]),
            pltpu.make_async_copy(down.at[0], w_down, load.at[2]),
            pltpu.make_async_copy(stream_in.at[3], stream, load.at[3]),
        ]
        for copy in loads:
            copy.start()
        greet([peers[k] for k in steps] + [peer for _, peer in along_z + along_y] + [sibling])

        def block(place):
            return pl.ds(pl.multiple_of(place * BLOCK, BLOCK), BLOCK)

        def chunks(work, place=0):
            def one(r, carry):
                begin = r * step
                work(
                    pl.ds(pl.multiple_of(begin, step), step),
                    pl.ds(pl.multiple_of(place * BLOCK + begin, step), step),
                )
                return carry

            lax.fori_loop(0, BLOCK // step, one, 0)

        sent = []
        given = ({}, {}, {})

        def arrived(stage, got):
            for k in steps:
                i = stage * 3 + k - 1
                remote(got.at[k - 1], got.at[k - 1], send.at[i], recv.at[i], sibling).wait_recv()

        def push(src, dst, i, peer):
            copy = remote(src, dst, send.at[i], recv.at[i], peer)
            copy.start()
            sent.append(copy)
            return copy

        def give_part(stage, k, got, product):
            if k == 0:
                own[...] = product
                return
            slot = stage % 2
            if stage == 2:
                given[0][k].wait_send()
            part[slot, k - 1] = product.astype(BF16)
            given[stage][k] = push(part.at[slot, k - 1], got.at[k - 1], stage * 3 + k - 1, peers[k])

        def spread(buf, base):
            def piece(place, top):
                begin = pl.multiple_of(place * BLOCK + (0 if top else half), half)
                return buf.at[pl.ds(begin, half)]

            first = [
                push(piece(x, True), piece(x, True), base, peers[1]),
                push(piece(x, False), piece(x, False), base + 2, peers[3]),
                push(piece(x, False), piece(x, False), base + 1, peers[1]),
                push(piece(x, True), piece(x, True), base + 3, peers[3]),
            ]

            def forward():
                first[0].wait_recv()
                one = push(piece(left, True), piece(left, True), base + 4, peers[1])
                first[1].wait_recv()
                two = push(piece(right, False), piece(right, False), base + 5, peers[3])
                return one, two

            return first, forward

        def gathered(buf, base, work):
            first, forward = spread(buf, base)
            work(0, x)
            one, two = forward()
            first[2].wait_recv()
            work(3, left)
            first[3].wait_recv()
            work(1, right)
            one.wait_recv()
            two.wait_recv()
            work(2, far)

        loads[0].wait()
        for k in (2, 1, 3, 0):
            place = x if k == 0 else places[k]
            give_part(0, k, got1, dot_nt(heads[block(place), :], w_out[...]))
        aux[...] = jnp.zeros_like(aux)
        aux[:mixers, :] = in_given[...].astype(jnp.float32)
        da_in[...] = aux[...].astype(BF16)
        padded[...] = jnp.zeros_like(padded)
        padded[0, :mixers, :mixers] = net_given[...].astype(jnp.float32)
        padded[1, :1, :mixers] = bias_given[...]
        padded[2, :mixers, :] = mix_given[...]
        padded[2] = jnp.transpose(padded[2])
        loads[3].wait()
        arrived(0, got1)

        def to_mid(at, there):
            value = stream[at, :] + own[at, :]
            for k in range(3):
                value = value + got1[k, at, :].astype(jnp.float32)
            residual[at, :] = value
            centered = value - row_mean(value)
            scale = lax.rsqrt(row_mean(centered * centered) + EPSILON)
            inv[at, :BLOCK] = jnp.broadcast_to(scale, (step, BLOCK))
            normed = centered * scale
            unit[at, :] = normed
            mid_all[there, :] = (normed * gains[3:4, :]).astype(BF16)

        chunks(to_mid, x)

        waited = []

        def feed(k, place):
            if not waited:
                loads[1].wait()
            total[...] = dot_nn(mid_all[block(place), :], w_up[...])

            def bend(at, there):
                value = total[at, :]
                active[there, :] = (0.5 * value * (1.0 + erf(value * 0.7071067811865476))).astype(BF16)
                slope[there, :] = value

            chunks(bend, place)
            if not waited:
                loads[2].wait()
                waited.append(True)
            give_part(1, k, got3, dot_nt(active[block(place), :], w_down[...]))

        gathered(mid_all, 9, feed)

        def bend_more(r, carry):
            at = pl.ds(pl.multiple_of(r * step, step), step)
            slope[at, :] = gelu_both(slope[at, :])[1]
            return carry

        lax.fori_loop(0, rows_all // step, bend_more, 0)
        arrived(1, got3)

        def to_out(at, _):
            value = residual[at, :] + own[at, :]
            for k in range(3):
                value = value + got3[k, at, :].astype(jnp.float32)
            block_out[at, :] = value.astype(BF16)
            scale = lax.rsqrt(row_mean(value * value) + EPSILON)
            inv[at, BLOCK:] = jnp.broadcast_to(scale, (step, BLOCK))
            residual[at, :] = value * scale
            flat[at, :] = (value * scale * gains[4:5, :]).astype(BF16)

        chunks(to_out)
        da_out = padded[0].astype(BF16)
        inner_act, inner_slope = gelu_both(dot_nt(flat[...], da_in[...]))
        inner_act = inner_act.astype(BF16)
        mix_next[...] = jnp.transpose(dot_nn(inner_act, da_out) + padded[1, :1, :])[:mixers]
        mix_cot = padded[2].astype(BF16)
        inner_cot = (dot_nt(mix_cot, da_out) * inner_slope).astype(BF16)
        aux[...] = dot_nn(inner_cot, da_in[...])
        sums[...] = jnp.zeros_like(sums)

        def to_cot(at, there):
            rms_unit = residual[at, :]
            grad = aux[at, :]
            product = grad * rms_unit
            sums[0] += product[:8] + product[8:]
            scaled = grad * gains[4:5, :]
            scale = inv[at, BLOCK : BLOCK + 1]
            value = out_grad[at, :].astype(jnp.float32) + scale * (
                scaled - rms_unit * row_mean(scaled * rms_unit)
            )
            residual[at, :] = value
            cot_all[there, :] = value.astype(BF16)

        chunks(to_cot, x)

        def small_grads():
            aux[...] = dot_tn(inner_cot, flat[...])
            net = dot_tn(inner_act, mix_cot)
            bias = jnp.sum(padded[2], axis=0, keepdims=True)
            row = lax.broadcasted_iota(jnp.int32, (8, BLOCK), 0)
            for i in range(16):
                place = (i // 4, i % 4)
                result[place + (slice(0, MIXERS),)] = aux[:MIXERS, i * BLOCK : (i + 1) * BLOCK]
                if i < MIXERS // 8:
                    tail = net[i * 8 : (i + 1) * 8]
                else:
                    tail = jnp.where(row == 0, bias, 0.0)
                result[place + (slice(MIXERS, SIDE_ROWS),)] = tail

        side = {}

        def side_start():
            small_grads()
            side[0] = exchange(lambda py: result.at[py], y_slots, y, along_y, sends, recvs, 0)
            y_slots[y] = result[y]

        def side_z():
            for copy in side[0]:
                copy.wait()
            z_part[...] = y_slots[0] + y_slots[1] + y_slots[2] + y_slots[3]
            side[1] = exchange(lambda pz: z_part.at[pz], z_slots, z, along_z, sends, recvs, 3)
            z_slots[z] = z_part[z]

        def side_core():
            for copy in side[1]:
                copy.wait()
            c_part[...] = z_slots[0] + z_slots[1] + z_slots[2] + z_slots[3]
            side[2] = remote(c_part, c_slot, sends.at[6], recvs.at[6], sibling)
            side[2].start()

        def side_x():
            side[2].wait()
            x_slots[x] = c_part[...] + c_slot[...]
            along_x = [(places[k], peers[k]) for k in steps]
            side[3] = exchange(x_slots.at[x], x_slots, x, along_x, sends, recvs, 7)

        def side_up_z():
            for copy in side[3]:
                copy.wait()
            side_sum[y, z] = x_slots[0] + x_slots[1] + x_slots[2] + x_slots[3]
            side[4] = exchange(side_sum.at[y, z], side_sum.at[y], z, along_z, sends, recvs, 10)

        def side_up_y():
            for copy in side[4]:
                copy.wait()
            side[5] = exchange(side_sum.at[y], side_sum, y, along_y, sends, recvs, 13)

        def feed_back(k, place):
            total[...] = dot_nn(cot_all[block(place), :], w_down[...])

            def bend(at, there):
                up_cot[there, :] = (total[at, :] * slope[there, :].astype(jnp.float32)).astype(BF16)

            chunks(bend, place)
            give_part(2, k, got1, dot_nt(up_cot[block(place), :], w_up[...]))

        first, forward = spread(cot_all, 15)
        side_start()
        feed_back(0, x)
        one, two = forward()
        first[2].wait_recv()
        feed_back(3, left)
        first[3].wait_recv()
        feed_back(1, right)
        side_z()
        one.wait_recv()
        two.wait_recv()
        feed_back(2, far)
        side_core()

        def weight_grad(which, left_side, right_side):
            def copies(m):
                slot = lax.rem(m, 2)
                mine = grad_stage.at[slot, pl.ds(pl.multiple_of(c * BLOCK, BLOCK), BLOCK)]
                theirs = grad_stage.at[slot, pl.ds(pl.multiple_of((1 - c) * BLOCK, BLOCK), BLOCK)]
                i = which * tiles + m
                stays = (w_up, w_down)[which].at[pl.ds(pl.multiple_of(m * BLOCK, BLOCK), BLOCK)]
                return (
                    pltpu.make_async_copy(mine, stays, gkeep.at[slot]),
                    remote(theirs, other.at[which, m], gsend.at[i], grecv.at[i], sibling),
                )

            def finish(m):
                stay, go = copies(m)
                stay.wait()
                go.wait_send()

            def one(m, carry):
                @pl.when(m >= 2)
                def _():
                    finish(m - 2)

                cols = pl.ds(pl.multiple_of(m * tile, tile), tile)
                grad_stage[lax.rem(m, 2)] = dot_tn(left_side[:, cols], right_side[...]).astype(BF16)
                for copy in copies(m):
                    copy.start()
                return carry

            lax.fori_loop(0, tiles, one, 0)
            finish(tiles - 2)
            finish(tiles - 1)

        def other_came(which):
            def one(m, carry):
                i = which * tiles + m
                remote(other.at[which, m], other.at[which, m], gsend.at[i], grecv.at[i], sibling).wait_recv()
                return carry

            return one

        def fetch_other(which):
            lax.fori_loop(0, tiles, other_came(which), 0)
            for m in range(tiles):
                fetch(which, m).start()

        def fetch(which, m):
            there = (w_up, w_down)[which].at[pl.ds((tiles + m) * BLOCK, BLOCK)]
            return pltpu.make_async_copy(other.at[which, m], there, dload.at[which * tiles + m])

        def add_cores(which):
            whole = (w_up, w_down)[which]
            for m in range(tiles):
                fetch(which, m).wait()

            def one(r, carry):
                at = pl.ds(pl.multiple_of(r * step, step), step)
                there = pl.ds(pl.multiple_of(tiles * BLOCK + r * step, step), step)
                whole[at, :] = (whole[at, :].astype(jnp.float32) + whole[there, :].astype(jnp.float32)).astype(BF16)
                return carry

            lax.fori_loop(0, tiles * BLOCK // step, one, 0)
            done = pltpu.make_async_copy(
                whole.at[pl.ds(0, tiles * BLOCK)], (up_sum, down_sum)[which], gkeep.at[2 + which]
            )
            done.start()
            return done

        weight_grad(1, cot_all, active)
        side_x()
        arrived(2, got1)

        def to_residual(at, there):
            grad = own[at, :]
            for k in range(3):
                grad = grad + got1[k, at, :].astype(jnp.float32)
            mid_unit = unit[at, :]
            product = grad * mid_unit
            sums[1] += product[:8] + product[8:]
            scaled = grad * gains[3:4, :]
            scale = inv[at, 0:1]
            value = residual[at, :] + scale * (
                scaled - row_mean(scaled) - mid_unit * row_mean(scaled * mid_unit)
            )
            residual_grad[at, :] = value
            attn_cot[there, :] = value.astype(BF16)

        chunks(to_residual, x)
        first, forward = spread(attn_cot, 21)

        def head_back(place):
            heads_cot[block(place), :] = dot_nn(attn_cot[block(place), :], w_out[...]).astype(BF16)

        side_up_z()
        head_back(x)
        one, two = forward()
        fetch_other(1)
        weight_grad(0, mid_all, up_cot)
        side_up_y()
        down_done = add_cores(1)
        fetch_other(0)
        gain_grads[...] = jnp.sum(sums[...], axis=1)
        first[2].wait_recv()
        head_back(left)
        first[3].wait_recv()
        head_back(right)
        one.wait_recv()
        two.wait_recv()
        head_back(far)

        def out_grad_copy(m):
            rows = pl.ds(pl.multiple_of(m * tile, tile), tile)
            slot = lax.rem(m, 2)
            return pltpu.make_async_copy(
                grad_stage.at[slot, :, pl.ds(0, head_cols)], out_proj_grad.at[rows], gkeep.at[slot]
            )

        def out_grad_tile(m, carry):
            @pl.when(m >= 2)
            def _():
                out_grad_copy(m - 2).wait()

            cols = pl.ds(pl.multiple_of(m * tile, tile), tile)
            grad_stage[lax.rem(m, 2), :, :head_cols] = dot_tn(attn_cot[:, cols], heads[...]).astype(BF16)
            out_grad_copy(m).start()
            return carry

        lax.fori_loop(0, tiles, out_grad_tile, 0)
        out_grad_copy(tiles - 2).wait()
        out_grad_copy(tiles - 1).wait()
        for copy in side[5]:
            copy.wait()
        for i in range(16):
            chunk = side_sum[i // 4, i % 4]
            in_grad[:, i * BLOCK : (i + 1) * BLOCK] = chunk[:mixers]
            if i < MIXERS // 8:
                count = min(8, mixers - i * 8)
                net_grad[i * 8 : i * 8 + count, :] = chunk[MIXERS : MIXERS + count, :mixers]
        bias_grad[...] = side_sum[3, 3, MIXERS : MIXERS + 1, :mixers]
        up_done = add_cores(0)
        down_done.wait()
        up_done.wait()
        for i, copy in enumerate(sent):
            if all(copy is not first for first in given[0].values()):
                copy.wait_send()

    f32 = jnp.float32
    vmem = pltpu.VMEM
    piece = (SIDE_ROWS, 128)
    return pl.pallas_call(
        kernel,
        out_shape=[
            shape((BLOCK, width)),
            shape((mixers, BLOCK), f32),
            shape((BLOCK, width), f32),
            shape(heads.shape),
            shape((2, width), f32),
            shape((2, tiles, BLOCK, hidden)),
            shape((width, head_cols)),
            shape((tiles * BLOCK, hidden)),
            shape((tiles * BLOCK, hidden)),
            shape((mixers, width), f32),
            shape((mixers, mixers), f32),
            shape((1, mixers), f32),
        ],
        in_specs=[VMEM, HBM, HBM, HBM, HBM] + [VMEM] * 6,
        out_specs=[VMEM] * 5 + [HBM] * 4 + [VMEM] * 3,
        scratch_shapes=[
            vmem((width, head_cols), BF16),
            vmem((width, hidden), BF16),
            vmem((width, hidden), BF16),
            vmem((rows_all, width), BF16),
            vmem((rows_all, hidden), BF16),
            vmem((rows_all, hidden), f32),
            vmem((rows_all, width), BF16),
            vmem((rows_all, hidden), BF16),
            vmem((rows_all, width), BF16),
            vmem((2, 3, BLOCK, width), BF16),
            vmem((3, BLOCK, width), BF16),
            vmem((3, BLOCK, width), BF16),
            vmem((BLOCK, width), f32),
            vmem((BLOCK, width), f32),
            vmem((BLOCK, width), f32),
            vmem((BLOCK, width), f32),
            vmem((BLOCK, width), BF16),
            vmem((BLOCK, width), f32),
            vmem((BLOCK, 2 * BLOCK), f32),
            vmem((2, tile, hidden), BF16),
            vmem((2, 8, width), f32),
            vmem((4, 4) + piece, f32),
            vmem((4,) + piece, f32),
            vmem((4,) + piece, f32),
            vmem(piece, f32),
            vmem(piece, f32),
            vmem((4,) + piece, f32),
            vmem((4, 4) + piece, f32),
            vmem((4, 4) + piece, f32),
            vmem((BLOCK, width), f32),
            vmem((BLOCK, width), BF16),
            vmem((3, BLOCK, BLOCK), f32),
            pltpu.SemaphoreType.DMA((4,)),
            pltpu.SemaphoreType.DMA((27,)),
            pltpu.SemaphoreType.DMA((27,)),
            pltpu.SemaphoreType.DMA((2 * tiles,)),
            pltpu.SemaphoreType.DMA((2 * tiles,)),
            pltpu.SemaphoreType.DMA((4,)),
            pltpu.SemaphoreType.DMA((16,)),
            pltpu.SemaphoreType.DMA((16,)),
            pltpu.SemaphoreType.DMA((2 * tiles,)),
        ],
        compiler_params=pltpu.CompilerParams(
            collective_id=4, has_side_effects=True, vmem_limit_bytes=VMEM_LIMIT
        ),
        name="middle",
    )(heads, small, up, down, stream, gains, da_in, da_out, da_bias, out_grad, mix_cot_in)


def project(streams, gains, small, tables, down, docs):
    width = streams.shape[2]
    cols = small.shape[2]
    rows_all = 4 * BLOCK
    step = 16
    half = BLOCK // 2
    order = (1, 2, 0)

    def kernel(
        streams_in, gains, small, tables_in, down, docs,
        queries_out, keys_out, values_out, other_keys_out, other_values_out, heads, lse_out, normed_out, full_down,
        queries, keys, values, other_keys, other_values, lse, streams, tables, places_in, weights, normed, load, send, recv, zsend, zrecv, local, wsend, wrecv,
    ):
        x, zl, zh, y, c = coords()
        partner = device(x, 1 - zl, zh, y, c)
        places = {k: (x + k) % 4 for k in (1, 2, 3)}
        right, left, far = places[1], places[3], places[2]
        peers = {k: device(places[k], zl, zh, y, c) for k in (1, 3)}
        loads = [pltpu.make_async_copy(small.at[i], weights.at[i], load.at[i]) for i in range(3)]
        loads += [pltpu.make_async_copy(streams_in.at[i], streams.at[i], load.at[3 + i]) for i in range(3)]
        loads.append(pltpu.make_async_copy(tables_in.at[:, :, zl], tables, load.at[6]))
        for i in (4, 5, 3, 6, 1, 2, 0):
            loads[i].start()
        greeted, start, relay_z, relay_y, finish = weight_gather(
            (down,), (full_down,), (x, zl, zh, y, c), wsend, wrecv, 0
        )
        greet(greeted + [peers[1], peers[3]])
        kept = start(local, 3)

        def block(place):
            return pl.ds(pl.multiple_of(place * BLOCK, BLOCK), BLOCK)

        def piece(i, place, top):
            begin = pl.multiple_of(place * BLOCK + (0 if top else half), half)
            return normed.at[i, pl.ds(begin, half)]

        copies = {}

        def push(i, number, place, top, peer):
            part = piece(i, place, top)
            j = i * 6 + number
            copies[i, number] = remote(part, part, send.at[j], recv.at[j], peer)
            copies[i, number].start()

        for i in order:

            def norm(r, carry, i=i):
                at = pl.ds(pl.multiple_of(r * step, step), step)
                there = pl.ds(pl.multiple_of(x * BLOCK + r * step, step), step)
                value = streams[i, at, :]
                centered = value - row_mean(value)
                scale = lax.rsqrt(row_mean(centered * centered) + EPSILON)
                normed[i, there, :] = (centered * scale * gains[i : i + 1, :]).astype(BF16)
                return carry

            loads[3 + i].wait()
            lax.fori_loop(0, BLOCK // step, norm, 0)
            push(i, 0, x, True, peers[1])
            push(i, 2, x, False, peers[3])
            push(i, 1, x, False, peers[1])
            push(i, 3, x, True, peers[3])

        given = []

        def work(i, place):
            result = dot_nn(normed[i, block(place), :], weights[i])
            out = (queries, keys, values)[i]
            if i == 2:
                out[block(place), :] = result.astype(BF16)
            else:
                at = block(place)
                for h in range(cols // HD):
                    part = result[:, h * HD : (h + 1) * HD]
                    ahead, behind = pltpu.roll(part, HD - ROT // 2, 1), pltpu.roll(part, ROT // 2, 1)
                    turned = part * tables[0, place] + ahead * tables[1, place] + behind * tables[2, place]
                    out[at, h * HD : (h + 1) * HD] = turned.astype(BF16)
            if i > 0:
                j = len(given)
                other = (None, other_keys, other_values)[i]
                given.append(remote(out.at[block(place)], other.at[block(place)], zsend.at[j], zrecv.at[j], partner))
                given[-1].start()

        loads[6].wait()
        for i in order:
            loads[i].wait()
            work(i, x)
        relay_z()
        key_places = set_places(docs, zl, places_in)
        lse[...] = jnp.zeros_like(lse)
        for i in order:
            copies[i, 0].wait_recv()
            push(i, 4, left, True, peers[1])
            copies[i, 2].wait_recv()
            push(i, 5, right, False, peers[3])
            copies[i, 1].wait_recv()
            work(i, left)
            copies[i, 3].wait_recv()
            work(i, right)
            relay_y((1, 2, 0).index(i))
        stores = []
        for i in order:
            copies[i, 4].wait_recv()
            copies[i, 5].wait_recv()
            stores.append(pltpu.make_async_copy(normed.at[i], normed_out.at[i], local.at[i]))
            stores[-1].start()
            work(i, far)
        relay_y(3)
        for copy in given:
            copy.wait()
        kept_here = (queries, keys, values, other_keys, other_values)
        outs = (queries_out, keys_out, values_out, other_keys_out, other_values_out)
        for i, (src, dst) in enumerate(zip(kept_here, outs)):
            stores.append(pltpu.make_async_copy(src, dst, local.at[4 + i]))
            stores[-1].start()
        attend(queries, keys, values, other_keys, other_values, places_in, key_places, heads, lse)
        stores.append(pltpu.make_async_copy(lse, lse_out, local.at[9]))
        stores[-1].start()
        finish()
        for copy in stores + kept:
            copy.wait()
        for copy in copies.values():
            copy.wait_send()

    vmem = pltpu.VMEM
    sem = pltpu.SemaphoreType.DMA
    return pl.pallas_call(
        kernel,
        out_shape=[shape((rows_all, cols))] * 6
        + [
            shape((rows_all, HD), jnp.float32),
            shape((3, rows_all, width)),
            shape((1, down.shape[1] * 16, down.shape[2] * 2)),
        ],
        in_specs=[HBM, VMEM, HBM, HBM, ANY, VMEM],
        out_specs=[HBM] * 5 + [VMEM] + [HBM] * 3,
        scratch_shapes=[vmem((rows_all, cols), BF16)] * 5
        + [
            vmem((rows_all, HD), jnp.float32),
            vmem((3, BLOCK, width), jnp.float32),
            vmem((3, 4, BLOCK, HD), jnp.float32),
            vmem((rows_all, HD), jnp.float32),
            vmem((3, width, cols), BF16),
            vmem((3, rows_all, width), BF16),
            sem((7,)),
            sem((18,)),
            sem((18,)),
            sem((8,)),
            sem((8,)),
            sem((10,)),
            sem((32,)),
            sem((32,)),
        ],
        compiler_params=pltpu.CompilerParams(
            collective_id=2, has_side_effects=True, vmem_limit_bytes=VMEM_LIMIT
        ),
        name="project",
    )(streams, gains, small, tables, down, docs)


def inward(attention, lse, heads_cot, docs, small, normed, out_proj_grad, streams, residual_grad, gains, late_gains, tables, down):
    rows_all, cols = heads_cot.shape
    width = streams.shape[2]
    step = 16
    half = BLOCK // 2
    tile = 2 * BLOCK
    tiles = width // tile
    hidden = down.shape[3]
    thin = hidden // 2

    def kernel(
        q_in, k_in, v_in, ok_in, ov_in, lse_in, cot, docs, small, normed, out_proj_grad, streams, residual_grad,
        gains, late,
        tables_in, down,
        stream_cot, gain_grads, small_sum, down_out,
        weights, inputs, cots, got_k, got_v, far_part, near, hop, got, own, grad, swapped, sums, down_y, down_part, down_z, stream,
        tables, places_in, dq, dk, dv, give_k, give_v, key_sum, value_sum, q, k, v, ok, ov, lse,
        ksend, krecv, load, send, recv, ssend, srecv, gsend, grecv, local,
    ):
        x, zl, zh, y, c = coords()
        z = zh * 2 + zl
        z = zh * 2 + zl
        along_z, along_y = z_peers(x, zl, zh, y, c), y_peers(x, zl, zh, y, c)
        partner = device(x, 1 - zl, zh, y, c)
        sibling = device(x, zl, zh, y, 1 - c)
        places = {k: (x + k) % 4 for k in (1, 2, 3)}
        peers = {k: device(places[k], zl, zh, y, c) for k in (1, 3)}
        early = [
            pltpu.make_async_copy(src, dst, load.at[9 + i])
            for i, (src, dst) in enumerate(
                ((q_in, q), (k_in, k), (v_in, v), (ok_in, ok), (ov_in, ov), (lse_in, lse))
            )
        ]
        for copy in early:
            copy.start()
        loads = [pltpu.make_async_copy(small.at[i], weights.at[i], load.at[i]) for i in range(3)]
        loads += [pltpu.make_async_copy(normed.at[i], inputs.at[i], load.at[3 + i]) for i in range(3)]
        loads.append(pltpu.make_async_copy(out_proj_grad, grad.at[0], load.at[6]))
        loads.append(pltpu.make_async_copy(streams.at[pl.ds(0, 3)], stream, load.at[7]))
        loads.append(pltpu.make_async_copy(tables_in.at[:, :, zl], tables, load.at[8]))
        for copy in loads:
            copy.start()
        greet([peers[1], peers[3], sibling] + [peer for _, peer in along_z + along_y])
        sides = []

        def side(src, dst, peer):
            i = len(sides)
            sides.append(remote(src, dst, ssend.at[i], srecv.at[i], peer))
            sides[-1].start()

        for py, peer in along_y:
            side(down.at[:, py], down_y.at[y], peer)
        locals_ = [pltpu.make_async_copy(down.at[:, y], down_y.at[y], local.at[0])]
        for copy in locals_:
            copy.start()

        def block(place):
            return pl.ds(pl.multiple_of(place * BLOCK, BLOCK), BLOCK)

        def turn_back(value, place, there):
            def one(at):
                part = value(at)
                ahead, behind = pltpu.roll(part, HD - ROT // 2, 1), pltpu.roll(part, ROT // 2, 1)
                table = [tables[t, place, there, :] for t in range(3)]
                return part * table[0] - ahead * table[1] - behind * table[2]

            return one

        def to_cots(i, value):
            def one(r, carry):
                at = pl.ds(pl.multiple_of(r * step, step), step)
                per = BLOCK // step
                there = pl.ds(pl.multiple_of(lax.rem(r, per) * step, step), step)
                for h in range(cols // HD):
                    head = slice(h * HD, (h + 1) * HD)
                    cots[i, at, head] = value(at, head, lax.div(r, per), there).astype(BF16)
                return carry

            lax.fori_loop(0, rows_all // step, one, 0)

        def turned(value):
            return lambda at, head, place, there: turn_back(lambda at: value(at, head), place, there)(at)

        started = []

        def push(src, dst, i, peer):
            started.append(remote(src, dst, send.at[i], recv.at[i], peer))
            started[-1].start()

        def far_sums(i):
            if i == 0:
                loads[0].wait()
            else:
                loads[i].wait()
            far_part[i] = dot_nt(cots[i, block(places[2]), :], weights[i]).astype(BF16)
            push(far_part.at[i, pl.ds(0, half)], hop.at[i, 0], i * 4, peers[1])
            push(far_part.at[i, pl.ds(half, half)], hop.at[i, 1], i * 4 + 1, peers[3])

        def near_sums(i):
            for k, side_of in ((1, 0), (3, 1)):
                product = dot_nt(cots[i, block(places[k]), :], weights[i])
                begin = side_of * half
                j = i * 4 + side_of
                remote(hop.at[i, side_of], hop.at[i, side_of], send.at[j], recv.at[j], sibling).wait_recv()
                near[i, side_of] = product.astype(BF16)
                merged = product[begin : begin + half] + hop[i, side_of].astype(jnp.float32)
                near[i, side_of, begin : begin + half] = merged.astype(BF16)
                push(near.at[i, side_of], got.at[i, side_of], i * 4 + 2 + side_of, peers[k])

        def own_sums(i):
            own[i] = dot_nt(cots[i, block(x), :], weights[i])

        swaps = []

        def weight_grad(i):
            slot = (1, 0, 1, 0)[i]
            if i < 3:
                loads[3 + i].wait()

                def one(m, carry):
                    at = pl.ds(pl.multiple_of(m * tile, tile), tile)
                    grad[slot, at, :] = dot_tn(inputs[i, :, at], cots[i]).astype(BF16)
                    return carry

                lax.fori_loop(0, tiles, one, 0)
            else:
                loads[6].wait()
            for m in range(tiles):
                begin = pl.multiple_of(m * tile + (1 - c) * BLOCK, BLOCK)
                j = i * tiles + m
                swaps.append(
                    remote(grad.at[slot, pl.ds(begin, BLOCK)], swapped.at[i, m], gsend.at[j], grecv.at[j], sibling)
                )
                swaps[-1].start()

        def add_cores(i):
            for m in range(tiles):
                swaps_of[i][m].wait()

            def one(r, carry):
                m, part = r // (BLOCK // step), lax.rem(r, BLOCK // step)
                at = pl.ds(pl.multiple_of(m * tile + c * BLOCK + part * step, step), step)
                there = pl.ds(pl.multiple_of(part * step, step), step)
                value = grad[(1, 0, 1, 0)[i], at, :].astype(jnp.float32) + swapped[i, m, there, :].astype(jnp.float32)
                swapped[i, m, there, :] = value.astype(BF16)
                return carry

            lax.fori_loop(0, tiles * BLOCK // step, one, 0)
            locals_.append(pltpu.make_async_copy(swapped.at[i], small_sum.at[:, i], local.at[1 + i]))
            locals_[-1].start()

        swaps_of = {}

        def grads_of(i):
            begin = len(swaps)
            weight_grad(i)
            swaps_of[i] = swaps[begin:]

        key_places = set_places(docs, zl, places_in)
        for copy in early:
            copy.wait()

        def swap(which, h):
            head = pl.ds(pl.multiple_of(h * HD, HD), HD)
            src, dst = (give_k, give_v)[which], (got_k, got_v)[which]
            j = h * 2 + which
            return remote(src.at[:, head], dst.at[:, head], ksend.at[j], krecv.at[j], partner)

        def give_head(h):
            swap(0, h).start()
            swap(1, h).start()

        attend_back(
            q, k, v, ok, ov, places_in, key_places, lse, cot, dq, dk, dv, give_k, give_v, key_sum, value_sum, give_head
        )
        loads[8].wait()
        to_cots(0, turned(lambda at, head: dq[at, head]))
        far_sums(0)
        near_sums(0)
        grads_of(3)
        grads_of(0)
        own_sums(0)
        for h in range(cols // HD):
            swap(0, h).wait()
        to_cots(1, turned(lambda at, head: dk[at, head] + got_k[at, head].astype(jnp.float32)))
        far_sums(1)
        for h in range(cols // HD):
            swap(1, h).wait()
        to_cots(2, lambda at, head, place, there: dv[at, head] + got_v[at, head].astype(jnp.float32))
        far_sums(2)
        near_sums(1)
        near_sums(2)
        add_cores(3)
        add_cores(0)
        grads_of(1)
        grads_of(2)
        own_sums(1)
        own_sums(2)
        for copy in sides + locals_[:1]:
            copy.wait()

        def add_four(parts, places, dst):
            def one(r, carry):
                at = pl.ds(pl.multiple_of(r * step, step), step)
                value = parts[(0,) + places + (at,)].astype(jnp.float32)
                for src in range(1, 4):
                    value = value + parts[(src,) + places + (at,)].astype(jnp.float32)
                dst[places + (at,)] = value.astype(dst.dtype)
                return carry

            lax.fori_loop(0, BLOCK // step, one, 0)

        def down_piece(high, low):
            return down_part.at[high, :, pl.ds(pl.multiple_of(low * thin, thin), thin)]

        for high in range(2):
            add_four(down_y, (high,), down_part)
        for pz, peer in along_z:
            side(down_piece(pz // 2, pz % 2), down_z.at[z], peer)
        down_z[z] = down_part[zh, :, pl.ds(pl.multiple_of(zl * thin, thin), thin)]
        add_cores(1)
        add_cores(2)
        loads[7].wait()
        sums[...] = jnp.zeros_like(sums)
        for i in range(3):
            for side_of in range(2):
                j = i * 4 + 2 + side_of
                remote(got.at[i, side_of], got.at[i, side_of], send.at[j], recv.at[j], sibling).wait_recv()

            def back(r, carry, i=i):
                at = pl.ds(pl.multiple_of(r * step, step), step)
                value = stream[i, at, :]
                centered = value - row_mean(value)
                scale = lax.rsqrt(row_mean(centered * centered) + EPSILON)
                unit = centered * scale
                above = own[i, at, :] + got[i, 0, at, :].astype(jnp.float32) + got[i, 1, at, :].astype(jnp.float32)
                product = above * unit
                sums[i] += product[:8] + product[8:]
                scaled = above * gains[i : i + 1, :]
                result = scale * (scaled - row_mean(scaled) - unit * row_mean(scaled * unit))
                stream_cot[i, at, :] = result.astype(BF16)
                return carry

            lax.fori_loop(0, BLOCK // step, back, 0)
        stream_cot[3] = residual_grad[...].astype(BF16)
        gain_grads[...] = jnp.zeros_like(gain_grads)
        for i in range(3):
            gain_grads[i : i + 1, :] = jnp.sum(sums[i], axis=0, keepdims=True)
        gain_grads[3:4, :] = late[1:2, :]
        gain_grads[4:5, :] = late[0:1, :]
        for copy in sides[3:]:
            copy.wait()
        add_four(down_z, (), down_out)
        for copy in started:
            copy.wait_send()
        for copy in locals_[1:]:
            copy.wait()

    f32 = jnp.float32
    vmem = pltpu.VMEM
    sem = pltpu.SemaphoreType.DMA
    return pl.pallas_call(
        kernel,
        out_shape=[
            shape((4, BLOCK, width)),
            shape((8, width), f32),
            shape((tiles, 4, BLOCK, cols)),
            shape((BLOCK, thin), f32),
        ],
        in_specs=[HBM] * 6 + [VMEM] * 2 + [HBM] * 4 + [VMEM] * 3 + [HBM] * 2,
        out_specs=[VMEM, VMEM, HBM, VMEM],
        scratch_shapes=[
            vmem((3, width, cols), BF16),
            vmem((3, rows_all, width), BF16),
            vmem((3, rows_all, cols), BF16),
            vmem((rows_all, cols), BF16),
            vmem((rows_all, cols), BF16),
            vmem((3, BLOCK, width), BF16),
            vmem((3, 2, BLOCK, width), BF16),
            vmem((3, 2, half, width), BF16),
            vmem((3, 2, BLOCK, width), BF16),
            vmem((3, BLOCK, width), f32),
            vmem((2, width, cols), BF16),
            vmem((4, tiles, BLOCK, cols), BF16),
            vmem((3, 8, width), f32),
            vmem((4, 2, BLOCK, hidden), BF16),
            vmem((2, BLOCK, hidden), BF16),
            vmem((4, BLOCK, thin), BF16),
            vmem((3, BLOCK, width), f32),
            vmem((3, 4, BLOCK, HD), f32),
            vmem((rows_all, HD), f32),
            vmem((rows_all, cols), f32),
            vmem((rows_all, cols), f32),
            vmem((rows_all, cols), f32),
            vmem((rows_all, cols), BF16),
            vmem((rows_all, cols), BF16),
            vmem((2, rows_all, HD), f32),
            vmem((2, rows_all, HD), f32),
        ]
        + [vmem((rows_all, cols), BF16)] * 5
        + [
            vmem((rows_all, HD), f32),
            sem((8,)),
            sem((8,)),
            sem((15,)),
            sem((12,)),
            sem((12,)),
            sem((8,)),
            sem((8,)),
            sem((4 * tiles,)),
            sem((4 * tiles,)),
            sem((5,)),
        ],
        compiler_params=pltpu.CompilerParams(
            collective_id=5, has_side_effects=True, vmem_limit_bytes=VMEM_LIMIT
        ),
        name="inward",
    )(
        *attention, lse, heads_cot, docs, small, normed, out_proj_grad, streams, residual_grad, gains, late_gains,
        tables, down
    )


def hand_out(top_hist, bottom_hist, top_weights, bottom_weights, stream_cot, gains, small, up):
    _, _, n, half, width = top_hist.shape
    cols = small.shape[3]
    thin = cols // 2
    hidden = up.shape[2] // 2
    step = 16
    lanes = 128

    def kernel(
        top_hist, bottom_hist, tw, bw, cot, gains, small, up,
        out, mix_out, gains_out, three_out, last_out, up_out,
        top, bottom, top_mix, bottom_mix, top_stage, bottom_stage, cot_z, cot_x, mixes, turned,
        x_slots, z_slots, y_slots, c_part, c_slot,
        small_y, small_part, small_z, up_y, up_part, up_z,
        load, csend, crecv, send, recv, msend, mrecv, local, sends, recvs, ssend, srecv,
    ):
        x, zl, zh, y, c = coords()
        z = zh * 2 + zl
        partner = device(x, 1 - zl, zh, y, c)
        peers = {k: device((x + k) % 4, zl, zh, y, c) for k in (1, 2, 3)}
        loads = [pltpu.make_async_copy(top_hist.at[o], top.at[o], load.at[o]) for o in range(2)]
        loads += [pltpu.make_async_copy(bottom_hist.at[k], bottom.at[k], load.at[2 + k]) for k in range(4)]
        for i in (0, 2, 1, 3, 5, 4):
            loads[i].start()
        along_x, along_z = x_peers(x, zl, zh, y, c), z_peers(x, zl, zh, y, c)
        along_y = y_peers(x, zl, zh, y, c)
        sibling = device(x, zl, zh, y, 1 - c)
        greet([peer for _, peer in along_x + along_z + along_y] + [sibling])
        sides = []

        def side(src, dst, peer):
            i = len(sides)
            sides.append(remote(src, dst, ssend.at[i], srecv.at[i], peer))
            sides[-1].start()

        first = exchange(gains, x_slots, x, along_x, sends, recvs, 0)
        x_slots[x] = gains[...]
        copies = []

        def push(src, dst, send, recv, i, peer):
            copies.append(remote(src, dst, send.at[i], recv.at[i], peer))
            copies[-1].start()

        push(cot.at[:, pl.ds(0, half)], cot_z, csend, crecv, 0, partner)
        for k in (1, 3, 2):
            push(cot.at[:, pl.ds(half, half)], cot_x.at[3 - k], csend, crecv, 1 + 3 - k, peers[k])
        for py, peer in along_y:
            for high in range(2):
                side(small.at[high * 4 + py], small_y.at[y, high], peer)
        for py, peer in along_y:
            for high in range(2):
                side(up.at[high * 4 + py], up_y.at[y, high], peer)
        locals_ = [
            pltpu.make_async_copy(small.at[y], small_y.at[y, 0], local.at[0]),
            pltpu.make_async_copy(small.at[4 + y], small_y.at[y, 1], local.at[1]),
            pltpu.make_async_copy(up.at[y], up_y.at[y, 0], local.at[2]),
            pltpu.make_async_copy(up.at[4 + y], up_y.at[y, 1], local.at[3]),
        ]
        for copy in locals_:
            copy.start()

        lane = lax.broadcasted_iota(jnp.int32, (step, lanes), 1)

        def grads_of(entry_of, factors_of, begin, cot_of, stage, slot):
            for j in range(n):

                def some_rows(r, carry, j=j):
                    at = pl.ds(pl.multiple_of(r * step, step), step)
                    factors = factors_of(at)
                    factors = [
                        jnp.broadcast_to(factors[:, begin + j * 4 + s : begin + j * 4 + s + 1], (step, lanes))
                        for s in range(4)
                    ]
                    totals = [jnp.zeros((step, lanes), jnp.float32) for _ in range(4)]
                    for block in range(width // lanes):
                        part = pl.ds(block * lanes, lanes)
                        entry = entry_of(j)[at, part].astype(jnp.float32)
                        mixed = jnp.zeros((step, lanes), jnp.float32)
                        for s in range(4):
                            piece = cot_of(s)[at, part].astype(jnp.float32)
                            mixed = mixed + factors[s] * piece
                            totals[s] = totals[s] + entry * piece
                        stage[j, at, part] = mixed.astype(BF16)
                    packed = jnp.zeros((step, lanes), jnp.float32) if j == 0 else mixes[at, :]
                    for s in range(4):
                        total = jnp.sum(totals[s], axis=1, keepdims=True)
                        packed = jnp.where(lane == j * 4 + s, total, packed)
                    mixes[at, :] = packed
                    return carry

                lax.fori_loop(0, half // step, some_rows, 0)
            turned[slot] = jnp.transpose(mixes[...])[:16]

        def out_rows(k, other, low):
            begin = ((x + k) % 4 * 2 + (1 - zl if other else zl)) * BLOCK + low * half
            return out.at[:, pl.ds(pl.multiple_of(begin, half), half)]

        def owner(k, other):
            return (x + k) % 4 * 2 + (1 - zl if other else zl)

        def keep(src, dst):
            locals_.append(pltpu.make_async_copy(src, dst, local.at[len(locals_)]))
            locals_[-1].start()

        def do_top(other, k):
            slot = other * 4 + k
            source = cot_z if other else cot
            cot_of = (lambda s: source.at[s]) if other else (lambda s: source.at[s, pl.ds(0, half)])
            grads_of(
                lambda j: top.at[other, k, j],
                lambda at: tw[other, at, :],
                k * 12,
                cot_of,
                top_stage.at[other, k],
                slot,
            )
            if k == 0:
                keep(top_stage.at[other, 0], out_rows(0, other, 0))
                keep(turned.at[slot], top_mix.at[owner(0, other)])
            else:
                i = other * 3 + k - 1
                push(top_stage.at[other, k], out_rows(0, other, 0), send, recv, i, peers[k])
                push(turned.at[slot], top_mix.at[owner(0, other)], msend, mrecv, i, peers[k])

        def do_bottom(k, other):
            slot = 8 + k * 2 + other
            cot_of = (lambda s: cot_x.at[k - 1, s]) if k else (lambda s: cot.at[s, pl.ds(half, half)])
            grads_of(
                lambda j: bottom.at[k, other, j],
                lambda at: bw[k, at, :],
                other * 12,
                cot_of,
                bottom_stage.at[k, other],
                slot,
            )
            if other:
                push(bottom_stage.at[k, 1], out_rows(k, 0, 1), send, recv, 6 + k, partner)
                push(turned.at[slot], bottom_mix.at[owner(k, 0)], msend, mrecv, 6 + k, partner)
            else:
                keep(bottom_stage.at[k, 0], out_rows(k, 0, 1))
                keep(turned.at[slot], bottom_mix.at[owner(k, 0)])

        def cot_came(ref, i):
            remote(ref, ref, csend.at[i], crecv.at[i], partner).wait_recv()

        mixes[...] = jnp.zeros_like(mixes)
        loads[0].wait()
        do_top(0, 1)
        do_top(0, 3)
        loads[2].wait()
        do_bottom(0, 1)
        do_top(0, 2)
        for copy in first:
            copy.wait()
        z_slots[z] = x_slots[0] + x_slots[1] + x_slots[2] + x_slots[3]
        second = exchange(z_slots.at[z], z_slots, z, along_z, sends, recvs, 3)
        cot_came(cot_z, 0)
        loads[1].wait()
        for k in (1, 3, 2):
            do_top(1, k)
        for k in (1, 3, 2):
            cot_came(cot_x.at[k - 1], k)
            loads[2 + k].wait()
            do_bottom(k, 1)
        do_top(0, 0)
        do_top(1, 0)
        for k in range(4):
            do_bottom(k, 0)
        for copy in second:
            copy.wait()
        y_slots[y] = z_slots[0] + z_slots[1] + z_slots[2] + z_slots[3]
        third = exchange(y_slots.at[y], y_slots, y, along_y, sends, recvs, 6)
        for copy in third:
            copy.wait()
        c_part[...] = y_slots[0] + y_slots[1] + y_slots[2] + y_slots[3]
        fourth = remote(c_part, c_slot, sends.at[9], recvs.at[9], sibling)
        fourth.start()
        fourth.wait()
        gains_out[...] = (c_part[...] + c_slot[...])[: gains_out.shape[0]]

        def add_four(parts, places, dst, column=None):
            def one(r, carry):
                at = pl.ds(pl.multiple_of(r * step, step), step)
                value = parts[(0,) + places + (at,)].astype(jnp.float32)
                for src in range(1, 4):
                    value = value + parts[(src,) + places + (at,)].astype(jnp.float32)
                if column is None:
                    dst[places + (at,)] = value.astype(dst.dtype)
                elif column < 3:
                    dst[column, at, :] = value
                else:
                    dst[at, :] = value
                return carry

            lax.fori_loop(0, BLOCK // step, one, 0)

        def small_piece(high, low):
            return small_part.at[high, :, :, pl.ds(pl.multiple_of(low * thin, thin), thin)]

        for copy in sides[:6] + locals_[:2]:
            copy.wait()
        for high in range(2):
            for i in range(4):
                add_four(small_y, (high, i), small_part)
        small_last = []
        for k, (pz, peer) in enumerate(along_z):
            small_last.append(
                remote(small_piece(pz // 2, pz % 2), small_z.at[z], ssend.at[12 + k], srecv.at[12 + k], peer)
            )
            small_last[-1].start()
        keep(small_piece(zh, zl), small_z.at[z])
        for copy in sides[6:] + locals_[2:4]:
            copy.wait()
        for high in range(2):
            add_four(up_y, (high,), up_part)

        def up_piece(high, low):
            return up_part.at[high, :, pl.ds(pl.multiple_of(low * hidden, hidden), hidden)]

        up_last = []
        for k, (pz, peer) in enumerate(along_z):
            up_last.append(
                remote(up_piece(pz // 2, pz % 2), up_z.at[z], ssend.at[15 + k], srecv.at[15 + k], peer)
            )
            up_last[-1].start()
        keep(up_piece(zh, zl), up_z.at[z])
        for copy in small_last + locals_[4:]:
            copy.wait()
        for i in range(4):
            add_four(small_z, (i,), three_out if i < 3 else last_out, i)
        for copy in up_last:
            copy.wait()
        add_four(up_z, (), up_out, 3)
        for copy in copies[:4]:
            copy.wait_send()
        for copy in copies[4:]:
            copy.wait()
        for place in range(8):
            both = jnp.concatenate([top_mix[place][:, :half], bottom_mix[place][:, :half]], axis=1)
            for s in range(4):
                for j in range(n):
                    row = j * 4 + s
                    mix_out[j, s : s + 1, place * BLOCK : (place + 1) * BLOCK] = both[row : row + 1]

    f32 = jnp.float32
    vmem = pltpu.VMEM
    sem = pltpu.SemaphoreType.DMA
    piece = (4, half, width)
    return pl.pallas_call(
        kernel,
        out_shape=[
            shape((n, 8 * BLOCK, width)),
            shape((n, 4, 8 * BLOCK), f32),
            shape((5, gains.shape[1]), f32),
            shape((3, BLOCK, thin), f32),
            shape((BLOCK, thin), f32),
            shape((BLOCK, hidden), f32),
        ],
        in_specs=[HBM, HBM, VMEM, VMEM, VMEM, VMEM, HBM, HBM],
        out_specs=[HBM, VMEM, VMEM, VMEM, VMEM, VMEM],
        scratch_shapes=[
            vmem(top_hist.shape, BF16),
            vmem(bottom_hist.shape, BF16),
            vmem((8, 16, lanes), f32),
            vmem((8, 16, lanes), f32),
            vmem(top_hist.shape, BF16),
            vmem(bottom_hist.shape, BF16),
            vmem(piece, BF16),
            vmem((3,) + piece, BF16),
            vmem((BLOCK, lanes), f32),
            vmem((16, 16, lanes), f32),
            vmem((4,) + gains.shape, f32),
            vmem((4,) + gains.shape, f32),
            vmem((4,) + gains.shape, f32),
            vmem(gains.shape, f32),
            vmem(gains.shape, f32),
            vmem((4, 2, 4, BLOCK, cols), BF16),
            vmem((2, 4, BLOCK, cols), BF16),
            vmem((4, 4, BLOCK, thin), BF16),
            vmem((4, 2, BLOCK, 2 * hidden), BF16),
            vmem((2, BLOCK, 2 * hidden), BF16),
            vmem((4, BLOCK, hidden), BF16),
            sem((6,)),
            sem((4,)),
            sem((4,)),
            sem((10,)),
            sem((10,)),
            sem((10,)),
            sem((10,)),
            sem((18,)),
            sem((10,)),
            sem((10,)),
            sem((18,)),
            sem((18,)),
        ],
        compiler_params=pltpu.CompilerParams(
            collective_id=6, has_side_effects=True, vmem_limit_bytes=VMEM_LIMIT
        ),
        name="hand_out",
    )(top_hist, bottom_hist, top_weights, bottom_weights, stream_cot, gains, small, up)


def rotary_columns(length):
    half_rot = ROT // 2
    frequency = 10000.0 ** (-2.0 * np.arange(half_rot, dtype=np.float32) / ROT).astype(np.float32)
    angles = np.arange(length, dtype=np.float32)[:, None] * frequency.astype(np.float32)[None, :]
    cosine, sine = np.cos(angles), np.sin(angles)
    table = np.zeros((3, length, HD), np.float32)
    table[0] = 1.0
    table[0, :, :half_rot] = cosine
    table[0, :, half_rot:ROT] = cosine
    table[1, :, :half_rot] = -sine
    table[2, :, half_rot:ROT] = sine
    return table.reshape(3, 4, 2, BLOCK, HD)


def place_outputs(arrays, cuts):
    def kernel(*refs):
        many = len(arrays)
        srcs, dsts, held, loads, stores = refs[:many], refs[many : 2 * many], refs[2 * many : -2], refs[-2], refs[-1]
        pieces = []
        for src, dst, kept, cut in zip(srcs, dsts, held, cuts):
            count = src.shape[0] // cut
            for i in range(cut):
                rows = pl.ds(i * count, count)
                j = len(pieces)
                pieces.append(
                    (
                        pltpu.make_async_copy(src.at[rows], kept.at[rows], loads.at[j]),
                        pltpu.make_async_copy(kept.at[rows], dst.at[rows], stores.at[j]),
                    )
                )
        for load, _ in pieces:
            load.start()
        for load, store in pieces:
            load.wait()
            store.start()
        for _, store in pieces:
            store.wait()

    return pl.pallas_call(
        kernel,
        out_shape=[shape(a.shape, a.dtype) for a in arrays],
        in_specs=[HBM] * len(arrays),
        out_specs=[HBM] * len(arrays),
        scratch_shapes=[pltpu.VMEM(a.shape, a.dtype) for a in arrays]
        + [pltpu.SemaphoreType.DMA((sum(cuts),))] * 2,
        compiler_params=pltpu.CompilerParams(vmem_limit_bytes=VMEM_LIMIT),
        name="place_outputs",
    )(*arrays)


def body(
    history,
    layer_ids,
    mix_weights,
    doc_ids,
    gains,
    w_qkv,
    w_out,
    w_up,
    w_down,
    da_in,
    da_out,
    da_bias,
    out_grad,
    mix_grad_in,
):
    slots, seq_len, width = history.shape
    small = jnp.concatenate([jnp.transpose(w_qkv, (1, 0, 2)), w_out[None]], axis=0)

    owned, top_hist, bottom_hist, full_small, full_up, top_weights, bottom_weights = collect(
        history, small, w_up[None], layer_ids, mix_weights
    )
    tables = jnp.asarray(rotary_columns(seq_len))
    docs = doc_ids.reshape(8, BLOCK)
    *attention, heads_flat, log_totals, gathered, full_down = project(
        owned, gains, full_small, tables, w_down[None], docs
    )
    (
        block_out,
        mix_next,
        residual_grad,
        heads_cot,
        late_gains,
        _,
        out_proj_grad,
        up_sum,
        down_sum,
        da_in_sum,
        da_out_sum,
        bias_sum,
    ) = middle(
        heads_flat,
        full_small,
        full_up,
        full_down,
        owned,
        gains,
        da_in.T,
        da_out,
        da_bias[None],
        out_grad,
        mix_grad_in.T,
    )
    stream_cot, gains_local, small_sum, down_sum = inward(
        attention,
        log_totals,
        heads_cot,
        docs,
        full_small,
        gathered,
        out_proj_grad,
        owned,
        residual_grad,
        gains,
        late_gains,
        tables,
        down_sum.reshape(2, 4, BLOCK, -1),
    )
    history_grad, mix_grad, gains_sum, qkv_sum, out_sum, up_sum = hand_out(
        top_hist,
        bottom_hist,
        top_weights,
        bottom_weights,
        stream_cot,
        gains_local,
        small_sum,
        up_sum.reshape(8, BLOCK, -1),
    )
    big = history_grad.reshape(-1, width)
    big, block_out, mix_next, mix_grad, gains_sum, qkv_sum, out_sum, up_sum, down_sum, in_sum, net_sum, bias_sum = (
        place_outputs(
            (
                big,
                block_out,
                mix_next,
                mix_grad,
                gains_sum,
                qkv_sum,
                out_sum,
                up_sum,
                down_sum,
                da_in_sum,
                da_out_sum,
                bias_sum,
            ),
            (12,) + (1,) * 11,
        )
    )
    return (
        block_out,
        mix_next.T,
        big.reshape(history_grad.shape),
        jnp.transpose(mix_grad, (1, 0, 2)),
        gains_sum,
        jnp.transpose(qkv_sum, (1, 0, 2)),
        out_sum,
        up_sum,
        down_sum,
        in_sum.T,
        net_sum,
        bias_sum[0],
    )


def solution(mesh):
    return jax.shard_map(
        body,
        mesh=mesh,
        in_specs=(
            P("hist", "tok", None),
            P(),
            P(None, None, "tok"),
            P("tok"),
            P(),
            P("tok", None, "hist"),
            P("tok", "hist"),
            P("tok", "hist"),
            P("tok", "hist"),
            P(),
            P(),
            P(),
            P(("tok", "hist"), None),
            P(("tok", "hist"), None),
        ),
        out_specs=(
            P(("tok", "hist"), None),
            P(("tok", "hist"), None),
            P("hist", "tok", None),
            P(None, "hist", "tok"),
            P(),
            P("tok", None, "hist"),
            P("tok", "hist"),
            P("tok", "hist"),
            P("tok", "hist"),
            P(),
            P(),
            P(),
        ),
        check_vma=False,
    )
```

```python
import jax
import jax.numpy as jnp
import numpy as np
from jax import lax
from jax.experimental import pallas as pl
from jax.experimental.pallas import tpu as pltpu
from jax.sharding import PartitionSpec as P

HD = 128
ROT = 32


EPSILON = 1e-05
NEGATIVE = -1e30
HIGHEST = lax.Precision.HIGHEST


def norm_rows(values):
    row_mean = jnp.mean(values, axis=-1, keepdims=True)
    centered = values - row_mean
    inv_std = lax.rsqrt(jnp.mean(centered * centered, axis=-1, keepdims=True) + EPSILON)
    return (centered * inv_std, inv_std)


def norm_back(grad_unit, norm_unit, inv_std):
    return inv_std * (
        grad_unit
        - jnp.mean(grad_unit, axis=-1, keepdims=True)
        - norm_unit * jnp.mean(grad_unit * norm_unit, axis=-1, keepdims=True)
    )


def gelu_slope(values):
    return (
        0.5 * (1.0 + lax.erf(values * 0.7071067811865476))
        + values * jnp.exp(-0.5 * values * values) * 0.3989422804014327
    )


def rotary_tables(length, rotated):
    half_rot = rotated // 2
    frequency = 10000.0 ** (-2.0 * jnp.arange(half_rot, dtype=jnp.float32) / rotated)
    angles = jnp.arange(length, dtype=jnp.float32)[:, None] * frequency[None, :]
    return (jnp.cos(angles), jnp.sin(angles))


def rotate(values, cosine, sine_table, direction):
    half_rot = cosine.shape[1]
    first_half = values[..., :half_rot]
    second_half = values[..., half_rot : 2 * half_rot]
    cos_part = cosine[:, None, :]
    sin_part = direction * sine_table[:, None, :]
    return jnp.concatenate(
        [
            first_half * cos_part - second_half * sin_part,
            second_half * cos_part + first_half * sin_part,
            values[..., 2 * half_rot :],
        ],
        axis=-1,
    )


def contract(left_side, right_side, left_dim, right_dim):
    return lax.dot_general(
        left_side,
        right_side,
        (((left_dim,), (right_dim,)), ((), ())),
        preferred_element_type=jnp.float32,
    )


MESH = pl.DeviceIdType.MESH
ANY = pl.BlockSpec(memory_space=pl.ANY)
HBM = pl.BlockSpec(memory_space=pltpu.HBM)
BF16 = jnp.bfloat16
BLOCK = 128
VMEM_LIMIT = 62 * 2**20


def coords():
    hist = lax.axis_index("hist")
    tok = lax.axis_index("tok")
    return hist // 2, hist % 2, tok // 8, (tok // 2) % 4, tok % 2


def device(x, zl, zh, y, c):
    return (x * 2 + zl, zh * 8 + y * 2 + c)


def greet(peers):
    barrier = pltpu.get_barrier_semaphore()
    for peer in peers:
        pl.semaphore_signal(barrier, inc=1, device_id=peer, device_id_type=MESH)
    pl.semaphore_wait(barrier, len(peers))


def remote(src, dst, send_sem, recv_sem, peer):
    return pltpu.make_async_remote_copy(
        src_ref=src,
        dst_ref=dst,
        send_sem=send_sem,
        recv_sem=recv_sem,
        device_id=peer,
        device_id_type=MESH,
    )


def comm_call(kernel, out_shapes, sems, collective_id, name, *args):
    return pl.pallas_call(
        kernel,
        out_shape=out_shapes,
        in_specs=[ANY] * len(args),
        out_specs=[ANY] * len(out_shapes),
        scratch_shapes=[
            pltpu.SemaphoreType.DMA((sems,)),
            pltpu.SemaphoreType.DMA((sems,)),
            pltpu.SemaphoreType.DMA((4,)),
        ],
        compiler_params=pltpu.CompilerParams(collective_id=collective_id, has_side_effects=True),
        name=name,
    )(*args)


def shape(dims, dtype=BF16):
    return jax.ShapeDtypeStruct(dims, dtype)


def x_peers(x, zl, zh, y, c):
    return [((x + k) % 4, device((x + k) % 4, zl, zh, y, c)) for k in (1, 3, 2)]


def z_peers(x, zl, zh, y, c):
    places = [(zh * 2 + zl + k) % 4 for k in (1, 3, 2)]
    return [(place, device(x, place % 2, place // 2, y, c)) for place in places]


def y_peers(x, zl, zh, y, c):
    return [((y + k) % 4, device(x, zl, zh, (y + k) % 4, c)) for k in (1, 3, 2)]


VMEM = pl.BlockSpec(memory_space=pltpu.VMEM)
SIDE_ROWS = 112
MIXERS = 104


def exchange(src, slots, mine, peers, send, recv, first):
    copies = []
    for k, (place, peer) in enumerate(peers):
        part = src(place) if callable(src) else src
        copies.append(remote(part, slots.at[mine], send.at[first + k], recv.at[first + k], peer))
        copies[-1].start()
    return copies


def weight_gather(srcs, fulls, place, send, recv, base):
    x, zl, zh, y, c = place
    partner = device(x, 1 - zl, zh, y, c)
    across = device(x, 1 - zl, 1 - zh, y, c)
    sibling = device(x, zl, zh, y, 1 - c)
    rows_of = [device(x, zl, zh, (y + k) % 4, c) for k in (1, 3, 2)]
    z_of = [(zl, zh), (1 - zl, zh), (1 - zl, 1 - zh), (zl, 1 - zh)]
    many = len(srcs)
    started = []

    def view(ref, b_zl, b_zh, b_y, b_c):
        wide = ref.shape[2] // 2
        row = (b_zh * 8 + b_y * 2 + b_c) * BLOCK
        return ref.at[
            :, pl.ds(pl.multiple_of(row, BLOCK), BLOCK), pl.ds(pl.multiple_of(b_zl * wide, wide), wide)
        ]

    def sem(zi, k, sib, a):
        return base + ((zi * 4 + k) * 2 + sib) * many + a

    def refs(zi, k, sib=0):
        by = (y + 4 - (0, 1, 3, 2)[k]) % 4
        return [view(full, *z_of[zi], by, 1 - c if sib else c) for full in fulls]

    def push(src, dst, i, peer):
        started.append(remote(src, dst, send.at[i], recv.at[i], peer))
        started[-1].start()

    def wait_block(zi, k, sib=0):
        for a, ref in enumerate(refs(zi, k, sib)):
            i = sem(zi, k, sib, a)
            remote(ref, ref, send.at[i], recv.at[i], sibling).wait_recv()

    def spread(zi, blocks):
        for a, src in enumerate(blocks):
            dst = view(fulls[a], *z_of[zi], y, c)
            for k, peer in enumerate(rows_of):
                push(src, dst, sem(zi, k + 1, 0, a), peer)
            push(src, dst, sem(zi, 0, 1, a), sibling)

    own = [view(full, zl, zh, y, c) for full in fulls]

    def start(local, first):
        for a, src in enumerate(srcs):
            push(src, own[a], sem(1, 0, 0, a), partner)
        for a, src in enumerate(srcs):
            push(src, own[a], sem(2, 0, 0, a), across)
        kept = [pltpu.make_async_copy(src, own[a], local.at[first + a]) for a, src in enumerate(srcs)]
        for copy in kept:
            copy.start()
        spread(0, srcs)
        return kept

    def relay_z():
        wait_block(1, 0)
        for a, ref in enumerate(refs(1, 0)):
            push(ref, ref, sem(3, 0, 0, a), across)
        spread(1, refs(1, 0))
        wait_block(2, 0)
        spread(2, refs(2, 0))
        wait_block(3, 0)
        spread(3, refs(3, 0))

    def relay_y(zi):
        for k in range(1, 4):
            wait_block(zi, k)
            for a, ref in enumerate(refs(zi, k)):
                push(ref, ref, sem(zi, k, 1, a), sibling)

    def finish():
        for zi in range(4):
            for k in range(4):
                wait_block(zi, k, 1)
        for copy in started:
            copy.wait_send()

    greeted = [partner, across, sibling] + rows_of
    return greeted, start, relay_z, relay_y, finish


def collect(history, three, last, up, layer_ids, mix_weights):
    slots, _, width = history.shape
    layers = mix_weights.shape[1]
    half = BLOCK // 2
    step = 16
    lanes = 128

    def kernel(
        hist, wa, wb, wc, ids, given, streams, top_out, bottom_out, full_a, full_b, full_c, tw, bw,
        top, bottom, acc, far_part, hop, part_x, got_x, part_z, got_z,
        wsend, wrecv, send, recv, local, store,
    ):
        here = coords()
        x, zl, zh, y, c = here
        partner = device(x, 1 - zl, zh, y, c)
        peers = {k: device((x + k) % 4, zl, zh, y, c) for k in (1, 2, 3)}
        greeted, start, relay_z, relay_y, finish = weight_gather(
            (wa, wb, wc), (full_a, full_b, full_c), here, wsend, wrecv, 0
        )
        greet(greeted + [peers[1], peers[2], peers[3]])

        def rows(k, other, low):
            begin = ((x + k) % 4 * 2 + (1 - zl if other else zl)) * BLOCK + low * half
            return hist.at[:, pl.ds(pl.multiple_of(begin, half), half)]

        copies = []

        def push(src, dst, i, peer):
            copies.append(remote(src, dst, send.at[i], recv.at[i], peer))
            copies[-1].start()

        def came(ref, i):
            remote(ref, ref, send.at[i], recv.at[i], partner).wait_recv()

        own = []
        for other in range(2):
            own.append(pltpu.make_async_copy(rows(0, other, 0), top.at[other, 0], local.at[other]))
        for k in range(4):
            own.append(pltpu.make_async_copy(rows(k, 0, 1), bottom.at[k, 0], local.at[2 + k]))
        for copy in own:
            copy.start()
        kept = start(local, 6)
        for k in (2, 1, 3, 0):
            push(rows(k, 1, 1), bottom.at[k, 1], k, partner)
        for other in (1, 0):
            for k in (1, 3, 2):
                push(rows(k, other, 0), top.at[other, 4 - k], 4 + 3 * other + 3 - k, peers[k])

        def columns_of(slots_here, owner, low, into):
            cols = pl.ds(pl.multiple_of(owner * BLOCK, BLOCK), BLOCK)
            column = lax.broadcasted_iota(jnp.int32, (lanes, layers), 0)
            layer = lax.broadcasted_iota(jnp.int32, (lanes, layers), 1)
            wanted = jnp.full((lanes, layers), -1, jnp.int32)
            for i, slot in enumerate(slots_here):
                wanted = jnp.where(column // 4 == i, ids[slot], wanted)
            total = jnp.zeros((lanes, BLOCK), jnp.float32)
            for s in range(4):
                pick = jnp.where((layer == wanted) & (column % 4 == s), 1.0, 0.0)
                total = total + lax.dot_general(
                    pick,
                    given[s, :, cols],
                    (((1,), (0,)), ((), ())),
                    precision=HIGHEST,
                    preferred_element_type=jnp.float32,
                )
            into[...] = jnp.transpose(total)[low * half : (low + 1) * half]

        for other in range(2):
            owner = x * 2 + (1 - zl if other else zl)
            columns_of([(x + k) % 4 * 6 + zl * 3 + j for k in range(4) for j in range(3)], owner, 0, tw.at[other])
        for k in range(4):
            wanted_slots = [x * 6 + (1 - zl if r else zl) * 3 + j for r in range(2) for j in range(3)]
            columns_of(wanted_slots, (x + k) % 4 * 2 + zl, 1, bw.at[k])

        def mix(entries, factors_of, groups, into, offset):
            def some_rows(r, carry):
                at = pl.ds(pl.multiple_of(r * step, step), step)
                there = pl.ds(pl.multiple_of(offset + r * step, step), step)
                for g in range(groups):
                    factors = [
                        [
                            jnp.broadcast_to(factors_of(at)[:, i * 4 + s : i * 4 + s + 1], (step, lanes))
                            for s in range(4)
                        ]
                        for i in range(g * 3, g * 3 + 3)
                    ]

                    def some_cols(b, inner, g=g, factors=factors):
                        cols = pl.ds(pl.multiple_of(b * lanes, lanes), lanes)
                        entry = [entries(g, e)[at, cols].astype(jnp.float32) for e in range(3)]
                        for s in range(4):
                            value = factors[0][s] * entry[0] + factors[1][s] * entry[1] + factors[2][s] * entry[2]
                            into[s, there, cols] = value if g == 0 else into[s, there, cols] + value
                        return inner

                    lax.fori_loop(0, width // lanes, some_cols, 0, unroll=4)
                return carry

            lax.fori_loop(0, half // step, some_rows, 0)

        def mix_top(other, into, offset):
            mix(lambda g, e: top.at[other, g, e], lambda at: tw[other, at, :], 4, into, offset)

        def mix_bottom(k, into, offset):
            mix(lambda g, e: bottom.at[k, g, e], lambda at: bw[k, at, :], 2, into, offset)

        stores = []

        def keep(src, dst):
            stores.append(pltpu.make_async_copy(src, dst, store.at[len(stores)]))
            stores[-1].start()

        def bottom_sums(k):
            came(bottom.at[k, 1], k)
            own[2 + k].wait()
            keep(bottom.at[k], bottom_out.at[k])
            if k == 0:
                mix_bottom(0, streams, half)
                return
            mix_bottom(k, acc, 0)
            if k == 2:
                far_part[...] = acc[...].astype(BF16)
                push(far_part.at[:, pl.ds(0, half // 2)], hop.at[0], 14, peers[1])
                push(far_part.at[:, pl.ds(half // 2, half // 2)], hop.at[1], 15, peers[3])
                return
            side = 0 if k == 1 else 1
            came(hop.at[side], 14 + side)
            merged = pl.ds(side * (half // 2), half // 2)
            for s in range(4):
                acc[s, merged] = acc[s, merged] + hop[side, s].astype(jnp.float32)
            part_x[side] = acc[...].astype(BF16)
            push(part_x.at[side], got_x.at[side], 10 + side, peers[k])

        relay_z()
        bottom_sums(2)
        own[1].wait()
        for k in (1, 2, 3):
            came(top.at[1, k], 4 + 3 + k - 1)
        keep(top.at[1], top_out.at[1])
        mix_top(1, acc, 0)
        part_z[...] = acc[...].astype(BF16)
        push(part_z, got_z, 13, partner)
        bottom_sums(1)
        relay_y(0)
        bottom_sums(3)
        own[0].wait()
        for k in (1, 2, 3):
            came(top.at[0, k], 4 + k - 1)
        keep(top.at[0], top_out.at[0])
        mix_top(0, streams, 0)
        relay_y(1)
        bottom_sums(0)
        relay_y(2)
        relay_y(3)
        came(got_z, 13)

        def add(r, carry, offset, parts):
            at = pl.ds(pl.multiple_of(r * step, step), step)
            there = pl.ds(pl.multiple_of(offset + r * step, step), step)
            for s in range(4):
                value = streams[s, there, :]
                for part in parts:
                    value = value + part(s, at)
                streams[s, there, :] = value
            return carry

        def add_all(offset, parts):
            lax.fori_loop(0, half // step, lambda r, carry: add(r, carry, offset, parts), 0)

        add_all(0, [lambda s, at: got_z[s, at, :].astype(jnp.float32)])
        for side in range(2):
            came(got_x.at[side], 10 + side)
        add_all(half, [lambda s, at, k=k: got_x[k, s, at, :].astype(jnp.float32) for k in range(2)])
        finish()
        for copy in kept + stores:
            copy.wait()
        for copy in copies:
            copy.wait_send()

    def whole(block):
        return shape((block.shape[0], block.shape[1] * 16, block.shape[2] * 2))

    vmem = pltpu.VMEM
    sem = pltpu.SemaphoreType.DMA
    top_shape, bottom_shape = (2, 4, slots, half, width), (4, 2, slots, half, width)
    piece = (4, half, width)
    return pl.pallas_call(
        kernel,
        out_shape=[
            shape((4, BLOCK, width), jnp.float32),
            shape(top_shape),
            shape(bottom_shape),
            whole(three),
            whole(last),
            whole(up),
            shape((2, half, lanes), jnp.float32),
            shape((4, half, lanes), jnp.float32),
        ],
        in_specs=[ANY, ANY, ANY, ANY, pl.BlockSpec(memory_space=pltpu.SMEM), VMEM],
        out_specs=[VMEM, HBM, HBM, HBM, HBM, HBM, VMEM, VMEM],
        scratch_shapes=[
            vmem(top_shape, BF16),
            vmem(bottom_shape, BF16),
            vmem(piece, jnp.float32),
            vmem(piece, BF16),
            vmem((2, 4, half // 2, width), BF16),
            vmem((2,) + piece, BF16),
            vmem((2,) + piece, BF16),
            vmem(piece, BF16),
            vmem(piece, BF16),
            sem((96,)),
            sem((96,)),
            sem((16,)),
            sem((16,)),
            sem((9,)),
            sem((6,)),
        ],
        compiler_params=pltpu.CompilerParams(
            collective_id=1, has_side_effects=True, vmem_limit_bytes=VMEM_LIMIT
        ),
        name="collect",
    )(history, three, last, up, layer_ids, mix_weights)


def dot_nt(left, right):
    return lax.dot_general(left, right, (((1,), (1,)), ((), ())), preferred_element_type=jnp.float32)


def dot_nn(left, right):
    return lax.dot_general(left, right, (((1,), (0,)), ((), ())), preferred_element_type=jnp.float32)


def dot_tn(left, right):
    return lax.dot_general(left, right, (((0,), (0,)), ((), ())), preferred_element_type=jnp.float32)


def token_places(docs, zl):
    rows = docs[...].astype(jnp.float32)
    cols = jnp.transpose(rows)
    first = zl == 0
    queries = [[], []]
    keys = [[], [], [], []]
    down = lax.broadcasted_iota(jnp.int32, (BLOCK, 1), 0)
    along = lax.broadcasted_iota(jnp.int32, (1, BLOCK), 1)
    for p in range(4):
        even, odd = cols[:, 2 * p : 2 * p + 1], cols[:, 2 * p + 1 : 2 * p + 2]
        queries[0].append((down + (2 * p + zl) * BLOCK).astype(jnp.float32))
        queries[1].append(jnp.where(first, even, odd))
        even, odd = rows[2 * p : 2 * p + 1], rows[2 * p + 1 : 2 * p + 2]
        for side, low in ((0, zl), (1, 1 - zl)):
            keys[2 * side].append((along + (2 * p + low) * BLOCK).astype(jnp.float32))
        keys[1].append(jnp.where(first, even, odd))
        keys[3].append(jnp.where(first, odd, even))
    return (
        [jnp.concatenate(part, axis=0) for part in queries],
        [jnp.concatenate(part, axis=1) for part in keys],
    )


def allowed_keys(query_pos, query_doc, keys, side):
    return (keys[2 * side] <= query_pos) & (keys[2 * side + 1] == query_doc)


def attend(q, k, v, ok, ov, places, keys, out, lse, at):
    cols = q.shape[1]
    scale = HD ** (-0.5)

    def one_head(h, carry):
        head = pl.ds(pl.multiple_of(h * HD, HD), HD)
        query_pos, query_doc = places[at, 0:1], places[at, 1:2]
        scores = []
        for side, key in enumerate((k, ok)):
            allowed = allowed_keys(query_pos, query_doc, keys, side)
            scores.append(jnp.where(allowed, dot_nt(q[at, head], key[:, head]) * scale, NEGATIVE))
        top = jnp.maximum(jnp.max(scores[0], axis=1, keepdims=True), jnp.max(scores[1], axis=1, keepdims=True))
        shifted = [jnp.exp(part - top) for part in scores]
        total = jnp.sum(shifted[0], axis=1, keepdims=True) + jnp.sum(shifted[1], axis=1, keepdims=True)
        share = 1.0 / total
        result = dot_nn((shifted[0] * share).astype(BF16), v[:, head])
        result = result + dot_nn((shifted[1] * share).astype(BF16), ov[:, head])
        out[at, head] = result.astype(BF16)
        lane = lax.broadcasted_iota(jnp.int32, (BLOCK, HD), 1)
        lse[at, :] = jnp.where(lane == h, top + jnp.log(total), lse[at, :])
        return carry

    lax.fori_loop(0, cols // HD, one_head, 0)


def attend_back(q, k, v, ok, ov, places, keys, lse, cot, dq, dk, dv, dok, dov, at, begin):
    cols = q.shape[1]
    scale = HD ** (-0.5)

    def add(into, head, value):
        if begin:
            into[:, head] = value
        else:
            into[:, head] = into[:, head] + value

    def one_head(h, carry):
        head = pl.ds(pl.multiple_of(h * HD, HD), HD)
        query_pos, query_doc = places[at, 0:1], places[at, 1:2]
        lane = lax.broadcasted_iota(jnp.int32, (BLOCK, HD), 1)
        log_total = jnp.sum(jnp.where(lane == h, lse[at, :], 0.0), axis=1, keepdims=True)
        probs, prob_grads = [], []
        for side, (key, value) in enumerate(((k, v), (ok, ov))):
            allowed = allowed_keys(query_pos, query_doc, keys, side)
            scores = jnp.where(allowed, dot_nt(q[at, head], key[:, head]) * scale, NEGATIVE)
            probs.append(jnp.exp(scores - log_total))
            prob_grads.append(dot_nt(cot[at, head], value[:, head]))
        row_dot = sum(jnp.sum(p * g, axis=1, keepdims=True) for p, g in zip(probs, prob_grads))
        query_grad = jnp.zeros((BLOCK, HD), jnp.float32)
        for key, key_grad, value_grad, p, g in zip((k, ok), (dk, dok), (dv, dov), probs, prob_grads):
            score_cot = (p * (g - row_dot)).astype(BF16)
            query_grad = query_grad + dot_nn(score_cot, key[:, head])
            add(key_grad, head, dot_tn(score_cot, q[at, head]) * scale)
            add(value_grad, head, dot_tn(p.astype(BF16), cot[at, head]))
        dq[at, head] = query_grad * scale
        return carry

    lax.fori_loop(0, cols // HD, one_head, 0)


def set_places(docs, zl, places):
    queries, keys = token_places(docs, zl)
    lane = lax.broadcasted_iota(jnp.int32, places.shape, 1)
    places[...] = jnp.where(lane == 0, queries[0], jnp.where(lane == 1, queries[1], 0.0))
    return keys


def erf(value):
    value = jnp.clip(value, -4.0, 4.0)
    square = value * value
    top = jnp.full_like(value, -2.72614225801306e-10)
    for factor in (
        2.77068142495902e-08,
        -2.10102402082508e-06,
        -5.69250639462346e-05,
        -7.34990630326855e-04,
        -2.95459980854025e-03,
        -1.60960333262415e-02,
    ):
        top = top * square + factor
    bottom = jnp.full_like(value, -1.45660718464996e-05)
    for factor in (-2.13374055278905e-04, -1.68282697438203e-03, -7.37332916720468e-03, -1.42647390514189e-02):
        bottom = bottom * square + factor
    return value * top / bottom


def gelu_both(value):
    share = 0.5 * (1.0 + erf(value * 0.7071067811865476))
    bell = jnp.exp(-0.5 * value * value) * 0.3989422804014327
    return value * share, share + value * bell


def row_mean(value):
    return jnp.mean(value, axis=1, keepdims=True)


def middle(attention, docs, last, up, down, stream, gains, da_in, da_out, da_bias, out_grad, mix_cot_in):
    rows_all, head_cols = attention[0].shape
    width, hidden = up.shape[1:]
    step = 16
    half = BLOCK // 2
    tile = 2 * BLOCK
    tiles = width // tile
    mixers = da_out.shape[0]

    def kernel(
        q_in, k_in, v_in, ok_in, ov_in, docs, last, up, down, stream_in, gains, in_given, net_given, bias_given,
        out_grad, mix_given,
        block_out, mix_next, residual_grad, gain_grads, other, up_sum, down_sum, in_grad, net_grad, bias_grad,
        dq_out, dk_out, dv_out, dok_out, dov_out, heads_out, attn_cot_out,
        heads, heads_cot, lse, places_in, key_rows, other_values_grad,
        w_out, w_up, w_down, mid_all, active, slope, cot_all, up_cot, attn_cot,
        part, got1, got3, own, residual, unit, total, flat, aux, inv, grad_stage, sums,
        y_slots, z_part, z_slots, c_part, c_slot, x_slots, result, side_sum,
        stream, da_in, padded, aload, astore, load, send, recv, gsend, grecv, gkeep, sends, recvs, dload,
    ):
        x, zl, zh, y, c = coords()
        z = zh * 2 + zl
        along_z, along_y = z_peers(x, zl, zh, y, c), y_peers(x, zl, zh, y, c)
        sibling = device(x, zl, zh, y, 1 - c)
        steps = (1, 3, 2)
        places = {k: (x + k) % 4 for k in steps}
        peers = {k: device(places[k], zl, zh, y, c) for k in steps}
        right, left, far = places[1], places[3], places[2]
        loads = [
            pltpu.make_async_copy(last.at[0], w_out, load.at[0]),
            pltpu.make_async_copy(up.at[0], w_up, load.at[1]),
            pltpu.make_async_copy(down.at[0], w_down, load.at[2]),
            pltpu.make_async_copy(stream_in.at[3], stream, load.at[3]),
        ]

        def cols_of(ref, i):
            return ref.at[:, pl.ds(i * head_cols, head_cols)]

        attention_refs = [cols_of(cot_all, i) for i in range(4)] + [cols_of(active, 0)]

        def load_attention(first):
            return [
                pltpu.make_async_copy(src, dst, aload.at[first + i])
                for i, (src, dst) in enumerate(zip((q_in, k_in, v_in, ok_in, ov_in), attention_refs))
            ]

        early = load_attention(0)
        for copy in early + loads:
            copy.start()
        greet([peers[k] for k in steps] + [peer for _, peer in along_z + along_y] + [sibling])

        def block(place):
            return pl.ds(pl.multiple_of(place * BLOCK, BLOCK), BLOCK)

        def chunks(work, place=0, begin=0, count=BLOCK // step):
            def one(r, carry):
                work(
                    pl.ds(pl.multiple_of(r * step, step), step),
                    pl.ds(pl.multiple_of(place * BLOCK + r * step, step), step),
                )
                return carry

            lax.fori_loop(begin, begin + count, one, 0)

        sent = []
        given = ({}, {}, {})

        def arrived(stage, got):
            for k in steps if stage else (1, 3):
                i = stage * 3 + k - 1
                remote(got.at[k - 1], got.at[k - 1], send.at[i], recv.at[i], sibling).wait_recv()

        def push(src, dst, i, peer):
            copy = remote(src, dst, send.at[i], recv.at[i], peer)
            copy.start()
            sent.append(copy)
            return copy

        def give_part(stage, k, got, product):
            if k == 0:
                own[...] = product
                return
            slot = stage % 2
            if stage == 2:
                for copy in hops if k == 2 else (given[0][k],):
                    copy.wait_send()
            part[slot, k - 1] = product.astype(BF16)
            given[stage][k] = push(part.at[slot, k - 1], got.at[k - 1], stage * 3 + k - 1, peers[k])

        def spread(buf, base, fill):
            def piece(place, top):
                begin = pl.multiple_of(place * BLOCK + (0 if top else half), half)
                return buf.at[pl.ds(begin, half)]

            first = [None] * 4
            chunks(fill, x, 0, half // step)
            first[0] = push(piece(x, True), piece(x, True), base, peers[1])
            first[3] = push(piece(x, True), piece(x, True), base + 3, peers[3])
            chunks(fill, x, half // step, half // step)
            first[1] = push(piece(x, False), piece(x, False), base + 2, peers[3])
            first[2] = push(piece(x, False), piece(x, False), base + 1, peers[1])

            def forward():
                first[0].wait_recv()
                one = push(piece(left, True), piece(left, True), base + 4, peers[1])
                first[1].wait_recv()
                two = push(piece(right, False), piece(right, False), base + 5, peers[3])
                return one, two

            return first, forward

        def gathered(buf, base, fill, work):
            first, forward = spread(buf, base, fill)
            work(0, x)
            one, two = forward()
            first[2].wait_recv()
            work(3, left)
            first[3].wait_recv()
            work(1, right)
            one.wait_recv()
            two.wait_recv()
            work(2, far)

        loads[0].wait()
        for i, row in enumerate(set_places(docs, zl, places_in)):
            key_rows[i : i + 1, :] = row
        key_places = [key_rows.at[pl.ds(i, 1)] for i in range(4)]
        lse[...] = jnp.zeros_like(lse)
        for copy in early:
            copy.wait()

        def attend_rows(place):
            keys = [row[...] for row in key_places]
            attend(*attention_refs, places_in, keys, heads, lse, block(place))

        attend_rows(far)
        part[0, 1] = dot_nt(heads[block(far), :], w_out[...]).astype(BF16)
        tops, bottoms = pl.ds(0, half), pl.ds(half, half)
        hops = (
            push(part.at[0, 1, tops], got1.at[1, tops], 1, peers[1]),
            push(part.at[0, 1, bottoms], got1.at[1, bottoms], 27, peers[3]),
        )
        attend_rows(right)
        total[...] = dot_nt(heads[block(right), :], w_out[...])
        attend_rows(left)
        aux[...] = dot_nt(heads[block(left), :], w_out[...])
        attend_rows(x)
        own[...] = dot_nt(heads[block(x), :], w_out[...])
        heads_kept = pltpu.make_async_copy(heads, heads_out, astore.at[0])
        heads_kept.start()
        hops[0].wait_recv()
        total[tops, :] = total[tops, :] + got1[1, tops, :].astype(jnp.float32)
        give_part(0, 1, got1, total[...])
        hops[1].wait_recv()
        aux[bottoms, :] = aux[bottoms, :] + got1[1, bottoms, :].astype(jnp.float32)
        give_part(0, 3, got1, aux[...])
        aux[...] = jnp.zeros_like(aux)
        aux[:mixers, :] = in_given[...].astype(jnp.float32)
        da_in[...] = aux[...].astype(BF16)
        padded[...] = jnp.zeros_like(padded)
        padded[0, :mixers, :mixers] = net_given[...].astype(jnp.float32)
        padded[1, :1, :mixers] = bias_given[...]
        padded[2, :mixers, :] = mix_given[...]
        padded[2] = jnp.transpose(padded[2])
        loads[3].wait()
        arrived(0, got1)

        def to_mid(at, there):
            value = stream[at, :] + own[at, :]
            for k in (0, 2):
                value = value + got1[k, at, :].astype(jnp.float32)
            residual[at, :] = value
            centered = value - row_mean(value)
            scale = lax.rsqrt(row_mean(centered * centered) + EPSILON)
            inv[at, :BLOCK] = jnp.broadcast_to(scale, (step, BLOCK))
            normed = centered * scale
            unit[at, :] = normed
            mid_all[there, :] = (normed * gains[3:4, :]).astype(BF16)


        waited = []

        def feed(k, place):
            if not waited:
                loads[1].wait()
            total[...] = dot_nn(mid_all[block(place), :], w_up[...])

            def bend(at, there):
                value = total[at, :]
                active[there, :] = (0.5 * value * (1.0 + erf(value * 0.7071067811865476))).astype(BF16)
                slope[there, :] = value

            chunks(bend, place)
            if not waited:
                loads[2].wait()
                waited.append(True)
            give_part(1, k, got3, dot_nt(active[block(place), :], w_down[...]))

        gathered(mid_all, 9, to_mid, feed)

        def bend_more(r, carry):
            at = pl.ds(pl.multiple_of(r * step, step), step)
            slope[at, :] = gelu_both(slope[at, :])[1]
            return carry

        lax.fori_loop(0, rows_all // step, bend_more, 0)
        arrived(1, got3)

        def to_out(at, _):
            value = residual[at, :] + own[at, :]
            for k in range(3):
                value = value + got3[k, at, :].astype(jnp.float32)
            block_out[at, :] = value.astype(BF16)
            scale = lax.rsqrt(row_mean(value * value) + EPSILON)
            inv[at, BLOCK:] = jnp.broadcast_to(scale, (step, BLOCK))
            residual[at, :] = value * scale
            flat[at, :] = (value * scale * gains[4:5, :]).astype(BF16)

        chunks(to_out)
        da_out = padded[0].astype(BF16)
        inner_act, inner_slope = gelu_both(dot_nt(flat[...], da_in[...]))
        inner_act = inner_act.astype(BF16)
        mix_next[...] = jnp.transpose(dot_nn(inner_act, da_out) + padded[1, :1, :])[:mixers]
        mix_cot = padded[2].astype(BF16)
        inner_cot = (dot_nt(mix_cot, da_out) * inner_slope).astype(BF16)
        aux[...] = dot_nn(inner_cot, da_in[...])
        sums[...] = jnp.zeros_like(sums)

        def to_cot(at, there):
            rms_unit = residual[at, :]
            grad = aux[at, :]
            product = grad * rms_unit
            sums[0] += product[:8] + product[8:]
            scaled = grad * gains[4:5, :]
            scale = inv[at, BLOCK : BLOCK + 1]
            value = out_grad[at, :].astype(jnp.float32) + scale * (
                scaled - rms_unit * row_mean(scaled * rms_unit)
            )
            residual[at, :] = value
            cot_all[there, :] = value.astype(BF16)


        def small_grads():
            aux[...] = dot_tn(inner_cot, flat[...])
            net = dot_tn(inner_act, mix_cot)
            bias = jnp.sum(padded[2], axis=0, keepdims=True)
            row = lax.broadcasted_iota(jnp.int32, (8, BLOCK), 0)
            for i in range(16):
                place = (i // 4, i % 4)
                result[place + (slice(0, MIXERS),)] = aux[:MIXERS, i * BLOCK : (i + 1) * BLOCK]
                if i < MIXERS // 8:
                    tail = net[i * 8 : (i + 1) * 8]
                else:
                    tail = jnp.where(row == 0, bias, 0.0)
                result[place + (slice(MIXERS, SIDE_ROWS),)] = tail

        side = {}

        def side_start():
            small_grads()
            side[0] = exchange(lambda py: result.at[py], y_slots, y, along_y, sends, recvs, 0)
            y_slots[y] = result[y]

        def side_z():
            for copy in side[0]:
                copy.wait()
            z_part[...] = y_slots[0] + y_slots[1] + y_slots[2] + y_slots[3]
            side[1] = exchange(lambda pz: z_part.at[pz], z_slots, z, along_z, sends, recvs, 3)
            z_slots[z] = z_part[z]

        def side_core():
            for copy in side[1]:
                copy.wait()
            c_part[...] = z_slots[0] + z_slots[1] + z_slots[2] + z_slots[3]
            side[2] = remote(c_part, c_slot, sends.at[6], recvs.at[6], sibling)
            side[2].start()

        def side_x():
            side[2].wait()
            x_slots[x] = c_part[...] + c_slot[...]
            along_x = [(places[k], peers[k]) for k in steps]
            side[3] = exchange(x_slots.at[x], x_slots, x, along_x, sends, recvs, 7)

        def side_up_z():
            for copy in side[3]:
                copy.wait()
            side_sum[y, z] = x_slots[0] + x_slots[1] + x_slots[2] + x_slots[3]
            side[4] = exchange(side_sum.at[y, z], side_sum.at[y], z, along_z, sends, recvs, 10)

        def side_up_y():
            for copy in side[4]:
                copy.wait()
            side[5] = exchange(side_sum.at[y], side_sum, y, along_y, sends, recvs, 13)

        def feed_back(k, place):
            total[...] = dot_nn(cot_all[block(place), :], w_down[...])

            def bend(at, there):
                up_cot[there, :] = (total[at, :] * slope[there, :].astype(jnp.float32)).astype(BF16)

            chunks(bend, place)
            give_part(2, k, got1, dot_nt(up_cot[block(place), :], w_up[...]))

        first, forward = spread(cot_all, 15, to_cot)
        side_start()
        feed_back(0, x)
        one, two = forward()
        first[2].wait_recv()
        feed_back(3, left)
        first[3].wait_recv()
        feed_back(1, right)
        side_z()
        one.wait_recv()
        two.wait_recv()
        feed_back(2, far)
        side_core()

        def weight_grad(which, left_side, right_side):
            def copies(m):
                slot = lax.rem(m, 2)
                mine = grad_stage.at[slot, pl.ds(pl.multiple_of(c * BLOCK, BLOCK), BLOCK)]
                theirs = grad_stage.at[slot, pl.ds(pl.multiple_of((1 - c) * BLOCK, BLOCK), BLOCK)]
                i = which * tiles + m
                stays = (w_up, w_down)[which].at[pl.ds(pl.multiple_of(m * BLOCK, BLOCK), BLOCK)]
                return (
                    pltpu.make_async_copy(mine, stays, gkeep.at[slot]),
                    remote(theirs, other.at[which, m], gsend.at[i], grecv.at[i], sibling),
                )

            def finish(m):
                stay, go = copies(m)
                stay.wait()
                go.wait_send()

            def one(m, carry):
                @pl.when(m >= 2)
                def _():
                    finish(m - 2)

                cols = pl.ds(pl.multiple_of(m * tile, tile), tile)
                grad_stage[lax.rem(m, 2)] = dot_tn(left_side[:, cols], right_side[...]).astype(BF16)
                for copy in copies(m):
                    copy.start()
                return carry

            lax.fori_loop(0, tiles, one, 0)
            finish(tiles - 2)
            finish(tiles - 1)

        def other_came(which):
            def one(m, carry):
                i = which * tiles + m
                remote(other.at[which, m], other.at[which, m], gsend.at[i], grecv.at[i], sibling).wait_recv()
                return carry

            return one

        def fetch_other(which):
            lax.fori_loop(0, tiles, other_came(which), 0)
            for m in range(tiles):
                fetch(which, m).start()

        def fetch(which, m):
            there = (w_up, w_down)[which].at[pl.ds((tiles + m) * BLOCK, BLOCK)]
            return pltpu.make_async_copy(other.at[which, m], there, dload.at[which * tiles + m])

        def add_cores(which):
            whole = (w_up, w_down)[which]
            for m in range(tiles):
                fetch(which, m).wait()

            def one(r, carry):
                at = pl.ds(pl.multiple_of(r * step, step), step)
                there = pl.ds(pl.multiple_of(tiles * BLOCK + r * step, step), step)
                whole[at, :] = (whole[at, :].astype(jnp.float32) + whole[there, :].astype(jnp.float32)).astype(BF16)
                return carry

            lax.fori_loop(0, tiles * BLOCK // step, one, 0)
            done = pltpu.make_async_copy(
                whole.at[pl.ds(0, tiles * BLOCK)], (up_sum, down_sum)[which], gkeep.at[2 + which]
            )
            done.start()
            return done

        weight_grad(1, cot_all, active)
        side_x()
        ended = [*first, one, two]
        for copy in ended:
            copy.wait_send()
        late = load_attention(5)
        for copy in late:
            copy.start()
        weight_grad(0, mid_all, up_cot)
        arrived(2, got1)

        def to_residual(at, there):
            grad = own[at, :]
            for k in range(3):
                grad = grad + got1[k, at, :].astype(jnp.float32)
            mid_unit = unit[at, :]
            product = grad * mid_unit
            sums[1] += product[:8] + product[8:]
            scaled = grad * gains[3:4, :]
            scale = inv[at, 0:1]
            value = residual[at, :] + scale * (
                scaled - row_mean(scaled) - mid_unit * row_mean(scaled * mid_unit)
            )
            residual_grad[at, :] = value
            attn_cot[there, :] = value.astype(BF16)

        first, forward = spread(attn_cot, 21, to_residual)

        grads = [cols_of(slope, i) for i in range(4)] + [other_values_grad]

        def head_back(place, begin=False):
            heads_cot[block(place), :] = dot_nn(attn_cot[block(place), :], w_out[...]).astype(BF16)
            keys = [row[...] for row in key_places]
            attend_back(
                *attention_refs, places_in, keys, lse, heads_cot, *grads, block(place), begin
            )

        side_up_z()
        for copy in late:
            copy.wait()
        head_back(x, True)
        one, two = forward()
        fetch_other(1)
        fetch_other(0)
        side_up_y()
        down_done = add_cores(1)
        gain_grads[...] = jnp.sum(sums[...], axis=1)
        first[2].wait_recv()
        head_back(left)
        first[3].wait_recv()
        head_back(right)
        one.wait_recv()
        two.wait_recv()
        head_back(far)
        cols_of(active, 1)[...] = grads[3][...].astype(BF16)
        cols_of(active, 2)[...] = grads[4][...].astype(BF16)
        stored = [heads_kept]
        for i, (src, dst) in enumerate(
            (
                (cols_of(active, 1), dok_out),
                (cols_of(active, 2), dov_out),
                (grads[0], dq_out),
                (grads[1], dk_out),
                (grads[2], dv_out),
                (attn_cot, attn_cot_out),
            )
        ):
            stored.append(pltpu.make_async_copy(src, dst, astore.at[1 + i]))
            stored[-1].start()
        for copy in side[5]:
            copy.wait()
        for i in range(16):
            chunk = side_sum[i // 4, i % 4]
            in_grad[:, i * BLOCK : (i + 1) * BLOCK] = chunk[:mixers]
            if i < MIXERS // 8:
                count = min(8, mixers - i * 8)
                net_grad[i * 8 : i * 8 + count, :] = chunk[MIXERS : MIXERS + count, :mixers]
        bias_grad[...] = side_sum[3, 3, MIXERS : MIXERS + 1, :mixers]
        up_done = add_cores(0)
        down_done.wait()
        up_done.wait()
        for copy in stored:
            copy.wait()
        for i, copy in enumerate(sent):
            if all(copy is not other_copy for other_copy in (*given[0].values(), *hops, *ended)):
                copy.wait_send()

    f32 = jnp.float32
    vmem = pltpu.VMEM
    piece = (SIDE_ROWS, 128)
    return pl.pallas_call(
        kernel,
        out_shape=[
            shape((BLOCK, width)),
            shape((mixers, BLOCK), f32),
            shape((BLOCK, width), f32),
            shape((2, width), f32),
            shape((2, tiles, BLOCK, hidden)),
            shape((tiles * BLOCK, hidden)),
            shape((tiles * BLOCK, hidden)),
            shape((mixers, width), f32),
            shape((mixers, mixers), f32),
            shape((1, mixers), f32),
        ]
        + [shape((rows_all, head_cols), f32)] * 3
        + [shape((rows_all, head_cols))] * 3
        + [shape((rows_all, width))],
        in_specs=[HBM] * 5 + [VMEM] + [HBM] * 4 + [VMEM] * 6,
        out_specs=[VMEM] * 4 + [HBM] * 3 + [VMEM] * 3 + [HBM] * 7,
        scratch_shapes=[
            vmem((rows_all, head_cols), BF16),
            vmem((rows_all, head_cols), BF16),
            vmem((rows_all, HD), f32),
            vmem((rows_all, HD), f32),
            vmem((8, rows_all), f32),
            vmem((rows_all, head_cols), f32),
            vmem((width, head_cols), BF16),
            vmem((width, hidden), BF16),
            vmem((width, hidden), BF16),
            vmem((rows_all, width), BF16),
            vmem((rows_all, hidden), BF16),
            vmem((rows_all, hidden), f32),
            vmem((rows_all, width), BF16),
            vmem((rows_all, hidden), BF16),
            vmem((rows_all, width), BF16),
            vmem((2, 3, BLOCK, width), BF16),
            vmem((3, BLOCK, width), BF16),
            vmem((3, BLOCK, width), BF16),
            vmem((BLOCK, width), f32),
            vmem((BLOCK, width), f32),
            vmem((BLOCK, width), f32),
            vmem((BLOCK, width), f32),
            vmem((BLOCK, width), BF16),
            vmem((BLOCK, width), f32),
            vmem((BLOCK, 2 * BLOCK), f32),
            vmem((2, tile, hidden), BF16),
            vmem((2, 8, width), f32),
            vmem((4, 4) + piece, f32),
            vmem((4,) + piece, f32),
            vmem((4,) + piece, f32),
            vmem(piece, f32),
            vmem(piece, f32),
            vmem((4,) + piece, f32),
            vmem((4, 4) + piece, f32),
            vmem((4, 4) + piece, f32),
            vmem((BLOCK, width), f32),
            vmem((BLOCK, width), BF16),
            vmem((3, BLOCK, BLOCK), f32),
            pltpu.SemaphoreType.DMA((10,)),
            pltpu.SemaphoreType.DMA((7,)),
            pltpu.SemaphoreType.DMA((4,)),
            pltpu.SemaphoreType.DMA((28,)),
            pltpu.SemaphoreType.DMA((28,)),
            pltpu.SemaphoreType.DMA((2 * tiles,)),
            pltpu.SemaphoreType.DMA((2 * tiles,)),
            pltpu.SemaphoreType.DMA((4,)),
            pltpu.SemaphoreType.DMA((16,)),
            pltpu.SemaphoreType.DMA((16,)),
            pltpu.SemaphoreType.DMA((2 * tiles,)),
        ],
        compiler_params=pltpu.CompilerParams(
            collective_id=4, has_side_effects=True, vmem_limit_bytes=VMEM_LIMIT
        ),
        name="middle",
    )(*attention, docs, last, up, down, stream, gains, da_in, da_out, da_bias, out_grad, mix_cot_in)


def project(streams, gains, small, tables, down):
    width = streams.shape[2]
    cols = small.shape[2]
    rows_all = 4 * BLOCK
    step = 16
    half = BLOCK // 2
    order = (1, 2, 0)

    def kernel(
        streams_in, gains, small, tables_in, down,
        queries_out, keys_out, values_out, other_keys_out, other_values_out, normed_out, full_down,
        queries, keys, values, other_keys, other_values, streams, tables, weights, normed, load, send, recv, zsend, zrecv, local, wsend, wrecv,
    ):
        x, zl, zh, y, c = coords()
        partner = device(x, 1 - zl, zh, y, c)
        places = {k: (x + k) % 4 for k in (1, 2, 3)}
        right, left, far = places[1], places[3], places[2]
        peers = {k: device(places[k], zl, zh, y, c) for k in (1, 3)}
        loads = [pltpu.make_async_copy(small.at[i], weights.at[i], load.at[i]) for i in range(3)]
        loads += [pltpu.make_async_copy(streams_in.at[i], streams.at[i], load.at[3 + i]) for i in range(3)]
        loads.append(pltpu.make_async_copy(tables_in.at[:, :, zl], tables, load.at[6]))
        for i in (4, 5, 3, 6, 1, 2, 0):
            loads[i].start()
        greeted, start, relay_z, relay_y, finish = weight_gather(
            (down,), (full_down,), (x, zl, zh, y, c), wsend, wrecv, 0
        )
        greet(greeted + [peers[1], peers[3]])
        kept = start(local, 3)

        def block(place):
            return pl.ds(pl.multiple_of(place * BLOCK, BLOCK), BLOCK)

        def piece(i, place, top):
            begin = pl.multiple_of(place * BLOCK + (0 if top else half), half)
            return normed.at[i, pl.ds(begin, half)]

        copies = {}

        def push(i, number, place, top, peer):
            part = piece(i, place, top)
            j = i * 6 + number
            copies[i, number] = remote(part, part, send.at[j], recv.at[j], peer)
            copies[i, number].start()

        for i in order:

            def norm(r, carry, i=i):
                at = pl.ds(pl.multiple_of(r * step, step), step)
                there = pl.ds(pl.multiple_of(x * BLOCK + r * step, step), step)
                value = streams[i, at, :]
                centered = value - row_mean(value)
                scale = lax.rsqrt(row_mean(centered * centered) + EPSILON)
                normed[i, there, :] = (centered * scale * gains[i : i + 1, :]).astype(BF16)
                return carry

            loads[3 + i].wait()
            lax.fori_loop(0, BLOCK // step, norm, 0)
            push(i, 0, x, True, peers[1])
            push(i, 2, x, False, peers[3])
            push(i, 1, x, False, peers[1])
            push(i, 3, x, True, peers[3])

        given = []

        def work(i, place):
            result = dot_nn(normed[i, block(place), :], weights[i])
            out = (queries, keys, values)[i]
            if i == 2:
                out[block(place), :] = result.astype(BF16)
            else:
                at = block(place)
                for h in range(cols // HD):
                    part = result[:, h * HD : (h + 1) * HD]
                    ahead, behind = pltpu.roll(part, HD - ROT // 2, 1), pltpu.roll(part, ROT // 2, 1)
                    turned = part * tables[0, place] + ahead * tables[1, place] + behind * tables[2, place]
                    out[at, h * HD : (h + 1) * HD] = turned.astype(BF16)
            if i > 0:
                j = len(given)
                other = (None, other_keys, other_values)[i]
                given.append(remote(out.at[block(place)], other.at[block(place)], zsend.at[j], zrecv.at[j], partner))
                given[-1].start()

        loads[6].wait()
        for i in order:
            loads[i].wait()
            work(i, x)
        relay_z()
        for i in order:
            copies[i, 0].wait_recv()
            push(i, 4, left, True, peers[1])
            copies[i, 2].wait_recv()
            push(i, 5, right, False, peers[3])
            copies[i, 1].wait_recv()
            work(i, left)
            copies[i, 3].wait_recv()
            work(i, right)
            relay_y((1, 2, 0).index(i))
        stores = []
        for i in order:
            copies[i, 4].wait_recv()
            copies[i, 5].wait_recv()
            stores.append(pltpu.make_async_copy(normed.at[i], normed_out.at[i], local.at[i]))
            stores[-1].start()
            work(i, far)
        relay_y(3)
        for copy in given:
            copy.wait()
        kept_here = (queries, keys, values, other_keys, other_values)
        outs = (queries_out, keys_out, values_out, other_keys_out, other_values_out)
        for i, (src, dst) in enumerate(zip(kept_here, outs)):
            stores.append(pltpu.make_async_copy(src, dst, local.at[4 + i]))
            stores[-1].start()
        finish()
        for copy in stores + kept:
            copy.wait()
        for copy in copies.values():
            copy.wait_send()

    vmem = pltpu.VMEM
    sem = pltpu.SemaphoreType.DMA
    return pl.pallas_call(
        kernel,
        out_shape=[shape((rows_all, cols))] * 5
        + [
            shape((3, rows_all, width)),
            shape((1, down.shape[1] * 16, down.shape[2] * 2)),
        ],
        in_specs=[HBM, VMEM, HBM, HBM, ANY],
        out_specs=[HBM] * 7,
        scratch_shapes=[vmem((rows_all, cols), BF16)] * 5
        + [
            vmem((3, BLOCK, width), jnp.float32),
            vmem((3, 4, BLOCK, HD), jnp.float32),
            vmem((3, width, cols), BF16),
            vmem((3, rows_all, width), BF16),
            sem((7,)),
            sem((18,)),
            sem((18,)),
            sem((8,)),
            sem((8,)),
            sem((9,)),
            sem((32,)),
            sem((32,)),
        ],
        compiler_params=pltpu.CompilerParams(
            collective_id=2, has_side_effects=True, vmem_limit_bytes=VMEM_LIMIT
        ),
        name="project",
    )(streams, gains, small, tables, down)


def inward(grads, gives, heads, attn_cot, small, normed, streams, residual_grad, gains, late_gains, tables, down):
    rows_all, cols = heads.shape
    width = streams.shape[2]
    step = 16
    half = BLOCK // 2
    tile = 2 * BLOCK
    tiles = width // tile
    hidden = down.shape[3]
    thin = hidden // 2

    def kernel(
        dq_in, dk_in, dv_in, give_k, give_v, heads_in, cot_in, small, normed, streams, residual_grad, gains, late,
        tables_in, down,
        stream_cot, gain_grads, small_sum, down_out,
        weights, inputs, cots, got_k, got_v, far_part, near, hop, got, own, grad, swapped, sums, down_y, down_part, down_z, stream,
        tables, dq, dk, dv, heads, attn_cot,
        ksend, krecv, load, send, recv, ssend, srecv, gsend, grecv, local,
    ):
        x, zl, zh, y, c = coords()
        z = zh * 2 + zl
        z = zh * 2 + zl
        along_z, along_y = z_peers(x, zl, zh, y, c), y_peers(x, zl, zh, y, c)
        partner = device(x, 1 - zl, zh, y, c)
        sibling = device(x, zl, zh, y, 1 - c)
        places = {k: (x + k) % 4 for k in (1, 2, 3)}
        peers = {k: device(places[k], zl, zh, y, c) for k in (1, 3)}
        early = [
            pltpu.make_async_copy(src, dst, load.at[9 + i])
            for i, (src, dst) in enumerate(
                ((dq_in, dq), (dk_in, dk), (dv_in, dv), (heads_in, heads), (cot_in, attn_cot))
            )
        ]
        for copy in early:
            copy.start()
        loads = [pltpu.make_async_copy(small.at[i], weights.at[i], load.at[i]) for i in range(3)]
        loads += [pltpu.make_async_copy(normed.at[i], inputs.at[i], load.at[3 + i]) for i in range(3)]
        loads.append(pltpu.make_async_copy(tables_in.at[:, :, zl], tables, load.at[8]))
        loads.append(pltpu.make_async_copy(streams.at[pl.ds(0, 3)], stream, load.at[7]))
        for copy in loads:
            copy.start()
        greet([peers[1], peers[3], sibling] + [peer for _, peer in along_z + along_y])
        sides = []

        def side(src, dst, peer):
            i = len(sides)
            sides.append(remote(src, dst, ssend.at[i], srecv.at[i], peer))
            sides[-1].start()

        swaps_z = [
            remote(src, dst, ksend.at[i], krecv.at[i], partner)
            for i, (src, dst) in enumerate(((give_k, got_k), (give_v, got_v)))
        ]
        swaps_z[0].start()
        for py, peer in along_y:
            side(down.at[:, py], down_y.at[y], peer)
        locals_ = [pltpu.make_async_copy(down.at[:, y], down_y.at[y], local.at[0])]
        for copy in locals_:
            copy.start()

        def block(place):
            return pl.ds(pl.multiple_of(place * BLOCK, BLOCK), BLOCK)

        def turn_back(value, place, there):
            def one(at):
                part = value(at)
                ahead, behind = pltpu.roll(part, HD - ROT // 2, 1), pltpu.roll(part, ROT // 2, 1)
                table = [tables[t, place, there, :] for t in range(3)]
                return part * table[0] - ahead * table[1] - behind * table[2]

            return one

        def to_cots(i, value):
            def one(r, carry):
                at = pl.ds(pl.multiple_of(r * step, step), step)
                per = BLOCK // step
                there = pl.ds(pl.multiple_of(lax.rem(r, per) * step, step), step)
                for h in range(cols // HD):
                    head = slice(h * HD, (h + 1) * HD)
                    cots[i, at, head] = value(at, head, lax.div(r, per), there).astype(BF16)
                return carry

            lax.fori_loop(0, rows_all // step, one, 0)

        def turned(value):
            return lambda at, head, place, there: turn_back(lambda at: value(at, head), place, there)(at)

        started = []

        def push(src, dst, i, peer):
            started.append(remote(src, dst, send.at[i], recv.at[i], peer))
            started[-1].start()

        def far_sums(i):
            if i == 0:
                loads[0].wait()
            else:
                loads[i].wait()
            far_part[i] = dot_nt(cots[i, block(places[2]), :], weights[i]).astype(BF16)
            push(far_part.at[i, pl.ds(0, half)], hop.at[i, 0], i * 4, peers[1])
            push(far_part.at[i, pl.ds(half, half)], hop.at[i, 1], i * 4 + 1, peers[3])

        def near_sums(i):
            for k, side_of in ((1, 0), (3, 1)):
                product = dot_nt(cots[i, block(places[k]), :], weights[i])
                begin = side_of * half
                j = i * 4 + side_of
                remote(hop.at[i, side_of], hop.at[i, side_of], send.at[j], recv.at[j], sibling).wait_recv()
                near[i, side_of] = product.astype(BF16)
                merged = product[begin : begin + half] + hop[i, side_of].astype(jnp.float32)
                near[i, side_of, begin : begin + half] = merged.astype(BF16)
                push(near.at[i, side_of], got.at[i, side_of], i * 4 + 2 + side_of, peers[k])

        def own_sums(i):
            own[i] = dot_nt(cots[i, block(x), :], weights[i])

        swaps = []

        def weight_grad(i):
            slot = (1, 0, 1, 0)[i]
            if i < 3:
                loads[3 + i].wait()
                left_side, right_side = inputs.at[i], cots.at[i]
            else:
                early[3].wait()
                early[4].wait()
                left_side, right_side = attn_cot, heads

            def one(m, carry):
                at = pl.ds(pl.multiple_of(m * tile, tile), tile)
                grad[slot, at, :] = dot_tn(left_side[:, at], right_side[...]).astype(BF16)
                return carry

            lax.fori_loop(0, tiles, one, 0)
            for m in range(tiles):
                begin = pl.multiple_of(m * tile + (1 - c) * BLOCK, BLOCK)
                j = i * tiles + m
                swaps.append(
                    remote(grad.at[slot, pl.ds(begin, BLOCK)], swapped.at[i, m], gsend.at[j], grecv.at[j], sibling)
                )
                swaps[-1].start()

        def add_cores(i):
            for m in range(tiles):
                swaps_of[i][m].wait()

            def one(r, carry):
                m, part = r // (BLOCK // step), lax.rem(r, BLOCK // step)
                at = pl.ds(pl.multiple_of(m * tile + c * BLOCK + part * step, step), step)
                there = pl.ds(pl.multiple_of(part * step, step), step)
                value = grad[(1, 0, 1, 0)[i], at, :].astype(jnp.float32) + swapped[i, m, there, :].astype(jnp.float32)
                swapped[i, m, there, :] = value.astype(BF16)
                return carry

            lax.fori_loop(0, tiles * BLOCK // step, one, 0)
            locals_.append(pltpu.make_async_copy(swapped.at[i], small_sum.at[:, i], local.at[1 + i]))
            locals_[-1].start()

        swaps_of = {}

        def grads_of(i):
            begin = len(swaps)
            weight_grad(i)
            swaps_of[i] = swaps[begin:]

        for copy in early[:3]:
            copy.wait()
        loads[6].wait()
        to_cots(0, turned(lambda at, head: dq[at, head]))
        far_sums(0)
        near_sums(0)
        swaps_z[0].wait_send()
        swaps_z[1].start()
        grads_of(3)
        grads_of(0)
        own_sums(0)
        swaps_z[0].wait_recv()
        to_cots(1, turned(lambda at, head: dk[at, head] + got_k[at, head].astype(jnp.float32)))
        far_sums(1)
        swaps_z[1].wait()
        to_cots(2, lambda at, head, place, there: dv[at, head] + got_v[at, head].astype(jnp.float32))
        far_sums(2)
        near_sums(1)
        near_sums(2)
        add_cores(3)
        add_cores(0)
        grads_of(1)
        grads_of(2)
        own_sums(1)
        own_sums(2)
        for copy in sides + locals_[:1]:
            copy.wait()

        def add_four(parts, places, dst):
            def one(r, carry):
                at = pl.ds(pl.multiple_of(r * step, step), step)
                value = parts[(0,) + places + (at,)].astype(jnp.float32)
                for src in range(1, 4):
                    value = value + parts[(src,) + places + (at,)].astype(jnp.float32)
                dst[places + (at,)] = value.astype(dst.dtype)
                return carry

            lax.fori_loop(0, BLOCK // step, one, 0)

        def down_piece(high, low):
            return down_part.at[high, :, pl.ds(pl.multiple_of(low * thin, thin), thin)]

        for high in range(2):
            add_four(down_y, (high,), down_part)
        for pz, peer in along_z:
            side(down_piece(pz // 2, pz % 2), down_z.at[z], peer)
        down_z[z] = down_part[zh, :, pl.ds(pl.multiple_of(zl * thin, thin), thin)]
        add_cores(1)
        add_cores(2)
        loads[7].wait()
        sums[...] = jnp.zeros_like(sums)
        for i in range(3):
            for side_of in range(2):
                j = i * 4 + 2 + side_of
                remote(got.at[i, side_of], got.at[i, side_of], send.at[j], recv.at[j], sibling).wait_recv()

            def back(r, carry, i=i):
                at = pl.ds(pl.multiple_of(r * step, step), step)
                value = stream[i, at, :]
                centered = value - row_mean(value)
                scale = lax.rsqrt(row_mean(centered * centered) + EPSILON)
                unit = centered * scale
                above = own[i, at, :] + got[i, 0, at, :].astype(jnp.float32) + got[i, 1, at, :].astype(jnp.float32)
                product = above * unit
                sums[i] += product[:8] + product[8:]
                scaled = above * gains[i : i + 1, :]
                result = scale * (scaled - row_mean(scaled) - unit * row_mean(scaled * unit))
                stream_cot[i, at, :] = result.astype(BF16)
                return carry

            lax.fori_loop(0, BLOCK // step, back, 0)
        stream_cot[3] = residual_grad[...].astype(BF16)
        gain_grads[...] = jnp.zeros_like(gain_grads)
        for i in range(3):
            gain_grads[i : i + 1, :] = jnp.sum(sums[i], axis=0, keepdims=True)
        gain_grads[3:4, :] = late[1:2, :]
        gain_grads[4:5, :] = late[0:1, :]
        for copy in sides[3:]:
            copy.wait()
        add_four(down_z, (), down_out)
        for copy in started:
            copy.wait_send()
        for copy in locals_[1:]:
            copy.wait()

    f32 = jnp.float32
    vmem = pltpu.VMEM
    sem = pltpu.SemaphoreType.DMA
    return pl.pallas_call(
        kernel,
        out_shape=[
            shape((4, BLOCK, width)),
            shape((8, width), f32),
            shape((tiles, 4, BLOCK, cols)),
            shape((BLOCK, thin), f32),
        ],
        in_specs=[HBM] * 10 + [VMEM] * 3 + [HBM] * 2,
        out_specs=[VMEM, VMEM, HBM, VMEM],
        scratch_shapes=[
            vmem((3, width, cols), BF16),
            vmem((3, rows_all, width), BF16),
            vmem((3, rows_all, cols), BF16),
            vmem((rows_all, cols), BF16),
            vmem((rows_all, cols), BF16),
            vmem((3, BLOCK, width), BF16),
            vmem((3, 2, BLOCK, width), BF16),
            vmem((3, 2, half, width), BF16),
            vmem((3, 2, BLOCK, width), BF16),
            vmem((3, BLOCK, width), f32),
            vmem((2, width, cols), BF16),
            vmem((4, tiles, BLOCK, cols), BF16),
            vmem((3, 8, width), f32),
            vmem((4, 2, BLOCK, hidden), BF16),
            vmem((2, BLOCK, hidden), BF16),
            vmem((4, BLOCK, thin), BF16),
            vmem((3, BLOCK, width), f32),
            vmem((3, 4, BLOCK, HD), f32),
            vmem((rows_all, cols), f32),
            vmem((rows_all, cols), f32),
            vmem((rows_all, cols), f32),
            vmem((rows_all, cols), BF16),
            vmem((rows_all, width), BF16),
            sem((2,)),
            sem((2,)),
            sem((15,)),
            sem((12,)),
            sem((12,)),
            sem((8,)),
            sem((8,)),
            sem((4 * tiles,)),
            sem((4 * tiles,)),
            sem((5,)),
        ],
        compiler_params=pltpu.CompilerParams(
            collective_id=5, has_side_effects=True, vmem_limit_bytes=VMEM_LIMIT
        ),
        name="inward",
    )(
        *grads, *gives, heads, attn_cot, small, normed, streams, residual_grad, gains, late_gains, tables, down
    )


def hand_out(top_hist, bottom_hist, top_weights, bottom_weights, stream_cot, gains, small, up):
    _, _, n, half, width = top_hist.shape
    cols = small.shape[3]
    thin = cols // 2
    hidden = up.shape[2] // 2
    step = 16
    lanes = 128

    def kernel(
        top_hist, bottom_hist, tw, bw, cot, gains, small, up,
        out, mix_out, gains_out, three_out, last_out, up_out,
        top, bottom, top_mix, bottom_mix, top_stage, bottom_stage, cot_z, cot_x, mixes, turned,
        x_slots, z_slots, y_slots, c_part, c_slot,
        small_y, small_part, small_z, up_y, up_part, up_z,
        load, csend, crecv, send, recv, msend, mrecv, local, sends, recvs, ssend, srecv,
    ):
        x, zl, zh, y, c = coords()
        z = zh * 2 + zl
        partner = device(x, 1 - zl, zh, y, c)
        peers = {k: device((x + k) % 4, zl, zh, y, c) for k in (1, 2, 3)}
        loads = [pltpu.make_async_copy(top_hist.at[o], top.at[o], load.at[o]) for o in range(2)]
        loads += [pltpu.make_async_copy(bottom_hist.at[k], bottom.at[k], load.at[2 + k]) for k in range(4)]
        for i in (0, 2, 1, 3, 5, 4):
            loads[i].start()
        along_x, along_z = x_peers(x, zl, zh, y, c), z_peers(x, zl, zh, y, c)
        along_y = y_peers(x, zl, zh, y, c)
        sibling = device(x, zl, zh, y, 1 - c)
        greet([peer for _, peer in along_x + along_z + along_y] + [sibling])
        sides = []

        def side(src, dst, peer):
            i = len(sides)
            sides.append(remote(src, dst, ssend.at[i], srecv.at[i], peer))
            sides[-1].start()

        first = exchange(gains, x_slots, x, along_x, sends, recvs, 0)
        x_slots[x] = gains[...]
        copies = []

        def push(src, dst, send, recv, i, peer):
            copies.append(remote(src, dst, send.at[i], recv.at[i], peer))
            copies[-1].start()

        push(cot.at[:, pl.ds(0, half)], cot_z, csend, crecv, 0, partner)
        for k in (1, 3, 2):
            push(cot.at[:, pl.ds(half, half)], cot_x.at[3 - k], csend, crecv, 1 + 3 - k, peers[k])
        for py, peer in along_y:
            for high in range(2):
                side(small.at[high * 4 + py], small_y.at[y, high], peer)
        for py, peer in along_y:
            for high in range(2):
                side(up.at[high * 4 + py], up_y.at[y, high], peer)
        locals_ = [
            pltpu.make_async_copy(small.at[y], small_y.at[y, 0], local.at[0]),
            pltpu.make_async_copy(small.at[4 + y], small_y.at[y, 1], local.at[1]),
            pltpu.make_async_copy(up.at[y], up_y.at[y, 0], local.at[2]),
            pltpu.make_async_copy(up.at[4 + y], up_y.at[y, 1], local.at[3]),
        ]
        for copy in locals_:
            copy.start()

        lane = lax.broadcasted_iota(jnp.int32, (step, lanes), 1)

        def grads_of(entry_of, factors_of, begin, cot_of, stage, slot):
            for j in range(n):

                def some_rows(r, carry, j=j):
                    at = pl.ds(pl.multiple_of(r * step, step), step)
                    factors = factors_of(at)
                    factors = [
                        jnp.broadcast_to(factors[:, begin + j * 4 + s : begin + j * 4 + s + 1], (step, lanes))
                        for s in range(4)
                    ]
                    totals = [jnp.zeros((step, lanes), jnp.float32) for _ in range(4)]
                    for block in range(width // lanes):
                        part = pl.ds(block * lanes, lanes)
                        entry = entry_of(j)[at, part].astype(jnp.float32)
                        mixed = jnp.zeros((step, lanes), jnp.float32)
                        for s in range(4):
                            piece = cot_of(s)[at, part].astype(jnp.float32)
                            mixed = mixed + factors[s] * piece
                            totals[s] = totals[s] + entry * piece
                        stage[j, at, part] = mixed.astype(BF16)
                    packed = jnp.zeros((step, lanes), jnp.float32) if j == 0 else mixes[at, :]
                    for s in range(4):
                        total = jnp.sum(totals[s], axis=1, keepdims=True)
                        packed = jnp.where(lane == j * 4 + s, total, packed)
                    mixes[at, :] = packed
                    return carry

                lax.fori_loop(0, half // step, some_rows, 0)
            turned[slot] = jnp.transpose(mixes[...])[:16]

        def out_rows(k, other, low):
            begin = ((x + k) % 4 * 2 + (1 - zl if other else zl)) * BLOCK + low * half
            return out.at[:, pl.ds(pl.multiple_of(begin, half), half)]

        def owner(k, other):
            return (x + k) % 4 * 2 + (1 - zl if other else zl)

        def keep(src, dst):
            locals_.append(pltpu.make_async_copy(src, dst, local.at[len(locals_)]))
            locals_[-1].start()

        def do_top(other, k):
            slot = other * 4 + k
            source = cot_z if other else cot
            cot_of = (lambda s: source.at[s]) if other else (lambda s: source.at[s, pl.ds(0, half)])
            grads_of(
                lambda j: top.at[other, k, j],
                lambda at: tw[other, at, :],
                k * 12,
                cot_of,
                top_stage.at[other, k],
                slot,
            )
            if k == 0:
                keep(top_stage.at[other, 0], out_rows(0, other, 0))
                keep(turned.at[slot], top_mix.at[owner(0, other)])
            else:
                i = other * 3 + k - 1
                push(top_stage.at[other, k], out_rows(0, other, 0), send, recv, i, peers[k])
                push(turned.at[slot], top_mix.at[owner(0, other)], msend, mrecv, i, peers[k])

        def do_bottom(k, other):
            slot = 8 + k * 2 + other
            cot_of = (lambda s: cot_x.at[k - 1, s]) if k else (lambda s: cot.at[s, pl.ds(half, half)])
            grads_of(
                lambda j: bottom.at[k, other, j],
                lambda at: bw[k, at, :],
                other * 12,
                cot_of,
                bottom_stage.at[k, other],
                slot,
            )
            if other:
                push(bottom_stage.at[k, 1], out_rows(k, 0, 1), send, recv, 6 + k, partner)
                push(turned.at[slot], bottom_mix.at[owner(k, 0)], msend, mrecv, 6 + k, partner)
            else:
                keep(bottom_stage.at[k, 0], out_rows(k, 0, 1))
                keep(turned.at[slot], bottom_mix.at[owner(k, 0)])

        def cot_came(ref, i):
            remote(ref, ref, csend.at[i], crecv.at[i], partner).wait_recv()

        mixes[...] = jnp.zeros_like(mixes)
        loads[0].wait()
        do_top(0, 1)
        do_top(0, 3)
        loads[2].wait()
        do_bottom(0, 1)
        do_top(0, 2)
        for copy in first:
            copy.wait()
        z_slots[z] = x_slots[0] + x_slots[1] + x_slots[2] + x_slots[3]
        second = exchange(z_slots.at[z], z_slots, z, along_z, sends, recvs, 3)
        cot_came(cot_z, 0)
        loads[1].wait()
        for k in (1, 3, 2):
            do_top(1, k)
        for k in (1, 3, 2):
            cot_came(cot_x.at[k - 1], k)
            loads[2 + k].wait()
            do_bottom(k, 1)
        do_top(0, 0)
        do_top(1, 0)
        for k in range(4):
            do_bottom(k, 0)
        for copy in second:
            copy.wait()
        y_slots[y] = z_slots[0] + z_slots[1] + z_slots[2] + z_slots[3]
        third = exchange(y_slots.at[y], y_slots, y, along_y, sends, recvs, 6)
        for copy in third:
            copy.wait()
        c_part[...] = y_slots[0] + y_slots[1] + y_slots[2] + y_slots[3]
        fourth = remote(c_part, c_slot, sends.at[9], recvs.at[9], sibling)
        fourth.start()
        fourth.wait()
        gains_out[...] = (c_part[...] + c_slot[...])[: gains_out.shape[0]]

        def add_four(parts, places, dst, column=None):
            def one(r, carry):
                at = pl.ds(pl.multiple_of(r * step, step), step)
                value = parts[(0,) + places + (at,)].astype(jnp.float32)
                for src in range(1, 4):
                    value = value + parts[(src,) + places + (at,)].astype(jnp.float32)
                if column is None:
                    dst[places + (at,)] = value.astype(dst.dtype)
                elif column < 3:
                    dst[column, at, :] = value
                else:
                    dst[at, :] = value
                return carry

            lax.fori_loop(0, BLOCK // step, one, 0)

        def small_piece(high, low):
            return small_part.at[high, :, :, pl.ds(pl.multiple_of(low * thin, thin), thin)]

        for copy in sides[:6] + locals_[:2]:
            copy.wait()
        for high in range(2):
            for i in range(4):
                add_four(small_y, (high, i), small_part)
        small_last = []
        for k, (pz, peer) in enumerate(along_z):
            small_last.append(
                remote(small_piece(pz // 2, pz % 2), small_z.at[z], ssend.at[12 + k], srecv.at[12 + k], peer)
            )
            small_last[-1].start()
        keep(small_piece(zh, zl), small_z.at[z])
        for copy in sides[6:] + locals_[2:4]:
            copy.wait()
        for high in range(2):
            add_four(up_y, (high,), up_part)

        def up_piece(high, low):
            return up_part.at[high, :, pl.ds(pl.multiple_of(low * hidden, hidden), hidden)]

        up_last = []
        for k, (pz, peer) in enumerate(along_z):
            up_last.append(
                remote(up_piece(pz // 2, pz % 2), up_z.at[z], ssend.at[15 + k], srecv.at[15 + k], peer)
            )
            up_last[-1].start()
        keep(up_piece(zh, zl), up_z.at[z])
        for copy in small_last + locals_[4:]:
            copy.wait()
        for i in range(4):
            add_four(small_z, (i,), three_out if i < 3 else last_out, i)
        for copy in up_last:
            copy.wait()
        add_four(up_z, (), up_out, 3)
        for copy in copies[:4]:
            copy.wait_send()
        for copy in copies[4:]:
            copy.wait()
        for place in range(8):
            both = jnp.concatenate([top_mix[place][:, :half], bottom_mix[place][:, :half]], axis=1)
            for s in range(4):
                for j in range(n):
                    row = j * 4 + s
                    mix_out[j, s : s + 1, place * BLOCK : (place + 1) * BLOCK] = both[row : row + 1]

    f32 = jnp.float32
    vmem = pltpu.VMEM
    sem = pltpu.SemaphoreType.DMA
    piece = (4, half, width)
    return pl.pallas_call(
        kernel,
        out_shape=[
            shape((n, 8 * BLOCK, width)),
            shape((n, 4, 8 * BLOCK), f32),
            shape((5, gains.shape[1]), f32),
            shape((3, BLOCK, thin), f32),
            shape((BLOCK, thin), f32),
            shape((BLOCK, hidden), f32),
        ],
        in_specs=[HBM, HBM, VMEM, VMEM, VMEM, VMEM, HBM, HBM],
        out_specs=[HBM, VMEM, VMEM, VMEM, VMEM, VMEM],
        scratch_shapes=[
            vmem(top_hist.shape, BF16),
            vmem(bottom_hist.shape, BF16),
            vmem((8, 16, lanes), f32),
            vmem((8, 16, lanes), f32),
            vmem(top_hist.shape, BF16),
            vmem(bottom_hist.shape, BF16),
            vmem(piece, BF16),
            vmem((3,) + piece, BF16),
            vmem((BLOCK, lanes), f32),
            vmem((16, 16, lanes), f32),
            vmem((4,) + gains.shape, f32),
            vmem((4,) + gains.shape, f32),
            vmem((4,) + gains.shape, f32),
            vmem(gains.shape, f32),
            vmem(gains.shape, f32),
            vmem((4, 2, 4, BLOCK, cols), BF16),
            vmem((2, 4, BLOCK, cols), BF16),
            vmem((4, 4, BLOCK, thin), BF16),
            vmem((4, 2, BLOCK, 2 * hidden), BF16),
            vmem((2, BLOCK, 2 * hidden), BF16),
            vmem((4, BLOCK, hidden), BF16),
            sem((6,)),
            sem((4,)),
            sem((4,)),
            sem((10,)),
            sem((10,)),
            sem((10,)),
            sem((10,)),
            sem((18,)),
            sem((10,)),
            sem((10,)),
            sem((18,)),
            sem((18,)),
        ],
        compiler_params=pltpu.CompilerParams(
            collective_id=6, has_side_effects=True, vmem_limit_bytes=VMEM_LIMIT
        ),
        name="hand_out",
    )(top_hist, bottom_hist, top_weights, bottom_weights, stream_cot, gains, small, up)


def rotary_columns(length):
    half_rot = ROT // 2
    frequency = 10000.0 ** (-2.0 * np.arange(half_rot, dtype=np.float32) / ROT).astype(np.float32)
    angles = np.arange(length, dtype=np.float32)[:, None] * frequency.astype(np.float32)[None, :]
    cosine, sine = np.cos(angles), np.sin(angles)
    table = np.zeros((3, length, HD), np.float32)
    table[0] = 1.0
    table[0, :, :half_rot] = cosine
    table[0, :, half_rot:ROT] = cosine
    table[1, :, :half_rot] = -sine
    table[2, :, half_rot:ROT] = sine
    return table.reshape(3, 4, 2, BLOCK, HD)


def place_outputs(arrays, cuts):
    def kernel(*refs):
        many = len(arrays)
        srcs, dsts, held, loads, stores = refs[:many], refs[many : 2 * many], refs[2 * many : -2], refs[-2], refs[-1]
        pieces = []
        for src, dst, kept, cut in zip(srcs, dsts, held, cuts):
            count = src.shape[0] // cut
            for i in range(cut):
                rows = pl.ds(i * count, count)
                j = len(pieces)
                pieces.append(
                    (
                        pltpu.make_async_copy(src.at[rows], kept.at[rows], loads.at[j]),
                        pltpu.make_async_copy(kept.at[rows], dst.at[rows], stores.at[j]),
                    )
                )
        for load, _ in pieces:
            load.start()
        for load, store in pieces:
            load.wait()
            store.start()
        for _, store in pieces:
            store.wait()

    return pl.pallas_call(
        kernel,
        out_shape=[shape(a.shape, a.dtype) for a in arrays],
        in_specs=[HBM] * len(arrays),
        out_specs=[HBM] * len(arrays),
        scratch_shapes=[pltpu.VMEM(a.shape, a.dtype) for a in arrays]
        + [pltpu.SemaphoreType.DMA((sum(cuts),))] * 2,
        compiler_params=pltpu.CompilerParams(vmem_limit_bytes=VMEM_LIMIT),
        name="place_outputs",
    )(*arrays)


def body(
    history,
    layer_ids,
    mix_weights,
    doc_ids,
    gains,
    w_qkv,
    w_out,
    w_up,
    w_down,
    da_in,
    da_out,
    da_bias,
    out_grad,
    mix_grad_in,
):
    slots, seq_len, width = history.shape

    owned, top_hist, bottom_hist, full_three, full_last, full_up, top_weights, bottom_weights = collect(
        history, jnp.transpose(w_qkv, (1, 0, 2)), w_out[None], w_up[None], layer_ids, mix_weights
    )
    tables = jnp.asarray(rotary_columns(seq_len))
    docs = doc_ids.reshape(8, BLOCK)
    *attention, gathered, full_down = project(owned, gains, full_three, tables, w_down[None])
    (
        block_out,
        mix_next,
        residual_grad,
        late_gains,
        _,
        up_sum,
        down_sum,
        da_in_sum,
        da_out_sum,
        bias_sum,
        query_grad,
        key_grad,
        value_grad,
        key_give,
        value_give,
        heads,
        attn_cot,
    ) = middle(
        attention,
        docs,
        full_last,
        full_up,
        full_down,
        owned,
        gains,
        da_in.T,
        da_out,
        da_bias[None],
        out_grad,
        mix_grad_in.T,
    )
    stream_cot, gains_local, small_sum, down_sum = inward(
        (query_grad, key_grad, value_grad),
        (key_give, value_give),
        heads,
        attn_cot,
        full_three,
        gathered,
        owned,
        residual_grad,
        gains,
        late_gains,
        tables,
        down_sum.reshape(2, 4, BLOCK, -1),
    )
    history_grad, mix_grad, gains_sum, qkv_sum, out_sum, up_sum = hand_out(
        top_hist,
        bottom_hist,
        top_weights,
        bottom_weights,
        stream_cot,
        gains_local,
        small_sum,
        up_sum.reshape(8, BLOCK, -1),
    )
    big = history_grad.reshape(-1, width)
    big, block_out, mix_next, mix_grad, gains_sum, qkv_sum, out_sum, up_sum, down_sum, in_sum, net_sum, bias_sum = (
        place_outputs(
            (
                big,
                block_out,
                mix_next,
                mix_grad,
                gains_sum,
                qkv_sum,
                out_sum,
                up_sum,
                down_sum,
                da_in_sum,
                da_out_sum,
                bias_sum,
            ),
            (24,) + (1,) * 11,
        )
    )
    return (
        block_out,
        mix_next.T,
        big.reshape(history_grad.shape),
        jnp.transpose(mix_grad, (1, 0, 2)),
        gains_sum,
        jnp.transpose(qkv_sum, (1, 0, 2)),
        out_sum,
        up_sum,
        down_sum,
        in_sum.T,
        net_sum,
        bias_sum[0],
    )


def solution(mesh):
    return jax.shard_map(
        body,
        mesh=mesh,
        in_specs=(
            P("hist", "tok", None),
            P(),
            P(None, None, "tok"),
            P("tok"),
            P(),
            P("tok", None, "hist"),
            P("tok", "hist"),
            P("tok", "hist"),
            P("tok", "hist"),
            P(),
            P(),
            P(),
            P(("tok", "hist"), None),
            P(("tok", "hist"), None),
        ),
        out_specs=(
            P(("tok", "hist"), None),
            P(("tok", "hist"), None),
            P("hist", "tok", None),
            P(None, "hist", "tok"),
            P(),
            P("tok", None, "hist"),
            P("tok", "hist"),
            P("tok", "hist"),
            P("tok", "hist"),
            P(),
            P(),
            P(),
        ),
        check_vma=False,
    )
```
